32 devices in a mesh: seq: 4 (over x, core), fsdp: 8 (over z, y).
Axes of the slice: x: 2, y: 2, z: 4, core: 2. Of those that a mesh axis runs over, the one named last changes fastest.
Arguments:
- patches: bfloat16 [2, 32, 1536, 768], P(None, ('seq', 'fsdp')), may hold values from -6 to 6
- positions: int32 [2, 2, 32, 1536], P(None, None, ('seq', 'fsdp')), may hold values from 0 to 63
- lengths: int32 [2, 32, 2], P(None, ('seq', 'fsdp')), may hold values from 128 to 1152, as said below
- res_weights: int32 [2, 32, 2], P(None, ('seq', 'fsdp')), may hold values from 1 to 6
- labels: int32 [2, 32, 2], P(None, ('seq', 'fsdp')), may hold values from 0 to 999
- block_slot: int32 [13], replicated, may hold values from 0 to 15, as said below
- blocks: float32 [13, 768, 768], P(None, 'fsdp')
- pos_table: float32 [2, 64, 768], P(None, None, 'fsdp'), may hold values from -3 to 3
- gains: float32 [5, 768], P(None, 'fsdp')
- head: float32 [768, 1000], P('fsdp'), may hold values from -0.21875 to 0.21875
- left_stats: float32 [16, 768, 768], P('fsdp')
- right_stats: float32 [16, 768, 768], P('fsdp')
- left_roots: float32 [16, 768, 768], P('fsdp')
- right_roots: float32 [16, 768, 768], P('fsdp')
- pos_first: float32 [2, 64, 768], P(None, None, 'fsdp'), may hold values from -5.722046e-06 to 5.722046e-06
- pos_second: float32 [2, 64, 768], P(None, None, 'fsdp'), may hold values from 6.207647e-13 to 2.4596338e-12
- gain_first: float32 [5, 768], P(None, 'fsdp'), may hold values from -2.670288e-05 to 2.670288e-05
- gain_second: float32 [5, 768], P(None, 'fsdp'), may hold values from 1.5226305e-11 to 6.2076476e-11
- head_first: float32 [768, 1000], P('fsdp'), may hold values from -5.722046e-06 to 5.722046e-06
- head_second: float32 [768, 1000], P('fsdp'), may hold values from 6.207647e-13 to 2.4596338e-12
Outputs:
- blocks_new: float32 [13, 768, 768], P(None, 'fsdp')
- block_grads: float32 [13, 768, 768], P(None, 'fsdp')
- left_new: float32 [16, 768, 768], P('fsdp')
- right_new: float32 [16, 768, 768], P('fsdp')
- pos_new: float32 [2, 64, 768], P(None, None, 'fsdp')
- pos_first_new: float32 [2, 64, 768], P(None, None, 'fsdp')
- pos_second_new: float32 [2, 64, 768], P(None, None, 'fsdp')
- gains_new: float32 [5, 768], P(None, 'fsdp')
- gain_first_new: float32 [5, 768], P(None, 'fsdp')
- gain_second_new: float32 [5, 768], P(None, 'fsdp')
- head_new: float32 [768, 1000], P('fsdp')
- head_first_new: float32 [768, 1000], P('fsdp')
- head_second_new: float32 [768, 1000], P('fsdp')
- clip_norm: float32 [], replicated
- loss_sum: float32 [], replicated
- weight_sum: float32 [], replicated
The draws below stay inside these ranges and needn't reach their ends.
Inputs may be any that keep to these rules, and one draw needn't show every extreme that they name: `lengths`: slot 0 of every pack holds a sequence of exactly 1152 patches, slot 1 one of 128 to 256; the remaining slots of the pack are padding. `block_slot`: distinct slots, one a block; slot s is owned by fsdp index s // 2; slots that no block names stay empty.
All inputs are finite; a program needn't handle non-finite values.
Results may differ from the reference program's by a relative error of at most 0.0095.
Values may be sent and summed in bfloat16 or wider, within the bound.
No kernel may reach another device: no remote copies, remote signals or barrier semaphores. Data moves between devices by JAX's collectives and lax.ppermute only.
A program may use at most 576 MiB of HBM per device.

```python
import math
import jax
import jax.numpy as jnp
from jax import lax

D = 768
HEADS = 12
HEAD = 64
PIX = 768
CLASSES = 1000
GRID = 64
PACK = 1536
SHORT = 256
LONG = 1152
MB = 2
STEP = 10
BLOCKS = 13
PACKS = 32
SHSLOTS = 16
NPARAM = 8537856
N_SEQ = 4
N_FSDP = 8


def symmetric(key, scale, spread, share):
    first, second = jax.random.split(key)
    diagonal = scale * jnp.exp(jax.random.uniform(first, (SHSLOTS, D), jnp.float32, -spread, spread))
    noise = jax.random.normal(second, (SHSLOTS, D, D), jnp.float32) * (share * scale / math.sqrt(D))
    noise = (noise + jnp.swapaxes(noise, 1, 2)) * 0.70710678
    identity = jnp.eye(D, dtype=jnp.float32)
    return noise * (1.0 - identity) + diagonal[:, :, None] * identity


def stat_scale():
    return 0.0526 * D * 0.0001 / NPARAM


def draw_lengths(key, part):
    key = jax.random.fold_in(key, 1)
    short = jax.random.randint(key, (MB, PACKS), SHORT // 2, SHORT + 1)
    short = short.at[0, 0].set(SHORT).at[0, PACKS - 1].set(SHORT // 2)
    longer = jnp.full((MB, PACKS), LONG, jnp.int32)
    return jnp.stack([longer, short.astype(jnp.int32)], axis=-1)


def draw_res_weights(key, part):
    key = jax.random.fold_in(key, 2)
    index = jnp.arange(PACKS)
    ramp = 3 * (index // N_FSDP) // N_SEQ + 3 * (index % N_FSDP) // N_FSDP
    noise = jax.random.randint(key, (MB, PACKS, 2), 0, 2)
    weights = 1 + noise + ramp[None, :, None]
    weights = weights.at[0, 0, 0].set(1).at[0, PACKS - 1, 0].set(6)
    return weights.astype(jnp.int32)


def draw_block_slot(key, part):
    key = jax.random.fold_in(key, 3)
    order = jax.random.permutation(key, SHSLOTS - 2) + 1
    chosen = jnp.concatenate([jnp.array([0, SHSLOTS - 1], jnp.int32), order[:BLOCKS - 2].astype(jnp.int32)])
    return jax.random.permutation(jax.random.fold_in(key, 7), chosen).astype(jnp.int32)


def draw_blocks(key, part):
    key = jax.random.fold_in(key, 5)
    factors = jnp.array([1.0, 1.0, 1.0, 1.0, 4.0, 1.0, 1.0, 1.0, 1.0, 0.5, 0.5, 0.5, 0.5], jnp.float32) * D ** (-0.5)
    values = jax.random.normal(key, (BLOCKS, D, D), jnp.float32)
    return values * factors[:, None, None]


def draw_gains(key, part):
    key = jax.random.fold_in(key, 6)
    steps = jnp.arange(D, dtype=jnp.float32) / (D - 1)
    ramp = 0.6 + 1.2 * steps
    noise = jnp.clip(0.15 * jax.random.normal(key, (5, D), jnp.float32), -0.45, 0.45)
    return ramp[None, :] * (1.0 + noise)


def draw_left_stats(key, part):
    key = jax.random.fold_in(key, 11)
    return symmetric(key, 2.0 * stat_scale(), 0.69, 0.3)


def draw_right_stats(key, part):
    key = jax.random.fold_in(key, 12)
    return symmetric(key, 2.0 * stat_scale(), 0.69, 0.3)


def draw_left_roots(key, part):
    key = jax.random.fold_in(key, 13)
    return symmetric(key, stat_scale() ** (-0.25), 0.69, 0.3)


def draw_right_roots(key, part):
    key = jax.random.fold_in(key, 14)
    return symmetric(key, stat_scale() ** (-0.25), 0.69, 0.3)


def set_ends(values, rng, least, top_value):
    extent = values.shape
    place = [jax.random.randint(jax.random.fold_in(rng, axis), (), 0, extent[axis]) for axis in range(len(extent))]
    values = values.at[tuple(place)].set(least)
    longest = extent.index(max(extent))
    place[longest] = (place[longest] + 1) % extent[longest]
    return values.at[tuple(place)].set(top_value)


def block_levels(stream_key, shape, shards, least, high):
    level = 1.0
    for axis_at, blocks in shards:
        draws = jax.random.uniform(jax.random.fold_in(jax.random.fold_in(stream_key, 6), axis_at), (blocks,), jnp.float32, least / len(shards), high / len(shards))
        level = level * jnp.repeat(jnp.exp(draws), shape[axis_at] // blocks).reshape((-1,) + (1,) * (len(shape) - 1 - axis_at))
    return level


def normal_values(key, shape, scale, bound, pieces=(), held_as=jnp.bfloat16):
    result = scale * jax.random.normal(key, shape, jnp.float32)
    if pieces:
        result = result * block_levels(key, shape, pieces, -0.22, 0.18)
    return jnp.clip(result, -bound, bound).astype(held_as)


def setup_inputs(seed: int = 0) -> dict:
    arg_keys = jax.random.split(jax.random.key(seed), 21)
    return {
        "patches": normal_values(arg_keys[0], (MB, PACKS, PACK, PIX), 1.0, 6.0, ((1, 32),)),
        "positions": set_ends(jax.random.randint(arg_keys[1], (2, MB, PACKS, PACK), 0, GRID), jax.random.fold_in(arg_keys[1], 1), 0, GRID - 1).astype(jnp.int32),
        "lengths": draw_lengths(jax.random.fold_in(arg_keys[20], 71), 0),
        "res_weights": draw_res_weights(jax.random.fold_in(arg_keys[20], 71), 0),
        "labels": set_ends(jax.random.randint(arg_keys[4], (MB, PACKS, 2), 0, CLASSES), jax.random.fold_in(arg_keys[4], 1), 0, CLASSES - 1).astype(jnp.int32),
        "block_slot": draw_block_slot(jax.random.fold_in(arg_keys[20], 71), 0),
        "blocks": draw_blocks(jax.random.fold_in(arg_keys[20], 71), 0),
        "pos_table": normal_values(arg_keys[7], (2, GRID, D), 0.5, 3.0, ((2, 8),), jnp.float32),
        "gains": draw_gains(jax.random.fold_in(arg_keys[20], 71), 0),
        "head": normal_values(arg_keys[9], (D, CLASSES), D ** -0.5, 0.21875, ((0, 8),), jnp.float32),
        "left_stats": draw_left_stats(jax.random.fold_in(arg_keys[20], 71), 0),
        "right_stats": draw_right_stats(jax.random.fold_in(arg_keys[20], 71), 0),
        "left_roots": draw_left_roots(jax.random.fold_in(arg_keys[20], 71), 0),
        "right_roots": draw_right_roots(jax.random.fold_in(arg_keys[20], 71), 0),
        "pos_first": normal_values(arg_keys[14], (2, GRID, D), (0.0011 * NPARAM ** -0.5), 5.7220458984375e-06, ((2, 8),), jnp.float32),
        "pos_second": jnp.clip(jnp.exp(math.log(2.4596338420862507e-12) - 1.37681563 * jax.random.uniform(arg_keys[15], (2, GRID, D), jnp.float32) ** block_levels(arg_keys[15], (2, GRID, D), ((2, 8),), -0.2, 0.2)), 6.207647243461345e-13, 2.4596338420862507e-12),
        "gain_first": normal_values(arg_keys[16], (5, D), (0.0055 * NPARAM ** -0.5), 2.6702880859375e-05, ((1, 8),), jnp.float32),
        "gain_second": jnp.clip(jnp.exp(math.log(6.20764759040604e-11) - 1.4053426 * jax.random.uniform(arg_keys[17], (5, D), jnp.float32) ** block_levels(arg_keys[17], (5, D), ((1, 8),), -0.2, 0.2)), 1.522630459216412e-11, 6.20764759040604e-11),
        "head_first": normal_values(arg_keys[18], (D, CLASSES), (0.0011 * NPARAM ** -0.5), 5.7220458984375e-06, ((0, 8),), jnp.float32),
        "head_second": jnp.clip(jnp.exp(math.log(2.4596338420862507e-12) - 1.37681563 * jax.random.uniform(arg_keys[19], (D, CLASSES), jnp.float32) ** block_levels(arg_keys[19], (D, CLASSES), ((0, 8),), -0.2, 0.2)), 6.207647243461345e-13, 2.4596338420862507e-12),
    }


highest = lax.Precision.HIGHEST
norm_eps = 1e-06
clip_bound = 0.01
stat_decay = 0.95
shampoo_rate = 0.1
decay_rate = 0.01
first_decay = 0.9
second_decay = 0.95
adam_rate = 0.04
table_rate = 0.5
gain_rate = 0.25
adam_eps = 1e-10

@jax.custom_vjp
def low(v):
    return lax.optimization_barrier(v.astype(jnp.bfloat16)).astype(jnp.float32)

@jax.custom_vjp
def low_back(v):
    return v

def low_keep(v):
    return (low(v), None)

def low_pass(kept, grad):
    return (grad,)

def back_keep(v):
    return (v, None)

def back_low(kept, grad):
    return (low(grad),)
low.defvjp(low_keep, low_pass)
low_back.defvjp(back_keep, back_low)

def layer_norm(values, gain):
    centred = values - lax.optimization_barrier(jnp.mean(values, axis=-1, keepdims=True))
    return centred * lax.rsqrt(lax.optimization_barrier(jnp.mean(centred * centred, axis=-1, keepdims=True)) + norm_eps) * gain

def product(left, right):
    return jnp.dot(left, right, precision=highest)

def pack_loss(params, item):
    blocks, table, gains, head = params
    patch_rows, place_rows, place_cols, pack_lengths, pack_weights, pack_labels = item
    width = blocks.shape[1]
    tokens = jnp.arange(PACK)
    segment = (tokens >= pack_lengths[0]).astype(jnp.int32) + (tokens >= pack_lengths[0] + pack_lengths[1]).astype(jnp.int32)
    grid = jnp.arange(GRID)
    row_hot = (place_rows[:, None] == grid[None, :]).astype(jnp.float32)
    col_hot = (place_cols[:, None] == grid[None, :]).astype(jnp.float32)
    embed = low_back(product(patch_rows, blocks[0]) + product(row_hot, table[0]) + product(col_hot, table[1]))
    first = low(layer_norm(embed, gains[0]))
    query = low_back(product(first, blocks[1])).reshape(PACK, HEADS, HEAD)
    keys = low_back(product(first, blocks[2])).reshape(PACK, HEADS, HEAD)
    values = low(low_back(product(first, blocks[3]))).reshape(PACK, HEADS, HEAD)
    query = low(layer_norm(query, gains[1].reshape(HEADS, HEAD)))
    keys = low(layer_norm(keys, gains[2].reshape(HEADS, HEAD)))
    scores = low_back(jnp.einsum('qhd,khd->hqk', query, keys, precision=highest) * HEAD ** (-0.5))
    same = segment[:, None] == segment[None, :]
    scores = jnp.where(same[None], scores, -1e+30)
    peak = lax.optimization_barrier(jnp.max(scores, axis=-1, keepdims=True))
    expo = jnp.exp(scores - peak)
    probs = low(expo / lax.optimization_barrier(jnp.sum(expo, axis=-1, keepdims=True)))
    mixed = low(low_back(jnp.einsum('hqk,khd->qhd', probs, values, precision=highest))).reshape(PACK, width)
    resid = embed + low_back(product(mixed, blocks[4]))
    second = low(layer_norm(resid, gains[3]))
    up = low_back(jnp.concatenate([product(second, blocks[5 + j]) for j in range(4)], axis=1))
    act = low(jax.nn.gelu(up, approximate=False))
    down = product(act[:, :width], blocks[9])
    for j in range(1, 4):
        down = down + product(act[:, j * width:(j + 1) * width], blocks[9 + j])
    final = layer_norm(resid + low_back(down), gains[4])
    member = (segment[None, :] == jnp.arange(2)[:, None]).astype(jnp.float32) / pack_lengths[:, None].astype(jnp.float32)
    pooled = low(product(member, final))
    logits = low_back(product(pooled, head))
    peak_logit = lax.optimization_barrier(jnp.max(logits, axis=-1, keepdims=True))
    log_total = peak_logit[:, 0] + jnp.log(lax.optimization_barrier(jnp.sum(jnp.exp(logits - peak_logit), axis=-1)))
    labels_hot = (pack_labels[:, None] == jnp.arange(CLASSES)[None, :]).astype(jnp.float32)
    picked = lax.optimization_barrier(jnp.sum(logits * labels_hot, axis=-1))
    return jnp.sum(pack_weights.astype(jnp.float32) * (log_total - picked))

def adam(weight, grad, first, second, rate, decay):
    first_new = first_decay * first + (1 - first_decay) * grad
    second_new = second_decay * second + (1 - second_decay) * grad * grad
    corrected = first_new / (1 - first_decay ** STEP) / (jnp.sqrt(second_new / (1 - second_decay ** STEP)) + adam_eps)
    return (weight - rate * (corrected + decay * weight), first_new, second_new)

def reference(patches, positions, lengths, res_weights, labels, block_slot, blocks, pos_table, gains, head, left_stats, right_stats, left_roots, right_roots, pos_first, pos_second, gain_first, gain_second, head_first, head_second):
    count = MB * PACKS
    items = (patches.astype(jnp.float32).reshape(count, PACK, PIX), positions[0].reshape(count, PACK), positions[1].reshape(count, PACK), lengths.reshape(count, 2), res_weights.reshape(count, 2), labels.reshape(count, 2))
    checked = jax.checkpoint(pack_loss)

    def total_loss(params):
        rounded = tuple((low(piece) for piece in params))

        def one_pack(carry, item):
            return (carry + checked(rounded, item), None)
        summed, _ = lax.scan(one_pack, jnp.zeros((), jnp.float32), items)
        return summed
    loss_sum, pullback = jax.vjp(total_loss, (blocks, pos_table, gains, head))
    grads = pullback(jnp.ones((), jnp.float32))[0]
    weight_sum = jnp.sum(res_weights).astype(jnp.float32)
    grads = tuple((piece / weight_sum for piece in grads))
    squares = jnp.sum(grads[0] * grads[0]) + jnp.sum(grads[1] * grads[1]) + jnp.sum(grads[2] * grads[2]) + jnp.sum(grads[3] * grads[3])
    clip_norm = jnp.sqrt(squares)
    factor = jnp.minimum(1.0, clip_bound / clip_norm)
    block_grads, table_grad, gain_grad, head_grad = tuple((piece * factor for piece in grads))
    slotted = jnp.zeros((SHSLOTS, D, D), jnp.float32).at[block_slot].set(block_grads)
    left_new = stat_decay * left_stats + (1 - stat_decay) * jnp.einsum('sij,skj->sik', slotted, slotted, precision=highest)
    right_new = stat_decay * right_stats + (1 - stat_decay) * jnp.einsum('sji,sjk->sik', slotted, slotted, precision=highest)
    inner = jnp.einsum('sij,sjk->sik', slotted, right_roots, precision=highest)
    direction = jnp.einsum('sij,sjk->sik', left_roots, inner, precision=highest)
    blocks_new = blocks - shampoo_rate * (direction[block_slot] + decay_rate * blocks)
    pos_new, pos_first_new, pos_second_new = adam(pos_table, table_grad, pos_first, pos_second, table_rate, decay_rate)
    gains_new, gain_first_new, gain_second_new = adam(gains, gain_grad, gain_first, gain_second, gain_rate, 0.0)
    head_new, head_first_new, head_second_new = adam(head, head_grad, head_first, head_second, adam_rate, decay_rate)
    return (blocks_new, block_grads, left_new, right_new, pos_new, pos_first_new, pos_second_new, gains_new, gain_first_new, gain_second_new, head_new, head_first_new, head_second_new, clip_norm, loss_sum, weight_sum)
```

```python
import functools
import math
import jax
import jax.numpy as jnp
from jax import lax
from jax.experimental import pallas as pl
from jax.experimental.pallas import tpu as pltpu
from jax.sharding import PartitionSpec as P

HEADS = 12
HEAD = 64
PACK = 1536
LONG = 1152
SHORT = 256
ROWS = LONG + SHORT
TILE = 352
STEP = 10
clip_bound = 0.01
stat_decay = 0.95
shampoo_rate = 0.1
decay_rate = 0.01
first_decay = 0.9
second_decay = 0.95
adam_rate = 0.04
table_rate = 0.5
gain_rate = 0.25
adam_eps = 1e-10
norm_eps = 1e-06
narrow = jnp.bfloat16
wide = jnp.float32
log2e = math.log2(math.e)
VM = 60 * 1024 * 1024


def params(limit=VM):
    return pltpu.CompilerParams(vmem_limit_bytes=limit)


def dot(a, b, ca=1, cb=0):
    return lax.dot_general(a, b, (((ca,), (cb,)), ((), ())), preferred_element_type=wide)


def norm_rows(v):
    c = v - jnp.mean(v, axis=-1, keepdims=True)
    r = lax.rsqrt(jnp.mean(c * c, axis=-1, keepdims=True) + norm_eps)
    return c * r, r


def back_rows(unit, r, scaled):
    return r * (
        scaled
        - jnp.mean(scaled, axis=-1, keepdims=True)
        - unit * jnp.mean(scaled * unit, axis=-1, keepdims=True)
    )


def spec(shape, index):
    return pl.BlockSpec(shape, index)


def held(shape):
    return pl.BlockSpec(shape, lambda *_: (0,) * len(shape), pipeline_mode=pl.Buffered(1))


def cost(flops, moved, trans=0):
    return pl.CostEstimate(flops=int(flops), bytes_accessed=int(moved), transcendentals=int(trans))


def embed_kernel(patch_ref, hot_ref, e_ref, table_ref, gain_ref, embed_ref, first_ref):
    v = dot(patch_ref[0, 0], e_ref[...]) + dot(hot_ref[0], table_ref[...])
    embed_ref[0] = v
    unit, _ = norm_rows(v)
    first_ref[0] = (unit * gain_ref[0:1]).astype(narrow)


def embed_call(patches, hot, e, table, gains):
    mb, width = patches.shape[0], e.shape[1]
    steps = ROWS // TILE
    return pl.pallas_call(
        embed_kernel,
        grid=(mb, steps),
        in_specs=[
            spec((1, 1, TILE, patches.shape[3]), lambda m, i: (m, 0, i, 0)),
            spec((1, TILE, hot.shape[2]), lambda m, i: (m, i, 0)),
            held(e.shape),
            held(table.shape),
            held(gains.shape),
        ],
        out_specs=[spec((1, TILE, width), lambda m, i: (m, i, 0))] * 2,
        out_shape=[
            jax.ShapeDtypeStruct((mb, ROWS, width), wide),
            jax.ShapeDtypeStruct((mb, ROWS, width), narrow),
        ],
        compiler_params=params(),
        cost_estimate=cost(2 * mb * ROWS * width * 896, 20e6),
    )(patches, hot, e, table, gains)


def group_mean(v, ones):
    return jnp.concatenate(
        [dot(v[:, at : at + 256].astype(narrow), ones) for at in range(0, v.shape[1], 256)], axis=1
    )


def project_kernel(first_ref, w_ref, gain_ref, ones_ref, q_ref, k_ref, v_ref, qraw_ref, kraw_ref):
    x = first_ref[0]
    ones = ones_ref[...]
    for i, (ref, raw_ref) in enumerate(((q_ref, qraw_ref), (k_ref, kraw_ref))):
        raw = dot(x, w_ref[i])
        raw_ref[0] = raw.astype(narrow)
        c = raw - group_mean(raw, ones)
        r = lax.rsqrt(group_mean(c * c, ones) + norm_eps)
        out = (c * r * gain_ref[1 + i : 2 + i]).astype(narrow)
        if i == 0:
            out = out * narrow(HEAD**-0.5)
        ref[0] = out
    v_ref[0] = dot(x, w_ref[2]).astype(narrow)


def project_call(first, w, gains, ones):
    mb, _, width = first.shape
    rows = spec((1, TILE, width), lambda m, i: (m, i, 0))
    return pl.pallas_call(
        project_kernel,
        grid=(mb, ROWS // TILE),
        in_specs=[rows, held(w.shape), held(gains.shape), held(ones.shape)],
        out_specs=[rows] * 5,
        out_shape=[jax.ShapeDtypeStruct((mb, ROWS, width), narrow)] * 5,
        compiler_params=params(),
        cost_estimate=cost(2 * mb * ROWS * width * width * 3, 30e6),
    )(first, w, gains, ones)


ROWS_Q = 384


def attend_kernel(lengths_ref, q_ref, k_ref, v_ref, mixed_ref, rest_ref, stat_ref):
    pack, pair = pl.program_id(0), pl.program_id(1)
    lane = lax.broadcasted_iota(jnp.int32, (1, 2 * HEAD), 1)

    def part(start, count, tile, masked):
        k = k_ref[0, start : start + count]
        v = v_ref[0, start : start + count]
        zero = jnp.zeros_like(k)
        one = jnp.ones_like(k)
        k_both = [jnp.where(lane < HEAD, k, zero), jnp.where(lane < HEAD, zero, k)]
        ext = jnp.concatenate(
            [
                jnp.concatenate([jnp.where(lane < HEAD, v, zero), jnp.where(lane < HEAD, one, zero)], axis=1),
                jnp.concatenate([jnp.where(lane < HEAD, zero, v), jnp.where(lane < HEAD, zero, one)], axis=1),
            ],
            axis=0,
        )
        for at in range(start, start + count, tile):
            q = q_ref[0, at : at + tile]
            expos, peaks = [], []
            for h in range(2):
                s = dot(q, k_both[h], 1, 1)
                if masked:
                    limit = lengths_ref[pack, 1]
                    row = lax.broadcasted_iota(jnp.int32, s.shape, 0) + (at - start)
                    col = lax.broadcasted_iota(jnp.int32, s.shape, 1)
                    s = jnp.where((row < limit) == (col < limit), s, -1e30)
                peak = jnp.max(s, axis=1, keepdims=True)
                expos.append(jnp.exp2(s * log2e - peak * log2e).astype(narrow))
                peaks.append(peak)
            both = dot(jnp.concatenate(expos, axis=1), ext)
            total = both[:, 2 * HEAD :]
            mixed = both[:, : 2 * HEAD] / total
            rounded = mixed.astype(narrow)
            mixed_ref[0, at : at + tile] = rounded
            rest_ref[0, at : at + tile] = (mixed - rounded.astype(wide)).astype(narrow)
            lse = (jnp.where(lane < HEAD, peaks[0], peaks[1]) + jnp.log(total)) * log2e
            for h in range(2):
                column = jnp.sum(jnp.where(lane == h * HEAD, lse, 0.0), axis=1, keepdims=True)
                old = stat_ref[0, at : at + tile]
                stat_ref[0, at : at + tile] = jnp.where(lane == 2 * pair + h, column, old)

    part(0, LONG, ROWS_Q, False)
    part(LONG, SHORT, SHORT, True)


def attend_call(lengths, q, k, v):
    mb, _, width = q.shape
    block = pl.BlockSpec((1, ROWS, 2 * HEAD), lambda m, p, *_: (m, 0, p))
    pairs = width // (2 * HEAD)
    moved = mb * ROWS * width * 8
    return pl.pallas_call(
        attend_kernel,
        grid_spec=pltpu.PrefetchScalarGridSpec(
            num_scalar_prefetch=1,
            grid=(mb, pairs),
            in_specs=[block] * 3,
            out_specs=[block, block, pl.BlockSpec((1, ROWS, 128), lambda m, p, *_: (m, 0, 0))],
        ),
        out_shape=[
            jax.ShapeDtypeStruct((mb, ROWS, width), narrow),
            jax.ShapeDtypeStruct((mb, ROWS, width), narrow),
            jax.ShapeDtypeStruct((mb, ROWS, 128), wide),
        ],
        compiler_params=params(),
        cost_estimate=cost(16 * mb * 2 * pairs * (LONG**2 + SHORT**2) * HEAD, moved),
    )(lengths, q, k, v)


def cdf_and_slope(up):
    e = jnp.exp2(up * up * (-0.5 * log2e))
    d = 1.0 + (0.3275911 * 0.5**0.5) * jnp.abs(up)
    t = pl.reciprocal(d, approx=True)
    t = t * (2.0 - d * t)
    poly = t * (0.5 * 1.061405429) + (0.5 * -1.453152027)
    poly = poly * t + (0.5 * 1.421413741)
    poly = poly * t + (0.5 * -0.284496736)
    poly = poly * t + (0.5 * 0.254829592)
    tail = poly * t * e
    cdf = jnp.where(up < 0, tail, 1.0 - tail)
    slope = cdf + up * e * 0.3989422804014327
    return cdf, slope


def forward_kernel(
    lengths_ref, embed_ref, mixed_ref, w_ref, gain_ref,
    second_ref, act_ref, slope_ref, unit2_ref, unit3_ref, stat_ref, pool_ref,
):
    pack, step = pl.program_id(0), pl.program_id(1)
    width = embed_ref.shape[2]
    resid = embed_ref[0] + dot(mixed_ref[0], w_ref[0])
    unit, r2 = norm_rows(resid)
    unit2_ref[0] = unit.astype(narrow)
    second = (unit * gain_ref[3:4]).astype(narrow)
    second_ref[0] = second
    outcome = resid
    for j in range(4):
        up = dot(second, w_ref[1 + j])
        cdf, slope = cdf_and_slope(up)
        act = (up * cdf).astype(narrow)
        act_ref[j, 0] = act
        slope_ref[j, 0] = slope.astype(narrow)
        outcome = outcome + dot(act, w_ref[5 + j])
    unit, r3 = norm_rows(outcome)
    unit3_ref[0] = unit.astype(narrow)
    lane = lax.broadcasted_iota(jnp.int32, (1, 128), 1)
    stat_ref[0] = jnp.where(lane == 0, r2, r3)
    final = unit * gain_ref[4:5]

    @pl.when(step == 0)
    def _():
        pool_ref[...] = jnp.zeros_like(pool_ref)

    row = lax.broadcasted_iota(jnp.int32, (TILE, 1), 0) + step * TILE
    first_len, second_len = lengths_ref[pack, 0], lengths_ref[pack, 1]
    inside = (row < first_len, (row >= first_len) & (row < first_len + second_len))
    for s in range(2):
        total = jnp.sum(jnp.where(inside[s], final, 0.0), axis=0, keepdims=True)
        pool_ref[0, s : s + 1] += total


def forward_call(lengths, embed, mixed, w, gains):
    mb, _, width = embed.shape
    rows = pl.BlockSpec((1, TILE, width), lambda m, i, *_: (m, i, 0))
    wider = pl.BlockSpec((4, 1, TILE, width), lambda m, i, *_: (0, m, i, 0))
    return pl.pallas_call(
        forward_kernel,
        grid_spec=pltpu.PrefetchScalarGridSpec(
            num_scalar_prefetch=1,
            grid=(mb, ROWS // TILE),
            in_specs=[rows, rows, held(w.shape), held(gains.shape)],
            out_specs=[
                rows, wider, wider, rows, rows,
                pl.BlockSpec((1, TILE, 128), lambda m, i, *_: (m, i, 0)),
                pl.BlockSpec((1, 8, width), lambda m, i, *_: (m, 0, 0)),
            ],
        ),
        out_shape=[
            jax.ShapeDtypeStruct((mb, ROWS, width), narrow),
            jax.ShapeDtypeStruct((4, mb, ROWS, width), narrow),
            jax.ShapeDtypeStruct((4, mb, ROWS, width), narrow),
            jax.ShapeDtypeStruct((mb, ROWS, width), narrow),
            jax.ShapeDtypeStruct((mb, ROWS, width), narrow),
            jax.ShapeDtypeStruct((mb, ROWS, 128), wide),
            jax.ShapeDtypeStruct((mb, 8, width), wide),
        ],
        compiler_params=params(),
        cost_estimate=cost(2 * mb * ROWS * width * width * 9, 80e6),
    )(lengths, embed, mixed, w, gains)


def head_kernel(pool_ref, scale_ref, weight_ref, label_ref, head_ref, loss_ref, dhead_ref, dpool_ref):
    pooled = (pool_ref[...] * scale_ref[:, 0:1]).astype(narrow)
    logits = dot(pooled, head_ref[...])
    peak = jnp.max(logits, axis=1, keepdims=True)
    expo = jnp.exp(logits - peak)
    total = jnp.sum(expo, axis=1, keepdims=True)
    hot = lax.broadcasted_iota(jnp.int32, logits.shape, 1) == label_ref[:, 0:1]
    picked = jnp.sum(jnp.where(hot, logits, 0.0), axis=1, keepdims=True)
    weight = weight_ref[:, 0:1].astype(wide)
    loss = jnp.where(weight > 0, weight * (peak + jnp.log(total) - picked), 0.0)
    loss_ref[...] = jnp.broadcast_to(jnp.sum(loss, axis=0, keepdims=True), loss_ref.shape)
    dlogits = (weight * (expo / total - hot.astype(wide))).astype(narrow)
    dhead_ref[...] = dot(pooled, dlogits, 0, 0).astype(dhead_ref.dtype)
    dpool_ref[...] = dot(dlogits, head_ref[...], 1, 1) * scale_ref[:, 0:1]


def head_call(pool, scale, weight, label, head, out=wide):
    rows, width = pool.shape
    return pl.pallas_call(
        head_kernel,
        out_shape=[
            jax.ShapeDtypeStruct((8, 128), wide),
            jax.ShapeDtypeStruct(head.shape, out),
            jax.ShapeDtypeStruct((rows, width), wide),
        ],
        compiler_params=params(),
        cost_estimate=cost(6 * rows * width * 1000, 8e6),
    )(pool, scale, weight, label, head)


def backward_kernel(
    lengths_ref, dpool_ref, unit3_ref, unit2_ref, stat_ref, slope_ref, mixed_ref, rest_ref, w_ref, gain_ref, pick_ref,
    dm_ref, dup_ref, dr_ref, dmixed_ref, delta_ref, dgain_ref,
):
    pack, step = pl.program_id(0), pl.program_id(1)
    row = lax.broadcasted_iota(jnp.int32, (TILE, 1), 0) + step * TILE
    first_len, second_len = lengths_ref[pack, 0], lengths_ref[pack, 1]
    dfinal = jnp.where(
        row < first_len,
        dpool_ref[0, 0:1],
        jnp.where(row < first_len + second_len, dpool_ref[0, 1:2], 0.0),
    )
    unit3 = unit3_ref[0].astype(wide)
    r2, r3 = stat_ref[0, :, 0:1], stat_ref[0, :, 1:2]
    doutcome = back_rows(unit3, r3, dfinal * gain_ref[4:5])
    dgf = jnp.sum(dfinal * unit3, axis=0, keepdims=True)
    dm = doutcome.astype(narrow)
    dm_ref[0] = dm
    dsecond = None
    for j in range(4):
        dact = dot(dm, w_ref[5 + j], 1, 1)
        dup = (dact * slope_ref[j, 0].astype(wide)).astype(narrow)
        dup_ref[j, 0] = dup
        term = dot(dup, w_ref[1 + j], 1, 1)
        dsecond = term if dsecond is None else dsecond + term
    unit2 = unit2_ref[0].astype(wide)
    dg2 = jnp.sum(dsecond * unit2, axis=0, keepdims=True)
    dresid = doutcome + back_rows(unit2, r2, dsecond * gain_ref[3:4])
    dr = dresid.astype(narrow)
    dr_ref[0] = dr
    dmixed = dot(dr, w_ref[0], 1, 1).astype(narrow)
    dmixed_ref[0] = dmixed
    product = dmixed.astype(wide) * (mixed_ref[0].astype(wide) + rest_ref[0].astype(wide))
    high = product.astype(narrow)
    low = (product - high.astype(wide)).astype(narrow)
    delta_ref[0] = dot(high, pick_ref[...]) + dot(low, pick_ref[...])

    @pl.when((pack == 0) & (step == 0))
    def _():
        dgain_ref[...] = jnp.zeros_like(dgain_ref)

    dgain_ref[3:4] += dg2
    dgain_ref[4:5] += dgf


def backward_call(lengths, dpool, unit3, unit2, stat, slope, mixed, rest, w, gains, pick):
    mb, _, width = unit3.shape
    rows = pl.BlockSpec((1, TILE, width), lambda m, i, *_: (m, i, 0))
    lanes = pl.BlockSpec((1, TILE, 128), lambda m, i, *_: (m, i, 0))
    wider = pl.BlockSpec((4, 1, TILE, width), lambda m, i, *_: (0, m, i, 0))
    return pl.pallas_call(
        backward_kernel,
        grid_spec=pltpu.PrefetchScalarGridSpec(
            num_scalar_prefetch=1,
            grid=(mb, ROWS // TILE),
            in_specs=[
                pl.BlockSpec((1, 2, width), lambda m, i, *_: (m, 0, 0)),
                rows, rows, lanes, wider, rows, rows,
                held(w.shape), held(gains.shape), held(pick.shape),
            ],
            out_specs=[rows, wider, rows, rows, lanes, pl.BlockSpec((8, width), lambda m, i, *_: (0, 0))],
        ),
        out_shape=[
            jax.ShapeDtypeStruct((mb, ROWS, width), narrow),
            jax.ShapeDtypeStruct((4, mb, ROWS, width), narrow),
            jax.ShapeDtypeStruct((mb, ROWS, width), narrow),
            jax.ShapeDtypeStruct((mb, ROWS, width), narrow),
            jax.ShapeDtypeStruct((mb, ROWS, 128), wide),
            jax.ShapeDtypeStruct((8, width), wide),
        ],
        compiler_params=params(),
        cost_estimate=cost(2 * mb * ROWS * width * width * 9, 70e6),
    )(lengths, dpool, unit3, unit2, stat, slope, mixed, rest, w, gains, pick)


def attend_back_kernel(
    lengths_ref, q_ref, k_ref, v_ref, do_ref, qraw_ref, kraw_ref, stat_ref, gain_ref, ones_ref,
    dq_ref, dk_ref, dv_ref, dgain_ref, dq_acc, dk_acc, dv_acc,
):
    pack = pl.program_id(1)
    lane = lax.broadcasted_iota(jnp.int32, (1, 2 * HEAD), 1)

    def both(x, axis=0):
        zero = jnp.zeros_like(x)
        return jnp.concatenate([jnp.where(lane < HEAD, x, zero), jnp.where(lane < HEAD, zero, x)], axis=axis)

    def part(start, count, tile, chunk, masked):
        for ti in range(start, start + count, tile):
            q2 = both(q_ref[0, ti : ti + tile])
            do2 = both(do_ref[0, ti : ti + tile])
            lse = jnp.concatenate([stat_ref[0, h : h + 1, ti : ti + tile] for h in (0, 1)], axis=1)
            delta = jnp.concatenate([stat_ref[0, h : h + 1, ti : ti + tile] for h in (2, 3)], axis=1)
            for ui in range(start, start + count, chunk):
                k = k_ref[0, ui : ui + chunk]
                v = v_ref[0, ui : ui + chunk]
                s = dot(k, q2, 1, 1)
                p = jnp.exp2(s * log2e - lse)
                if masked:
                    limit = lengths_ref[pack, 1]
                    row = lax.broadcasted_iota(jnp.int32, s.shape, 0) + (ui - start)
                    col = lax.broadcasted_iota(jnp.int32, s.shape, 1)
                    col = jnp.where(col < tile, col, col - tile) + (ti - start)
                    p = jnp.where((row < limit) == (col < limit), p, 0.0)
                dp = dot(v, do2, 1, 1)
                ds = (p * (dp - delta)).astype(narrow)
                dv_new = dot(p.astype(narrow), do2)
                dk_new = dot(ds, q2)
                k2 = both(k)
                ds_rows = jnp.concatenate([ds[:, :tile], ds[:, tile:]], axis=0)
                dq_new = dot(ds_rows, k2, 0, 0)
                if ti == start:
                    dv_acc[ui : ui + chunk] = dv_new
                    dk_acc[ui : ui + chunk] = dk_new
                else:
                    dv_acc[ui : ui + chunk] += dv_new
                    dk_acc[ui : ui + chunk] += dk_new
                if ui == start:
                    dq_acc[ti : ti + tile] = dq_new
                else:
                    dq_acc[ti : ti + tile] += dq_new

    part(0, LONG, 384, 384, False)
    part(LONG, SHORT, SHORT, SHORT, True)
    dv_ref[0] = dv_acc[...].astype(narrow)
    ones = ones_ref[...]

    def mean(x):
        return dot(x.astype(narrow), ones)

    @pl.when(pack == 0)
    def _():
        dgain_ref[...] = jnp.zeros_like(dgain_ref)

    for i, (acc, raw_ref, ref, factor) in enumerate(
        ((dq_acc, qraw_ref, dq_ref, HEAD**-0.5), (dk_acc, kraw_ref, dk_ref, 1.0))
    ):
        raw = raw_ref[0].astype(wide)
        c = raw - mean(raw)
        r = lax.rsqrt(mean(c * c) + norm_eps)
        unit = c * r
        dy = acc[...] * factor
        dgain_ref[0, i : i + 1] += jnp.sum(dy * unit, axis=0, keepdims=True)
        scaled = dy * gain_ref[1 + i : 2 + i]
        ref[0] = (r * (scaled - mean(scaled) - unit * mean(scaled * unit))).astype(narrow)


def attend_back_call(lengths, q, k, v, do, qraw, kraw, stat, gains, ones, first_pair, pairs):
    mb, _, width = q.shape
    block = pl.BlockSpec((1, ROWS, 2 * HEAD), lambda p, m, *_: (m, 0, p + first_pair))
    out = pl.BlockSpec((1, ROWS, 2 * HEAD), lambda p, m, *_: (m, 0, p))
    shape = jax.ShapeDtypeStruct((mb, ROWS, pairs * 2 * HEAD), narrow)
    return pl.pallas_call(
        attend_back_kernel,
        grid_spec=pltpu.PrefetchScalarGridSpec(
            num_scalar_prefetch=1,
            grid=(pairs, mb),
            in_specs=[
                block, block, block, block, block, block,
                pl.BlockSpec((1, 8, ROWS), lambda p, m, *_: (m, p + first_pair, 0)),
                pl.BlockSpec((8, 2 * HEAD), lambda p, m, *_: (0, p + first_pair)),
                pl.BlockSpec((2 * HEAD, 2 * HEAD), lambda p, m, *_: (0, 0)),
            ],
            out_specs=[out, out, out, pl.BlockSpec((1, 8, 2 * HEAD), lambda p, m, *_: (p, 0, 0))],
            scratch_shapes=[pltpu.VMEM((ROWS, 2 * HEAD), wide)] * 3,
        ),
        out_shape=[shape, shape, shape, jax.ShapeDtypeStruct((pairs, 8, 2 * HEAD), wide)],
        compiler_params=params(),
        cost_estimate=cost(20 * mb * 2 * pairs * (LONG**2 + SHORT**2) * HEAD * 2, mb * ROWS * pairs * 128 * 18),
    )(lengths, q, k, v, do, qraw, kraw, stat, gains, ones)


def first_kernel(*refs, parts):
    grads = refs[: 3 * parts]
    embed_ref, dr_ref, w_ref, gain_ref, out_ref, dgain_ref = refs[3 * parts :]
    step = pl.program_id(0) * pl.num_programs(1) + pl.program_id(1)
    total = None
    for i in range(3):
        rows = jnp.concatenate([grads[3 * p + i][0] for p in range(parts)], axis=1)
        term = dot(rows, w_ref[i], 1, 1)
        total = term if total is None else total + term
    unit, r = norm_rows(embed_ref[0])

    @pl.when(step == 0)
    def _():
        dgain_ref[...] = jnp.zeros_like(dgain_ref)

    dgain_ref[0:1] += jnp.sum(total * unit, axis=0, keepdims=True)
    out_ref[0] = (dr_ref[0].astype(wide) + back_rows(unit, r, total * gain_ref[0:1])).astype(narrow)


def first_call(grads, embed, dr, w, gains):
    mb, _, width = embed.shape
    rows = spec((1, TILE, width), lambda m, i: (m, i, 0))
    parts = len(grads) // 3
    return pl.pallas_call(
        functools.partial(first_kernel, parts=parts),
        grid=(mb, ROWS // TILE),
        in_specs=[spec((1, TILE, g.shape[2]), lambda m, i: (m, i, 0)) for g in grads]
        + [rows, rows, held(w.shape), held(gains.shape)],
        out_specs=[rows, spec((8, width), lambda m, i: (0, 0))],
        out_shape=[
            jax.ShapeDtypeStruct((mb, ROWS, width), narrow),
            jax.ShapeDtypeStruct((8, width), wide),
        ],
        compiler_params=params(),
        cost_estimate=cost(2 * mb * ROWS * width * width * 3, 32e6),
    )(*grads, embed, dr, w, gains)


def fold(parts):
    while len(parts) > 1:
        parts = [parts[i] + parts[i + 1] for i in range(0, len(parts), 2)]
    return parts[0]


def swap(x, axis, bits):
    if bits == 0:
        return x
    return lax.ppermute(x, axis, [(i, i ^ bits) for i in range(lax.axis_size(axis))])


def tied(x, *after):
    return lax.optimization_barrier((x, *after))[0]


def pick_index(x, index, dim):
    return lax.dynamic_index_in_dim(x, index, dim, keepdims=False)


def y_size():
    return 1 << ((lax.axis_size("fsdp").bit_length() - 1) // 2)


def levels():
    across, deep = lax.axis_size("seq"), lax.axis_size("fsdp")
    y = y_size()
    return (("seq", 1, 2), ("seq", 2, across // 2), ("fsdp", 1, y), ("fsdp", y, deep // y))


def scatter_sum(grad):
    n, rows, width = grad.shape
    core, x, y, z = levels()
    part = rows // (core[2] * x[2] * y[2] * z[2])
    view = grad.reshape(n, z[2], y[2], x[2], core[2], part, width)
    for dim, (axis, stride, size) in ((4, core), (3, x), (2, y), (1, z)):
        at = lax.axis_index(axis) // stride % size
        parts = [
            swap(pick_index(view, at ^ k, dim).astype(narrow), axis, k * stride).astype(wide)
            for k in range(size)
        ]
        view = fold(parts)
    return view


def all_sum(x):
    for axis in ("fsdp", "seq"):
        x = fold([swap(x, axis, k) for k in range(lax.axis_size(axis))])
    return x


def place_kernel(*refs, count):
    base_ref, sources, out_ref, sem = refs[0], refs[1 : 1 + count], refs[1 + count], refs[2 + count]
    copies = [
        pltpu.make_async_copy(ref, out_ref.at[base_ref[0] ^ i], sem.at[i]) for i, ref in enumerate(sources)
    ]
    for copy in copies:
        copy.start()
    for copy in copies:
        copy.wait()


def placed(parts, base):
    return pl.pallas_call(
        functools.partial(place_kernel, count=len(parts)),
        in_specs=[pl.BlockSpec(memory_space=pltpu.SMEM)] + [pl.BlockSpec(memory_space=pl.ANY)] * len(parts),
        out_specs=pl.BlockSpec(memory_space=pl.ANY),
        out_shape=jax.ShapeDtypeStruct((len(parts), *parts[0].shape), parts[0].dtype),
        scratch_shapes=[pltpu.SemaphoreType.DMA((len(parts),))],
        cost_estimate=cost(0, 2 * len(parts) * parts[0].size * 2),
    )(base.reshape(1).astype(jnp.int32), *parts)


def across(x):
    size = lax.axis_size("seq")
    me = lax.axis_index("seq")
    held_parts = [swap(x, "seq", k) for k in range(0, size, 2)]
    pair = held_parts + [swap(part, "seq", 1) for part in held_parts]
    half = size // 2
    order = [pair[(k // 2) + (k % 2) * half] for k in range(size)]
    return placed(order, me)


def gather_rows(shard):
    n, rows, width = shard.shape
    size, deep = lax.axis_size("seq"), lax.axis_size("fsdp")
    me = lax.axis_index("seq")
    mine = pick_index(shard.reshape(n, size, rows // size, width), me, 1)
    every = placed([swap(mine, "fsdp", k) for k in range(deep)], lax.axis_index("fsdp"))
    full = across(every)
    return full.transpose(2, 1, 0, 3, 4).reshape(n, deep * rows, width)


def gather_direct(x):
    return placed([swap(x, "fsdp", k) for k in range(lax.axis_size("fsdp"))], lax.axis_index("fsdp"))


def adam(weight, grad, first, second, rate, decay):
    first_new = first_decay * first + (1 - first_decay) * grad
    second_new = second_decay * second + (1 - second_decay) * grad * grad
    corrected = (
        first_new
        / (1 - first_decay**STEP)
        / (jnp.sqrt(second_new / (1 - second_decay**STEP)) + adam_eps)
    )
    return (weight - rate * (corrected + decay * weight), first_new, second_new)


def product(spec_text, a, b):
    return jnp.einsum(spec_text, a, b, preferred_element_type=wide)


def local(
    patches, positions, lengths, res_weights, labels, block_slot, blocks, pos_table, gains, head,
    left_stats, right_stats, left_roots, right_roots,
    pos_first, pos_second, gain_first, gain_second, head_first, head_second,
):
    mb = patches.shape[0]
    deep, size = lax.axis_size("fsdp"), lax.axis_size("seq")
    me_f, me_s = lax.axis_index("fsdp"), lax.axis_index("seq")
    lengths, res_weights, labels = (x[:, 0] for x in (lengths, res_weights, labels))
    lanes = pos_table.shape[2]
    width = lanes * deep
    grid_rows = pos_table.shape[1]
    low = blocks.astype(narrow)

    small = jnp.concatenate(
        [pos_table.reshape(2 * grid_rows, lanes), gains, jnp.zeros((3, lanes), wide)], axis=0
    ).astype(narrow)
    small = gather_direct(small).transpose(1, 0, 2).reshape(2 * grid_rows + 8, width)
    table = small[: 2 * grid_rows]
    gains_full = small[2 * grid_rows :].astype(wide)
    w_embed = gather_rows(low[0:1])
    w_project = gather_rows(low[1:4])
    w_rest = lax.all_gather(
        pick_index(tied(low[4:13], w_embed).reshape(9, size, -1, width), me_s, 1), ("fsdp", "seq"), axis=1, tiled=True
    )
    w_head = lax.all_gather(
        pick_index(tied(head.astype(narrow), w_embed).reshape(size, -1, head.shape[1]), me_s, 0), ("fsdp", "seq"), axis=0, tiled=True
    )

    places = positions[:, :, 0, :ROWS]
    grid = jnp.arange(grid_rows)
    hot = jnp.concatenate([places[i][:, :, None] == grid for i in range(2)], axis=2).astype(narrow)
    index = jnp.arange(256)
    ones = jnp.where(index[:, None] // HEAD == index[None] // HEAD, 1 / HEAD, 0).astype(narrow)
    pick = (jnp.arange(width)[:, None] // HEAD == jnp.arange(128)[None]).astype(narrow)
    embed, first = embed_call(patches, hot, w_embed[0], table, gains_full)
    query, keys, values, query_raw, key_raw = project_call(first, w_project, gains_full, ones)
    mixed, rest, stat = attend_call(lengths, query, keys, values)
    second, act, slope, unit2, unit3, row_stat, pool = forward_call(lengths, embed, mixed, w_rest, gains_full)

    seqs = 2 * mb
    spare = -seqs % 8

    def column(x):
        return jnp.broadcast_to(jnp.pad(x.reshape(seqs), (0, spare))[:, None], (seqs + spare, 128))

    pool = jnp.pad(pool[:, :2].reshape(seqs, width), ((0, spare), (0, 0)))
    loss, d_head, d_pool = head_call(
        pool, column(1.0 / lengths.astype(wide)), column(res_weights), column(labels), w_head, narrow
    )
    lane = jnp.arange(128)[None]
    totals = all_sum(jnp.where(lane == 0, loss[:1], jnp.where(lane == 1, jnp.sum(res_weights).astype(wide), 0.0)))
    loss_sum, weight_sum = totals[0, 0], totals[0, 1]

    dm, d_up, dr, d_mixed, delta, d_gain_rest = backward_call(
        lengths, d_pool[:seqs].reshape(mb, 2, width), unit3, unit2, row_stat, slope, mixed, rest, w_rest, gains_full, pick
    )
    d_down = product("kmpe,mpd->ked", act, dm).astype(narrow)
    d_upper = product("mpd,kmpe->kde", second, d_up).astype(narrow)
    d_out = product("mpd,mpe->de", mixed, dr).astype(narrow)
    own_down = scatter_sum(d_down)
    own_upper = scatter_sum(d_upper)
    own_out = scatter_sum(d_out[None])
    own_head = scatter_sum(d_head[None])[0]
    pairs = HEADS // 2
    stats = jnp.stack([s[:, :, :HEADS].reshape(mb, ROWS, pairs, 2) for s in (stat, delta)], axis=3)
    stats = jnp.pad(stats.transpose(0, 2, 3, 4, 1).reshape(mb, pairs, 4, ROWS), ((0, 0), (0, 0), (0, 4), (0, 0)))
    stats = stats.reshape(mb, 8 * pairs, ROWS)
    dq, dk, dv, d_gain_heads = attend_back_call(
        lengths, query, keys, values, d_mixed, query_raw, key_raw, stats, gains_full, ones[:128, :128], 0, pairs
    )
    d_project = jnp.stack([product("mpd,mpe->de", first, x).astype(narrow) for x in (dq, dk, dv)])
    own_project = scatter_sum(d_project)
    d_embed, d_gain_first = first_call((dq, dk, dv), embed, dr, w_project, gains_full)
    d_e = product("mpd,mpe->de", patches[:, 0, :ROWS], d_embed).astype(narrow)
    own_e = scatter_sum(d_e[None])
    d_table = product("mpd,mpe->de", hot, d_embed)
    d_gain_heads = d_gain_heads.transpose(1, 0, 2).reshape(8, width)
    d_small = jnp.concatenate(
        [d_table, d_gain_first[:1], d_gain_heads[:2], d_gain_rest[3:5], jnp.zeros((3, width), wide)], axis=0
    )
    d_small = d_small.reshape(-1, deep, lanes).transpose(1, 0, 2)
    d_small = fold([swap(pick_index(d_small, me_f ^ k, 0), "fsdp", k) for k in range(deep)])
    d_small = fold([swap(d_small, "seq", k) for k in range(size)]) / weight_sum

    own = (jnp.concatenate([own_e, own_project, own_out, own_upper, own_down]) / weight_sum).astype(narrow)
    own_head = (own_head / weight_sum).astype(narrow)
    squares = (
        jnp.sum(jnp.square(own.astype(wide)))
        + jnp.sum(jnp.square(own_head.astype(wide)))
        + jnp.where(me_s == 0, jnp.sum(jnp.square(d_small)), 0.0)
    )
    clip_norm = jnp.sqrt(all_sum(jnp.broadcast_to(squares, (1, 128)))[0, 0])
    factor = jnp.minimum(1.0, clip_bound / clip_norm)

    per = left_stats.shape[0]
    part = own.shape[1]
    slot_hot = block_slot[None, :] == jnp.arange(per * deep)[:, None]
    outgoing = jnp.einsum("sb,brd->srd", slot_hot.astype(narrow), own).reshape(deep, per, part, width)
    arrived = placed([swap(pick_index(outgoing, me_f ^ k, 0), "fsdp", k) for k in range(deep)], me_f)
    slotted = across(arrived)
    slotted = slotted.transpose(2, 1, 0, 3, 4).reshape(per, width, width)
    left_part = pick_index(left_roots.reshape(per, deep, size, part, width), me_s, 2).reshape(per, deep * part, width)
    inner = jnp.einsum("sij,sjk->sik", left_part, slotted.astype(wide), precision=lax.Precision.HIGH)
    direction = jnp.einsum("sij,sjk->sik", inner, right_roots, precision=lax.Precision.HIGH).astype(narrow)
    direction = direction.reshape(per, deep, part, width)
    back = placed([swap(pick_index(direction, me_f ^ k, 1), "fsdp", k) for k in range(deep)], me_f)
    back = back.reshape(per * deep, part, width)
    back = jnp.einsum("sb,srd->brd", slot_hot.astype(narrow), back)

    def rows_of(x):
        return x.transpose(1, 0, 2, 3).reshape(x.shape[1], size * part, x.shape[3])

    block_direction = rows_of(across(back)).astype(wide) * factor
    blocks_new = blocks - shampoo_rate * (block_direction + decay_rate * blocks)
    block_grads = rows_of(across(own)).astype(wide) * factor
    gram_left = product("sij,skj->sik", slotted, slotted)
    gram_right = product("sji,sjk->sik", slotted, slotted)
    left_new = stat_decay * left_stats + ((1 - stat_decay) * factor * factor) * gram_left
    right_new = stat_decay * right_stats + ((1 - stat_decay) * factor * factor) * gram_right

    table_grad = d_small[: 2 * grid_rows].reshape(2, grid_rows, lanes) * factor
    gain_grad = d_small[2 * grid_rows : 2 * grid_rows + 5] * factor
    head_grad = rows_of(across(own_head[None]))[0].astype(wide) * factor
    pos_new, pos_first_new, pos_second_new = adam(
        pos_table, table_grad, pos_first, pos_second, table_rate, decay_rate
    )
    gains_new, gain_first_new, gain_second_new = adam(gains, gain_grad, gain_first, gain_second, gain_rate, 0.0)
    head_new, head_first_new, head_second_new = adam(
        head, head_grad, head_first, head_second, adam_rate, decay_rate
    )
    return (
        blocks_new, block_grads, left_new, right_new, pos_new, pos_first_new, pos_second_new,
        gains_new, gain_first_new, gain_second_new, head_new, head_first_new, head_second_new,
        clip_norm, loss_sum, weight_sum,
    )


def solution(mesh):
    placed = (
        P(None, ("seq", "fsdp"), None, None),
        P(None, None, ("seq", "fsdp"), None),
        P(None, ("seq", "fsdp"), None),
        P(None, ("seq", "fsdp"), None),
        P(None, ("seq", "fsdp"), None),
        P(),
        P(None, "fsdp", None),
        P(None, None, "fsdp"),
        P(None, "fsdp"),
        P("fsdp", None),
        P("fsdp", None, None),
        P("fsdp", None, None),
        P("fsdp", None, None),
        P("fsdp", None, None),
        P(None, None, "fsdp"),
        P(None, None, "fsdp"),
        P(None, "fsdp"),
        P(None, "fsdp"),
        P("fsdp", None),
        P("fsdp", None),
    )
    return jax.shard_map(
        local,
        mesh=mesh,
        in_specs=placed,
        out_specs=(
            P(None, "fsdp", None),
            P(None, "fsdp", None),
            P("fsdp", None, None),
            P("fsdp", None, None),
            P(None, None, "fsdp"),
            P(None, None, "fsdp"),
            P(None, None, "fsdp"),
            P(None, "fsdp"),
            P(None, "fsdp"),
            P(None, "fsdp"),
            P("fsdp", None),
            P("fsdp", None),
            P("fsdp", None),
            P(),
            P(),
            P(),
        ),
        check_vma=False,
    )
```

```python
import functools
import math
import jax
import jax.numpy as jnp
from jax import lax
from jax.experimental import pallas as pl
from jax.experimental.pallas import tpu as pltpu
from jax.sharding import PartitionSpec as P

HEADS = 12
HEAD = 64
PACK = 1536
LONG = 1152
SHORT = 256
ROWS = LONG + SHORT
TILE = 352
STEP = 10
clip_bound = 0.01
stat_decay = 0.95
shampoo_rate = 0.1
decay_rate = 0.01
first_decay = 0.9
second_decay = 0.95
adam_rate = 0.04
table_rate = 0.5
gain_rate = 0.25
adam_eps = 1e-10
norm_eps = 1e-06
narrow = jnp.bfloat16
wide = jnp.float32
log2e = math.log2(math.e)
VM = 60 * 1024 * 1024


def params(limit=VM):
    return pltpu.CompilerParams(vmem_limit_bytes=limit)


def dot(a, b, ca=1, cb=0):
    return lax.dot_general(a, b, (((ca,), (cb,)), ((), ())), preferred_element_type=wide)


def norm_rows(v):
    c = v - jnp.mean(v, axis=-1, keepdims=True)
    r = lax.rsqrt(jnp.mean(c * c, axis=-1, keepdims=True) + norm_eps)
    return c * r, r


def back_rows(unit, r, scaled):
    return r * (
        scaled
        - jnp.mean(scaled, axis=-1, keepdims=True)
        - unit * jnp.mean(scaled * unit, axis=-1, keepdims=True)
    )


def spec(shape, index):
    return pl.BlockSpec(shape, index)


def held(shape):
    return pl.BlockSpec(shape, lambda *_: (0,) * len(shape), pipeline_mode=pl.Buffered(1))


def cost(flops, moved, trans=0):
    return pl.CostEstimate(flops=int(flops), bytes_accessed=int(moved), transcendentals=int(trans))


def embed_kernel(patch_ref, hot_ref, e_ref, gain_ref, embed_ref, first_ref):
    width = embed_ref.shape[2]
    v = dot(patch_ref[0, 0], e_ref[:, :width]) + dot(hot_ref[0], e_ref[:, width : width + 128], 1, 1)
    embed_ref[0] = v
    unit, _ = norm_rows(v)
    first_ref[0] = (unit * gain_ref[0:1]).astype(narrow)


def embed_call(patches, hot, e, gains):
    mb, width = patches.shape[0], gains.shape[1]
    steps = ROWS // TILE
    return pl.pallas_call(
        embed_kernel,
        grid=(mb, steps),
        in_specs=[
            spec((1, 1, TILE, patches.shape[3]), lambda m, i: (m, 0, i, 0)),
            spec((1, TILE, hot.shape[2]), lambda m, i: (m, i, 0)),
            held(e.shape),
            held(gains.shape),
        ],
        out_specs=[spec((1, TILE, width), lambda m, i: (m, i, 0))] * 2,
        out_shape=[
            jax.ShapeDtypeStruct((mb, ROWS, width), wide),
            jax.ShapeDtypeStruct((mb, ROWS, width), narrow),
        ],
        compiler_params=params(),
        cost_estimate=cost(2 * mb * ROWS * width * 896, 20e6),
    )(patches, hot, e, gains)


def group_mean(v, ones):
    return jnp.concatenate(
        [dot(v[:, at : at + 256].astype(narrow), ones) for at in range(0, v.shape[1], 256)], axis=1
    )


def project_kernel(first_ref, w_ref, gain_ref, ones_ref, q_ref, k_ref, v_ref, *kept):
    x = first_ref[0]
    width = x.shape[1]
    ones = ones_ref[...]
    for i, ref in enumerate((q_ref, k_ref)):
        raw = dot(x, w_ref[:, i * width : (i + 1) * width])
        c = raw - group_mean(raw, ones)
        r = lax.rsqrt(group_mean(c * c, ones) + norm_eps)
        unit = c * r
        kept[i][0] = unit.astype(narrow)
        kept[2 + i][0] = r.astype(narrow)
        out = (unit * gain_ref[1 + i : 2 + i]).astype(narrow)
        if i == 0:
            out = out * narrow(HEAD**-0.5)
        ref[0] = out
    v_ref[0] = dot(x, w_ref[:, 2 * width :]).astype(narrow)


def project_call(first, w, gains, ones):
    mb, _, width = first.shape
    rows = spec((1, TILE, width), lambda m, i: (m, i, 0))
    return pl.pallas_call(
        project_kernel,
        grid=(mb, ROWS // TILE),
        in_specs=[rows, held(w.shape), held(gains.shape), held(ones.shape)],
        out_specs=[rows] * 7,
        out_shape=[jax.ShapeDtypeStruct((mb, ROWS, width), narrow)] * 7,
        compiler_params=params(),
        cost_estimate=cost(2 * mb * ROWS * width * width * 3, 30e6),
    )(first, w, gains, ones)


ROWS_Q = 384


def attend_kernel(lengths_ref, q_ref, k_ref, v_ref, mixed_ref, rest_ref, stat_ref):
    pack, pair = pl.program_id(0), pl.program_id(1)
    lane = lax.broadcasted_iota(jnp.int32, (1, 2 * HEAD), 1)

    def part(start, count, tile, masked):
        k = k_ref[0, start : start + count]
        v = v_ref[0, start : start + count]
        zero = jnp.zeros_like(k)
        one = jnp.ones_like(k)
        k_both = [jnp.where(lane < HEAD, k, zero), jnp.where(lane < HEAD, zero, k)]
        ext = jnp.concatenate(
            [
                jnp.concatenate([jnp.where(lane < HEAD, v, zero), jnp.where(lane < HEAD, one, zero)], axis=1),
                jnp.concatenate([jnp.where(lane < HEAD, zero, v), jnp.where(lane < HEAD, zero, one)], axis=1),
            ],
            axis=0,
        )
        for at in range(start, start + count, tile):
            q = q_ref[0, at : at + tile]
            expos, peaks = [], []
            for h in range(2):
                s = dot(q, k_both[h], 1, 1)
                if masked:
                    limit = lengths_ref[pack, 1]
                    row = lax.broadcasted_iota(jnp.int32, s.shape, 0) + (at - start)
                    col = lax.broadcasted_iota(jnp.int32, s.shape, 1)
                    s = jnp.where((row < limit) == (col < limit), s, -1e30)
                peak = jnp.max(s, axis=1, keepdims=True)
                expos.append(jnp.exp2(s * log2e - peak * log2e).astype(narrow))
                peaks.append(peak)
            both = dot(jnp.concatenate(expos, axis=1), ext)
            total = both[:, 2 * HEAD :]
            mixed = both[:, : 2 * HEAD] / total
            rounded = mixed.astype(narrow)
            mixed_ref[0, at : at + tile] = rounded
            rest_ref[0, at : at + tile] = (mixed - rounded.astype(wide)).astype(narrow)
            lse = (jnp.where(lane < HEAD, peaks[0], peaks[1]) + jnp.log(total)) * log2e
            for h in range(2):
                column = jnp.sum(jnp.where(lane == h * HEAD, lse, 0.0), axis=1, keepdims=True)
                old = stat_ref[0, at : at + tile]
                stat_ref[0, at : at + tile] = jnp.where(lane == 2 * pair + h, column, old)

    part(0, LONG, ROWS_Q, False)
    part(LONG, SHORT, SHORT, True)


def attend_call(lengths, q, k, v):
    mb, _, width = q.shape
    block = pl.BlockSpec((1, ROWS, 2 * HEAD), lambda m, p, *_: (m, 0, p))
    pairs = width // (2 * HEAD)
    moved = mb * ROWS * width * 8
    return pl.pallas_call(
        attend_kernel,
        grid_spec=pltpu.PrefetchScalarGridSpec(
            num_scalar_prefetch=1,
            grid=(mb, pairs),
            in_specs=[block] * 3,
            out_specs=[block, block, pl.BlockSpec((1, ROWS, 128), lambda m, p, *_: (m, 0, 0))],
        ),
        out_shape=[
            jax.ShapeDtypeStruct((mb, ROWS, width), narrow),
            jax.ShapeDtypeStruct((mb, ROWS, width), narrow),
            jax.ShapeDtypeStruct((mb, ROWS, 128), wide),
        ],
        compiler_params=params(),
        cost_estimate=cost(16 * mb * 2 * pairs * (LONG**2 + SHORT**2) * HEAD, moved),
    )(lengths, q, k, v)


def cdf_and_slope(up):
    cdf = 0.5 + 0.5 * lax.erf(up * 0.7071067811865476)
    slope = cdf + up * (jnp.exp2(up * up * (-0.5 * log2e)) * 0.3989422804014327)
    return cdf, slope


def forward_kernel(
    lengths_ref, embed_ref, mixed_ref, w_ref, gain_ref,
    second_ref, act_ref, slope_ref, unit2_ref, unit3_ref, stat_ref, pool_ref,
):
    pack, step = pl.program_id(0), pl.program_id(1)
    width = embed_ref.shape[2]
    resid = embed_ref[0] + dot(mixed_ref[0], w_ref[0])
    unit, r2 = norm_rows(resid)
    unit2_ref[0] = unit.astype(narrow)
    second = (unit * gain_ref[3:4]).astype(narrow)
    second_ref[0] = second
    outcome = resid
    for j in range(4):
        up = dot(second, w_ref[1 + j])
        cdf, slope = cdf_and_slope(up)
        act = (up * cdf).astype(narrow)
        act_ref[j, 0] = act
        slope_ref[j, 0] = slope.astype(narrow)
        outcome = outcome + dot(act, w_ref[5 + j])
    unit, r3 = norm_rows(outcome)
    unit3_ref[0] = unit.astype(narrow)
    lane = lax.broadcasted_iota(jnp.int32, (1, 128), 1)
    stat_ref[0] = jnp.where(lane == 0, r2, r3)
    final = unit * gain_ref[4:5]

    @pl.when(step == 0)
    def _():
        pool_ref[...] = jnp.zeros_like(pool_ref)

    row = lax.broadcasted_iota(jnp.int32, (TILE, 1), 0) + step * TILE
    first_len, second_len = lengths_ref[pack, 0], lengths_ref[pack, 1]
    inside = (row < first_len, (row >= first_len) & (row < first_len + second_len))
    for s in range(2):
        total = jnp.sum(jnp.where(inside[s], final, 0.0), axis=0, keepdims=True)
        pool_ref[0, s : s + 1] += total


def forward_call(lengths, embed, mixed, w, gains):
    mb, _, width = embed.shape
    rows = pl.BlockSpec((1, TILE, width), lambda m, i, *_: (m, i, 0))
    wider = pl.BlockSpec((4, 1, TILE, width), lambda m, i, *_: (0, m, i, 0))
    return pl.pallas_call(
        forward_kernel,
        grid_spec=pltpu.PrefetchScalarGridSpec(
            num_scalar_prefetch=1,
            grid=(mb, ROWS // TILE),
            in_specs=[rows, rows, held(w.shape), held(gains.shape)],
            out_specs=[
                rows, wider, wider, rows, rows,
                pl.BlockSpec((1, TILE, 128), lambda m, i, *_: (m, i, 0)),
                pl.BlockSpec((1, 8, width), lambda m, i, *_: (m, 0, 0)),
            ],
        ),
        out_shape=[
            jax.ShapeDtypeStruct((mb, ROWS, width), narrow),
            jax.ShapeDtypeStruct((4, mb, ROWS, width), narrow),
            jax.ShapeDtypeStruct((4, mb, ROWS, width), narrow),
            jax.ShapeDtypeStruct((mb, ROWS, width), narrow),
            jax.ShapeDtypeStruct((mb, ROWS, width), narrow),
            jax.ShapeDtypeStruct((mb, ROWS, 128), wide),
            jax.ShapeDtypeStruct((mb, 8, width), wide),
        ],
        compiler_params=params(),
        cost_estimate=cost(2 * mb * ROWS * width * width * 9, 80e6),
    )(lengths, embed, mixed, w, gains)


def head_kernel(pool_ref, scale_ref, weight_ref, label_ref, head_ref, loss_ref, dhead_ref, dpool_ref):
    pooled = (pool_ref[...] * scale_ref[:, 0:1]).astype(narrow)
    logits = dot(pooled, head_ref[...])
    peak = jnp.max(logits, axis=1, keepdims=True)
    expo = jnp.exp(logits - peak)
    total = jnp.sum(expo, axis=1, keepdims=True)
    hot = lax.broadcasted_iota(jnp.int32, logits.shape, 1) == label_ref[:, 0:1]
    picked = jnp.sum(jnp.where(hot, logits, 0.0), axis=1, keepdims=True)
    weight = weight_ref[:, 0:1].astype(wide)
    loss = jnp.where(weight > 0, weight * (peak + jnp.log(total) - picked), 0.0)
    loss_ref[...] = jnp.broadcast_to(jnp.sum(loss, axis=0, keepdims=True), loss_ref.shape)
    dlogits = (weight * (expo / total - hot.astype(wide))).astype(narrow)
    dhead_ref[...] = dot(pooled, dlogits, 0, 0).astype(dhead_ref.dtype)
    dpool_ref[...] = dot(dlogits, head_ref[...], 1, 1) * scale_ref[:, 0:1]


def head_call(pool, scale, weight, label, head, out=wide):
    rows, width = pool.shape
    return pl.pallas_call(
        head_kernel,
        out_shape=[
            jax.ShapeDtypeStruct((8, 128), wide),
            jax.ShapeDtypeStruct(head.shape, out),
            jax.ShapeDtypeStruct((rows, width), wide),
        ],
        compiler_params=params(),
        cost_estimate=cost(6 * rows * width * 1000, 8e6),
    )(pool, scale, weight, label, head)


def backward_kernel(
    lengths_ref, dpool_ref, unit3_ref, unit2_ref, stat_ref, slope_ref, mixed_ref, rest_ref, w_ref, gain_ref, pick_ref,
    dm_ref, dup_ref, dr_ref, dmixed_ref, delta_ref, dgain_ref,
):
    pack, step = pl.program_id(0), pl.program_id(1)
    row = lax.broadcasted_iota(jnp.int32, (TILE, 1), 0) + step * TILE
    first_len, second_len = lengths_ref[pack, 0], lengths_ref[pack, 1]
    dfinal = jnp.where(
        row < first_len,
        dpool_ref[0, 0:1],
        jnp.where(row < first_len + second_len, dpool_ref[0, 1:2], 0.0),
    )
    unit3 = unit3_ref[0].astype(wide)
    r2, r3 = stat_ref[0, :, 0:1], stat_ref[0, :, 1:2]
    doutcome = back_rows(unit3, r3, dfinal * gain_ref[4:5])
    dgf = jnp.sum(dfinal * unit3, axis=0, keepdims=True)
    dm = doutcome.astype(narrow)
    dm_ref[0] = dm
    dsecond = None
    for j in range(4):
        dact = dot(dm, w_ref[5 + j], 1, 1)
        dup = (dact * slope_ref[j, 0].astype(wide)).astype(narrow)
        dup_ref[j, 0] = dup
        term = dot(dup, w_ref[1 + j], 1, 1)
        dsecond = term if dsecond is None else dsecond + term
    unit2 = unit2_ref[0].astype(wide)
    dg2 = jnp.sum(dsecond * unit2, axis=0, keepdims=True)
    dresid = doutcome + back_rows(unit2, r2, dsecond * gain_ref[3:4])
    dr = dresid.astype(narrow)
    dr_ref[0] = dr
    dmixed = dot(dr, w_ref[0], 1, 1).astype(narrow)
    dmixed_ref[0] = dmixed
    product = dmixed.astype(wide) * (mixed_ref[0].astype(wide) + rest_ref[0].astype(wide))
    high = product.astype(narrow)
    low = (product - high.astype(wide)).astype(narrow)
    delta_ref[0] = dot(high, pick_ref[...]) + dot(low, pick_ref[...])

    @pl.when((pack == 0) & (step == 0))
    def _():
        dgain_ref[...] = jnp.zeros_like(dgain_ref)

    dgain_ref[3:4] += dg2
    dgain_ref[4:5] += dgf


def backward_call(lengths, dpool, unit3, unit2, stat, slope, mixed, rest, w, gains, pick):
    mb, _, width = unit3.shape
    rows = pl.BlockSpec((1, TILE, width), lambda m, i, *_: (m, i, 0))
    lanes = pl.BlockSpec((1, TILE, 128), lambda m, i, *_: (m, i, 0))
    wider = pl.BlockSpec((4, 1, TILE, width), lambda m, i, *_: (0, m, i, 0))
    return pl.pallas_call(
        backward_kernel,
        grid_spec=pltpu.PrefetchScalarGridSpec(
            num_scalar_prefetch=1,
            grid=(mb, ROWS // TILE),
            in_specs=[
                pl.BlockSpec((1, 2, width), lambda m, i, *_: (m, 0, 0)),
                rows, rows, lanes, wider, rows, rows,
                held(w.shape), held(gains.shape), held(pick.shape),
            ],
            out_specs=[rows, wider, rows, rows, lanes, pl.BlockSpec((8, width), lambda m, i, *_: (0, 0))],
        ),
        out_shape=[
            jax.ShapeDtypeStruct((mb, ROWS, width), narrow),
            jax.ShapeDtypeStruct((4, mb, ROWS, width), narrow),
            jax.ShapeDtypeStruct((mb, ROWS, width), narrow),
            jax.ShapeDtypeStruct((mb, ROWS, width), narrow),
            jax.ShapeDtypeStruct((mb, ROWS, 128), wide),
            jax.ShapeDtypeStruct((8, width), wide),
        ],
        compiler_params=params(),
        cost_estimate=cost(2 * mb * ROWS * width * width * 9, 70e6),
    )(lengths, dpool, unit3, unit2, stat, slope, mixed, rest, w, gains, pick)


def attend_back_kernel(
    lengths_ref, q_ref, k_ref, v_ref, do_ref, qunit_ref, kunit_ref, qr_ref, kr_ref, stat_ref, gain_ref, ones_ref,
    dq_ref, dk_ref, dv_ref, dgain_ref, dq_acc, dk_acc, dv_acc,
):
    pack = pl.program_id(1)
    lane = lax.broadcasted_iota(jnp.int32, (1, 2 * HEAD), 1)

    def both(x, axis=0):
        zero = jnp.zeros_like(x)
        return jnp.concatenate([jnp.where(lane < HEAD, x, zero), jnp.where(lane < HEAD, zero, x)], axis=axis)

    def part(start, count, tile, chunk, masked):
        for ti in range(start, start + count, tile):
            q2 = both(q_ref[0, ti : ti + tile])
            do2 = both(do_ref[0, ti : ti + tile])
            lse = jnp.concatenate([stat_ref[0, h : h + 1, ti : ti + tile] for h in (0, 1)], axis=1)
            delta = jnp.concatenate([stat_ref[0, h : h + 1, ti : ti + tile] for h in (2, 3)], axis=1)
            for ui in range(start, start + count, chunk):
                k = k_ref[0, ui : ui + chunk]
                v = v_ref[0, ui : ui + chunk]
                s = dot(k, q2, 1, 1)
                p = jnp.exp2(s * log2e - lse)
                if masked:
                    limit = lengths_ref[pack, 1]
                    row = lax.broadcasted_iota(jnp.int32, s.shape, 0) + (ui - start)
                    col = lax.broadcasted_iota(jnp.int32, s.shape, 1)
                    col = jnp.where(col < tile, col, col - tile) + (ti - start)
                    p = jnp.where((row < limit) == (col < limit), p, 0.0)
                dp = dot(v, do2, 1, 1)
                ds = (p * (dp - delta)).astype(narrow)
                dv_new = dot(p.astype(narrow), do2)
                dk_new = dot(ds, q2)
                k2 = both(k)
                ds_rows = jnp.concatenate([ds[:, :tile], ds[:, tile:]], axis=0)
                dq_new = dot(ds_rows, k2, 0, 0)
                if ti == start:
                    dv_acc[ui : ui + chunk] = dv_new
                    dk_acc[ui : ui + chunk] = dk_new
                else:
                    dv_acc[ui : ui + chunk] += dv_new
                    dk_acc[ui : ui + chunk] += dk_new
                if ui == start:
                    dq_acc[ti : ti + tile] = dq_new
                else:
                    dq_acc[ti : ti + tile] += dq_new

    part(0, LONG, 384, 384, False)
    part(LONG, SHORT, SHORT, SHORT, True)
    dv_ref[0] = dv_acc[...].astype(narrow)
    ones = ones_ref[...]

    def mean(x):
        return dot(x.astype(narrow), ones)

    @pl.when(pack == 0)
    def _():
        dgain_ref[...] = jnp.zeros_like(dgain_ref)

    for i, (acc, unit_ref, r_ref, ref, factor) in enumerate(
        ((dq_acc, qunit_ref, qr_ref, dq_ref, HEAD**-0.5), (dk_acc, kunit_ref, kr_ref, dk_ref, 1.0))
    ):
        unit, r = unit_ref[0].astype(wide), r_ref[0].astype(wide)
        dy = acc[...] * factor
        dgain_ref[0, i : i + 1] += jnp.sum(dy * unit, axis=0, keepdims=True)
        scaled = dy * gain_ref[1 + i : 2 + i]
        ref[0] = (r * (scaled - mean(scaled) - unit * mean(scaled * unit))).astype(narrow)


def attend_back_call(lengths, q, k, v, do, kept, stat, gains, ones, first_pair, pairs):
    mb, _, width = q.shape
    block = pl.BlockSpec((1, ROWS, 2 * HEAD), lambda p, m, *_: (m, 0, p + first_pair))
    out = pl.BlockSpec((1, ROWS, 2 * HEAD), lambda p, m, *_: (m, 0, p))
    shape = jax.ShapeDtypeStruct((mb, ROWS, pairs * 2 * HEAD), narrow)
    return pl.pallas_call(
        attend_back_kernel,
        grid_spec=pltpu.PrefetchScalarGridSpec(
            num_scalar_prefetch=1,
            grid=(pairs, mb),
            in_specs=[
                *[block] * 8,
                pl.BlockSpec((1, 8, ROWS), lambda p, m, *_: (m, p + first_pair, 0)),
                pl.BlockSpec((8, 2 * HEAD), lambda p, m, *_: (0, p + first_pair)),
                pl.BlockSpec((2 * HEAD, 2 * HEAD), lambda p, m, *_: (0, 0)),
            ],
            out_specs=[out, out, out, pl.BlockSpec((1, 8, 2 * HEAD), lambda p, m, *_: (p, 0, 0))],
            scratch_shapes=[pltpu.VMEM((ROWS, 2 * HEAD), wide)] * 3,
        ),
        out_shape=[shape, shape, shape, jax.ShapeDtypeStruct((pairs, 8, 2 * HEAD), wide)],
        compiler_params=params(),
        cost_estimate=cost(20 * mb * 2 * pairs * (LONG**2 + SHORT**2) * HEAD * 2, mb * ROWS * pairs * 128 * 18),
    )(lengths, q, k, v, do, *kept, stat, gains, ones)


def first_kernel(*refs, parts):
    grads = refs[: 3 * parts]
    embed_ref, dr_ref, w_ref, gain_ref, out_ref, dgain_ref = refs[3 * parts :]
    step = pl.program_id(0) * pl.num_programs(1) + pl.program_id(1)
    width = embed_ref.shape[2]
    total = None
    for i in range(3):
        rows = jnp.concatenate([grads[3 * p + i][0] for p in range(parts)], axis=1)
        term = dot(rows, w_ref[:, i * width : (i + 1) * width], 1, 1)
        total = term if total is None else total + term
    unit, r = norm_rows(embed_ref[0])

    @pl.when(step == 0)
    def _():
        dgain_ref[...] = jnp.zeros_like(dgain_ref)

    dgain_ref[0:1] += jnp.sum(total * unit, axis=0, keepdims=True)
    out_ref[0] = (dr_ref[0].astype(wide) + back_rows(unit, r, total * gain_ref[0:1])).astype(narrow)


def first_call(grads, embed, dr, w, gains):
    mb, _, width = embed.shape
    rows = spec((1, TILE, width), lambda m, i: (m, i, 0))
    parts = len(grads) // 3
    return pl.pallas_call(
        functools.partial(first_kernel, parts=parts),
        grid=(mb, ROWS // TILE),
        in_specs=[spec((1, TILE, g.shape[2]), lambda m, i: (m, i, 0)) for g in grads]
        + [rows, rows, held(w.shape), held(gains.shape)],
        out_specs=[rows, spec((8, width), lambda m, i: (0, 0))],
        out_shape=[
            jax.ShapeDtypeStruct((mb, ROWS, width), narrow),
            jax.ShapeDtypeStruct((8, width), wide),
        ],
        compiler_params=params(),
        cost_estimate=cost(2 * mb * ROWS * width * width * 3, 32e6),
    )(*grads, embed, dr, w, gains)


def split_rows(value, own_ref, sent_ref, me, n):
    across, up, deep = own_ref.shape[:3]
    part = own_ref.shape[4]
    for x in range(across):
        for y in range(up):
            for z in range(deep):
                at = ((z * up + y) * across + x) * 2 * part
                first = value[at : at + part].astype(narrow)
                second = value[at + part : at + 2 * part].astype(narrow)
                own_ref[x, y, z, n] = jnp.where(me == 0, first, second)
                sent_ref[x, y, z, n] = jnp.where(me == 0, second, first)


def flat_rows(ref):
    return ref[...].reshape(-1, ref.shape[-1])


def weight_kernel(at_ref, act_ref, dm_ref, second_ref, dup_ref, own_ref, sent_ref):
    step = pl.program_id(0)

    def write(a_ref, b_ref):
        split_rows(dot(flat_rows(a_ref), flat_rows(b_ref), 0, 0), own_ref, sent_ref, at_ref[0], 0)

    pl.when(step < 4)(lambda: write(second_ref, dup_ref))
    pl.when(step >= 4)(lambda: write(act_ref, dm_ref))


def split_shape(rows):
    core, x, y, z = (level[2] for level in levels())
    return (x, y, z), rows // (core * x * y * z)


def core_at():
    return (lax.axis_index("seq") % 2).reshape(1).astype(jnp.int32)


def weight_call(act, dm, second, dup):
    width = dm.shape[2]
    (x, y, z), part = split_shape(width)
    rows = pl.BlockSpec(dm.shape, lambda i, *_: (0, 0, 0), pipeline_mode=pl.Buffered(1))
    out = pl.BlockSpec((x, y, z, 1, part, width), lambda i, *_: (0, 0, 0, i, 0, 0))
    one = (1, *dm.shape)
    return pl.pallas_call(
        weight_kernel,
        grid_spec=pltpu.PrefetchScalarGridSpec(
            num_scalar_prefetch=1,
            grid=(8,),
            in_specs=[
                pl.BlockSpec(one, lambda i, *_: (jnp.maximum(i - 4, 0), 0, 0, 0)),
                rows,
                rows,
                pl.BlockSpec(one, lambda i, *_: (jnp.minimum(i, 3), 0, 0, 0)),
            ],
            out_specs=[out, out],
        ),
        out_shape=[jax.ShapeDtypeStruct((x, y, z, 8, part, width), narrow)] * 2,
        compiler_params=params(),
        cost_estimate=cost(2 * 8 * dm.size * width, 60e6),
    )(core_at(), act, dm, second, dup)


def one_weight_kernel(at_ref, a_ref, *refs, count):
    b_refs, own_ref, sent_ref, total = refs[:count], refs[count], refs[count + 1], refs[count + 2]
    step = pl.program_id(0)
    last = step == pl.num_programs(0) - 1
    a = a_ref[0]
    at = 0
    for b_ref in b_refs:
        lanes = pl.ds(at, b_ref.shape[-1])
        at += b_ref.shape[-1]
        value = dot(a, b_ref[0], 0, 0)

        @pl.when(step == 0)
        def _(value=value, lanes=lanes):
            total[:, lanes] = value

        @pl.when((step > 0) & ~last)
        def _(value=value, lanes=lanes):
            total[:, lanes] += value

        @pl.when(last)
        def _(value=value, lanes=lanes):
            split_rows(total[:, lanes] + value, own_ref.at[..., lanes], sent_ref.at[..., lanes], at_ref[0], 0)


def one_weight_call(a, *b):
    mb, rows, depth = a.shape
    width = sum(x.shape[-1] for x in b)
    (x, y, z), part = split_shape(depth)
    shape = (x, y, z, 1, part, width)
    out = pl.BlockSpec(shape, lambda m, *_: (0,) * 6)
    return pl.pallas_call(
        functools.partial(one_weight_kernel, count=len(b)),
        grid_spec=pltpu.PrefetchScalarGridSpec(
            num_scalar_prefetch=1,
            grid=(mb,),
            in_specs=[pl.BlockSpec((1, *v.shape[1:]), lambda m, *_: (m, 0, 0)) for v in (a, *b)],
            out_specs=[out] * 2,
            scratch_shapes=[pltpu.VMEM((depth, width), wide)],
        ),
        out_shape=[jax.ShapeDtypeStruct(shape, narrow)] * 2,
        compiler_params=params(),
        cost_estimate=cost(2 * a.size * width, 12e6),
    )(core_at(), a, *b)


def embed_weight_kernel(at_ref, patch_ref, hot_ref, grad_ref, gain_ref, own_ref, sent_ref, total):
    step = pl.program_id(0)
    grad = grad_ref[0]
    width = grad.shape[1]
    value = dot(patch_ref[0, 0], grad, 0, 0)
    table = dot(grad, hot_ref[0], 0, 0)

    @pl.when(step == 0)
    def _():
        total[:, :width] = value
        total[:, width : width + 128] = table

    @pl.when(step > 0)
    def _():
        total[:, :width] += value
        total[:, width : width + 128] += table

    @pl.when(step == pl.num_programs(0) - 1)
    def _():
        total[:, width + 128 :] = gain_ref[...]
        split_rows(total[...], own_ref, sent_ref, at_ref[0], 0)


def embed_weight_call(patches, hot, grad, gain_columns):
    mb, _, width = grad.shape
    pixels = patches.shape[3]
    (x, y, z), part = split_shape(pixels)
    shape = (x, y, z, 1, part, width + 256)
    out = pl.BlockSpec(shape, lambda m, *_: (0,) * 6)
    return pl.pallas_call(
        embed_weight_kernel,
        grid_spec=pltpu.PrefetchScalarGridSpec(
            num_scalar_prefetch=1,
            grid=(mb,),
            in_specs=[
                pl.BlockSpec((1, 1, ROWS, pixels), lambda m, *_: (m, 0, 0, 0)),
                pl.BlockSpec((1, ROWS, hot.shape[2]), lambda m, *_: (m, 0, 0)),
                pl.BlockSpec((1, ROWS, width), lambda m, *_: (m, 0, 0)),
                pl.BlockSpec((width, 128), lambda m, *_: (0, 0)),
            ],
            out_specs=[out, out],
            scratch_shapes=[pltpu.VMEM((pixels, width + 256), wide)],
        ),
        out_shape=[jax.ShapeDtypeStruct(shape, narrow)] * 2,
        compiler_params=params(),
        cost_estimate=cost(2 * grad.size * (pixels + 128), 12e6),
    )(core_at(), patches, hot, grad, gain_columns)


def fold(parts):
    while len(parts) > 1:
        parts = [parts[i] + parts[i + 1] for i in range(0, len(parts), 2)]
    return parts[0]


def swap(x, axis, bits):
    if bits == 0:
        return x
    return lax.ppermute(x, axis, [(i, i ^ bits) for i in range(lax.axis_size(axis))])


def tied(x, *after):
    return lax.optimization_barrier((x, *after))[0]


def pick_index(x, index, dim):
    return lax.dynamic_index_in_dim(x, index, dim, keepdims=False)


def levels():
    across, deep = lax.axis_size("seq"), lax.axis_size("fsdp")
    y = 1 << ((deep.bit_length() - 1) // 2)
    return (("seq", 1, 2), ("seq", 2, across // 2), ("fsdp", 1, y), ("fsdp", y, deep // y))


CORE, X, Y, Z = range(4)


class Sum:
    def __init__(self, terms, which):
        axis, stride, size = levels()[which]
        at = lax.axis_index(axis) // stride % size

        def part(k):
            return fold([pick_index(term, at ^ k, 0).astype(wide) for term in terms])

        self.sent = [part(k).astype(narrow) for k in range(1, size)]
        self.terms = [part(0)] + [swap(x, axis, (k + 1) * stride) for k, x in enumerate(self.sent)]

    def after(self, *others):
        return [tied(self.terms[0], *others), *self.terms[1:]]

    def total(self):
        return fold([term.astype(wide) for term in self.terms])


def core_terms(own, sent):
    return [own, swap(sent, "seq", 1)]


def settle_kernel(at_ref, *refs, count, moves):
    sources, outs = refs[:count], refs[count:]
    for source, index, out, target in moves:
        outs[out][target(at_ref[0], at_ref[1])] = sources[source][index]


def mesh_at():
    return jnp.stack([lax.axis_index("fsdp"), lax.axis_index("seq")]).astype(jnp.int32)


def in_vmem(count):
    return [pl.BlockSpec(memory_space=pltpu.VMEM)] * count


def settled(parts, shapes, moves):
    size = sum(part.size for part in parts) * parts[0].dtype.itemsize
    return pl.pallas_call(
        functools.partial(settle_kernel, count=len(parts), moves=moves),
        in_specs=[pl.BlockSpec(memory_space=pltpu.SMEM)] + in_vmem(len(parts)),
        out_specs=in_vmem(len(shapes)),
        out_shape=[jax.ShapeDtypeStruct(shape, parts[0].dtype) for shape in shapes],
        compiler_params=params(),
        cost_estimate=cost(0, 2 * size),
    )(mesh_at(), *parts)


def seq_parts(x, *after):
    half = [swap(x, "seq", k) for k in range(0, lax.axis_size("seq"), 2)]
    if after:
        half = [half[0]] + [tied(y, *after) for y in half[1:]]
    return [part for y in half for part in (y, swap(y, "seq", 1))]


def settle_rows(parts, cuts, shapes):
    deep = parts[0].shape[0]
    moves = [
        (j, (k, slice(start, stop)), out, lambda f, s, j=j, k=k, index=index: (*index, k ^ f, j ^ s))
        for j in range(len(parts))
        for k in range(deep)
        for start, stop, out, index in cuts
    ]
    return settled(parts, shapes, moves)


def near_exchange(x):
    return jnp.stack([swap(x, "fsdp", k) for k in range(levels()[Y][2])])


def far_exchange(x):
    _, stride, far = levels()[Z]
    return [swap(x, "fsdp", k * stride) for k in range(far)]


def stacked(parts):
    return jnp.stack(parts).reshape(-1, *parts[0].shape[1:])


def my_rows(x):
    size = lax.axis_size("seq")
    return pick_index(x.reshape(x.shape[0], size, x.shape[1] // size, x.shape[2]), lax.axis_index("seq"), 1)


def grads_kernel(at_ref, factor_ref, *refs, count, part):
    parts, (out_ref, small_ref) = refs[:count], refs[count:]
    factor = factor_ref[0]
    for j, ref in enumerate(parts):
        to = at_ref[1] ^ j
        for b in range(out_ref.shape[0]):
            out_ref[b, to] = ref[b * part : (b + 1) * part].astype(wide) * factor
        small_ref[to] = ref[out_ref.shape[0] * part :].astype(wide) * factor


def collect_kernel(at_ref, slot_ref, scalar_ref, rest_ref, mid_ref, *refs, count, deep, per, columns):
    terms, (own_ref, *out_refs) = refs[:count], refs[count : count + 1 + deep]
    blocks = refs[-1]
    part, width = rest_ref.shape[1:]
    scale = 1.0 / scalar_ref[0]
    both = fold([ref[0].astype(wide) for ref in terms])
    late = both[:, width + 256 :]
    remain = width - columns
    pieces = [both[:, :width]]
    for i in range(3):
        first = mid_ref[:, width + i * columns : width + (i + 1) * columns]
        pieces.append(jnp.concatenate([first, late[:, i * remain : (i + 1) * remain]], axis=1))
    pieces.append(mid_ref[:, :width])
    pieces += [rest_ref[i] for i in range(rest_ref.shape[0])]
    squares = jnp.zeros((1, 1), wide)
    total = jnp.zeros((part, width), wide)
    for b, piece in enumerate(pieces):
        piece = (piece * scale).astype(narrow)
        blocks[b] = piece
        own_ref[b * part : (b + 1) * part] = piece
        total += jnp.square(piece.astype(wide))
    small = (both[:, width : width + 256] * scale).astype(narrow)
    third = part // 3
    small = small.astype(wide)
    squares = jnp.sum(total, keepdims=True) + jnp.sum(jnp.square(small), keepdims=True) + scalar_ref[1]
    small = jnp.concatenate([small[i * third : (i + 1) * third] for i in range(3)], axis=1)
    own_ref[len(pieces) * part :] = small.astype(narrow)
    row = lax.broadcasted_iota(jnp.int32, (8, width), 0)
    notes = jnp.zeros((8, width), wide)
    for at, value in ((0, squares), (3, jnp.full((1, 1), scalar_ref[2]))):
        for i in range(3):
            piece = value.astype(narrow).astype(wide)
            value = value - piece
            notes = jnp.where(row == at + i, piece, notes)
    notes = notes.astype(narrow)
    blocks[len(pieces)] = jnp.zeros((part, width), narrow)
    for k, out_ref in enumerate(out_refs):
        for i in range(per):
            slot = (at_ref[0] ^ k) * per + i
            found = len(pieces)
            for b in range(len(pieces)):
                found = jnp.where(slot_ref[b] == slot, b, found)
            out_ref[i * part : (i + 1) * part] = blocks[found]
        out_ref[per * part :] = notes


def collect_call(block_slot, scalars, rest, mid, terms, per, columns):
    part, width = rest.shape[1:]
    deep = lax.axis_size("fsdp")
    count = block_slot.shape[0]
    smem = pl.BlockSpec(memory_space=pltpu.SMEM)
    message = jax.ShapeDtypeStruct((per * part + 8, width), narrow)
    return pl.pallas_call(
        functools.partial(collect_kernel, count=len(terms), deep=deep, per=per, columns=columns),
        in_specs=[smem, smem, smem] + in_vmem(2 + len(terms)),
        out_specs=in_vmem(1 + deep),
        out_shape=[jax.ShapeDtypeStruct((count * part + part // 3, width), narrow)] + [message] * deep,
        scratch_shapes=[pltpu.VMEM((count + 1, part, width), narrow)],
        compiler_params=params(),
        cost_estimate=cost(0, 4e6),
    )(mesh_at(), block_slot, scalars, rest, mid, *terms)


def halves(x):
    high = x.astype(narrow)
    return high, (x - high.astype(wide)).astype(narrow)


def direction_kernel(at_ref, left_ref, right_ref, *refs, count, deep):
    parts, slotted_ref, notes_ref = refs[:count], refs[count], refs[count + 1]
    out_refs, rows, result = refs[count + 2 : count + 2 + deep], refs[-2], refs[-1]
    per, _, part, width = left_ref.shape
    for j, ref in enumerate(parts):
        for k in range(deep):
            f, s = at_ref[0] ^ k, at_ref[1] ^ j
            for i in range(per):
                rows[i, f * count + s] = ref[k, i * part : (i + 1) * part].astype(wide)
            notes_ref[f, s] = ref[k, per * part :]
    for i in range(per):
        grad = rows[i].reshape(deep * count * part, width).astype(narrow)
        slotted_ref[i] = grad
        left_high, left_low = halves(left_ref[i].reshape(deep * part, width))
        inner_high, inner_low = halves(dot(left_high, grad) + dot(left_low, grad))
        right_high, right_low = halves(right_ref[i])
        value = dot(inner_high, right_high) + dot(inner_low, right_high) + dot(inner_high, right_low)
        result[i] = value.reshape(deep, part, width)
    for k, out_ref in enumerate(out_refs):
        for i in range(per):
            out_ref[i] = result[i, at_ref[0] ^ k].astype(narrow)


def direction_call(left, right, parts):
    per, deep, part, width = left.shape
    count = len(parts)
    return pl.pallas_call(
        functools.partial(direction_kernel, count=count, deep=deep),
        in_specs=[pl.BlockSpec(memory_space=pltpu.SMEM)] + in_vmem(2 + count),
        out_specs=in_vmem(2 + deep),
        out_shape=[
            jax.ShapeDtypeStruct((per, width, width), narrow),
            jax.ShapeDtypeStruct((deep, count, 8, width), narrow),
        ]
        + [jax.ShapeDtypeStruct((per, part, width), narrow)] * deep,
        scratch_shapes=[
            pltpu.VMEM((per, deep * count, part, width), wide),
            pltpu.VMEM((per, deep, part, width), wide),
        ],
        compiler_params=params(),
        cost_estimate=cost(10 * per * deep * part * width * width, 16e6),
    )(mesh_at(), left, right, *parts)


def select_kernel(at_ref, slot_ref, *refs, deep):
    parts, out_ref, slots = refs[:deep], refs[deep], refs[deep + 1]
    per, part = parts[0].shape[:2]
    for k, ref in enumerate(parts):
        for i in range(per):
            slots[(at_ref[0] ^ k) * per + i] = ref[i]
    for b in range(out_ref.shape[0] // part):
        out_ref[b * part : (b + 1) * part] = slots[slot_ref[b]]


def select_call(block_slot, parts):
    per, part, width = parts[0].shape
    deep = len(parts)
    smem = pl.BlockSpec(memory_space=pltpu.SMEM)
    return pl.pallas_call(
        functools.partial(select_kernel, deep=deep),
        in_specs=[smem, smem] + in_vmem(deep),
        out_specs=pl.BlockSpec(memory_space=pltpu.VMEM),
        out_shape=jax.ShapeDtypeStruct((block_slot.shape[0] * part, width), narrow),
        scratch_shapes=[pltpu.VMEM((deep * per, part, width), narrow)],
        compiler_params=params(),
        cost_estimate=cost(0, 2e6),
    )(mesh_at(), block_slot, *parts)


def update_kernel(at_ref, factor_ref, block_ref, *refs, count, part):
    parts, out_ref = refs[:count], refs[count]
    factor = factor_ref[0]
    for j, ref in enumerate(parts):
        to = at_ref[1] ^ j
        for b in range(out_ref.shape[0]):
            old = block_ref[b, to]
            step = ref[b * part : (b + 1) * part].astype(wide) * factor
            out_ref[b, to] = old - shampoo_rate * (step + decay_rate * old)


def finish_call(kernel, factor, arrays, parts, part, shapes):
    smem = pl.BlockSpec(memory_space=pltpu.SMEM)
    return pl.pallas_call(
        functools.partial(kernel, count=len(parts), part=part),
        in_specs=[smem, smem] + in_vmem(len(arrays) + len(parts)),
        out_specs=in_vmem(len(shapes)),
        out_shape=[jax.ShapeDtypeStruct(shape, wide) for shape in shapes],
        compiler_params=params(),
        cost_estimate=cost(0, 12e6),
    )(mesh_at(), factor.reshape(1), *arrays, *parts)


def adam(weight, grad, first, second, rate, decay):
    first_new = first_decay * first + (1 - first_decay) * grad
    second_new = second_decay * second + (1 - second_decay) * grad * grad
    corrected = (
        first_new
        / (1 - first_decay**STEP)
        / (jnp.sqrt(second_new / (1 - second_decay**STEP)) + adam_eps)
    )
    return (weight - rate * (corrected + decay * weight), first_new, second_new)


def product(spec_text, a, b):
    return jnp.einsum(spec_text, a, b, preferred_element_type=wide)


def local(
    patches, positions, lengths, res_weights, labels, block_slot, blocks, pos_table, gains, head,
    left_stats, right_stats, left_roots, right_roots,
    pos_first, pos_second, gain_first, gain_second, head_first, head_second,
):
    mb = patches.shape[0]
    deep, size = lax.axis_size("fsdp"), lax.axis_size("seq")
    me_f, me_s = lax.axis_index("fsdp"), lax.axis_index("seq")
    lengths, res_weights, labels = (x[:, 0] for x in (lengths, res_weights, labels))
    lanes = pos_table.shape[2]
    width = lanes * deep
    grid_rows = pos_table.shape[1]

    part = blocks.shape[1] // size
    seen = jnp.broadcast_to(jnp.sum(res_weights).astype(wide), (lanes, 3))
    small = jnp.concatenate(
        [pos_table.reshape(2 * grid_rows, lanes).T, gains.T, seen, jnp.zeros((lanes, 120), wide)], axis=1
    ).astype(narrow)
    opening = my_rows(jnp.concatenate([blocks[0].astype(narrow), small], axis=1)[None])[0]
    project = my_rows(blocks[1:4]).astype(narrow).transpose(1, 0, 2).reshape(part, 3 * width)
    every = far_exchange(near_exchange(jnp.concatenate([opening, project], axis=1)))
    opening = seq_parts(stacked([x[:, :, : width + 256] for x in every]))
    project = stacked([x[:, :, width + 256 :] for x in every])
    w_embed = settle_rows(opening, [(0, part, 0, ())], [(deep, size, part, width + 256)])[0]
    w_embed = w_embed.reshape(width, width + 256)
    gains_full = w_embed[:, width + 128 :].T[:8].astype(wide)
    weight_sum = jnp.sum(gains_full[5].reshape(deep * size, part)[:, 0])
    w_rest = lax.all_gather(my_rows(tied(blocks[4:13], opening[-1])).astype(narrow), ("fsdp", "seq"), axis=1, tiled=True)
    w_head = lax.all_gather(tied(my_rows(head.astype(narrow)[None])[0], opening[-1]), ("fsdp", "seq"), axis=0, tiled=True)

    places = positions[:, :, 0, :ROWS]
    grid = jnp.arange(grid_rows)
    hot = jnp.concatenate([places[i][:, :, None] == grid for i in range(2)], axis=2).astype(narrow)
    index = jnp.arange(256)
    ones = jnp.where(index[:, None] // HEAD == index[None] // HEAD, 1 / HEAD, 0).astype(narrow)
    pick = (jnp.arange(width)[:, None] // HEAD == jnp.arange(128)[None]).astype(narrow)
    embed, first = embed_call(patches, hot, tied(w_embed, project), gains_full)
    w_project = settle_rows(
        seq_parts(tied(project, opening[-1]), first), [(0, part, 0, ())], [(deep, size, part, 3 * width)]
    )[0].reshape(width, 3 * width)
    query, keys, values, *kept = project_call(first, w_project, gains_full, ones)
    mixed, rest, stat = attend_call(lengths, query, keys, values)
    second, act, slope, unit2, unit3, row_stat, pool = forward_call(lengths, embed, mixed, w_rest, gains_full)

    seqs = 2 * mb
    spare = -seqs % 8

    def column(x):
        return jnp.broadcast_to(jnp.pad(x.reshape(seqs), (0, spare))[:, None], (seqs + spare, 128))

    pool = jnp.pad(pool[:, :2].reshape(seqs, width), ((0, spare), (0, 0)))
    loss, d_head, d_pool = head_call(
        pool, column(1.0 / lengths.astype(wide)), column(res_weights), column(labels), w_head
    )
    head_sum = lax.psum_scatter(d_head, "fsdp", scatter_dimension=0, tiled=True)

    dm, d_up, dr, d_mixed, delta, d_gain_rest = backward_call(
        lengths, d_pool[:seqs].reshape(mb, 2, width), unit3, unit2, row_stat, slope, mixed, rest, w_rest, gains_full, pick
    )
    rest_core = core_terms(*weight_call(act, dm, second, d_up))
    out_own, out_sent = one_weight_call(tied(mixed, rest_core[0]), dr)
    rest_x = Sum([tied(rest_core[0], out_own), rest_core[1]], X)

    pairs = HEADS // 2
    early = 4
    stats = jnp.stack([s[:, :, :HEADS].reshape(mb, ROWS, pairs, 2) for s in (stat, delta)], axis=3)
    stats = jnp.pad(stats.transpose(0, 2, 3, 4, 1).reshape(mb, pairs, 4, ROWS), ((0, 0), (0, 0), (0, 4), (0, 0)))
    stats = stats.reshape(mb, 8 * pairs, ROWS)

    def heads_back(after, start, count):
        out = attend_back_call(
            lengths, tied(query, *after), keys, values, d_mixed, kept, stats, gains_full,
            ones, start, count,
        )
        return out[:3], out[3]

    grads_one, gain_one = heads_back(rest_x.sent, 0, early)
    rest_y = Sum(rest_x.after(grads_one[0]), Y)
    head_sum = lax.psum(tied(head_sum, *rest_y.sent), "seq")
    one_own, one_sent = one_weight_call(tied(first, *rest_y.sent), *grads_one)
    mid_core = core_terms(
        jnp.concatenate([out_own, one_own], axis=5), jnp.concatenate([out_sent, one_sent], axis=5)
    )
    mid_x = Sum(mid_core, X)
    grads_two, gain_two = heads_back(rest_y.sent + mid_x.sent, early, pairs - early)
    rest_z = Sum(rest_y.after(grads_two[0]), Z)
    mid_y = Sum(mid_x.after(grads_two[0]), Y)
    late_core = core_terms(*one_weight_call(tied(first, *rest_z.sent, *mid_y.sent), *grads_two))
    late_x = Sum(late_core, X)
    mid_z = Sum(mid_y.after(late_core[0]), Z)
    d_embed, d_gain_first = first_call(
        (*grads_one, *grads_two), embed, tied(dr, *late_x.sent, *mid_z.sent), w_project, gains_full
    )
    late_y = Sum(late_x.after(d_embed), Y)
    own_rest, own_mid = fold([x.astype(wide) for x in rest_z.after(d_embed)]), fold(
        [x.astype(wide) for x in mid_z.after(d_embed)]
    )
    d_gain_heads = jnp.concatenate([gain_one, gain_two], axis=0).transpose(1, 0, 2).reshape(8, width)
    d_gains = jnp.concatenate(
        [d_gain_first[:1], d_gain_heads[:2], d_gain_rest[3:5], jnp.zeros((123, width), wide)], axis=0
    ).T
    head_sum = tied(head_sum, late_core[0]) / weight_sum
    head_squares = jnp.where(me_s == 0, jnp.sum(jnp.square(head_sum)), 0.0)
    scalars = jnp.stack([weight_sum, head_squares, loss[0, 0]])
    left_part = pick_index(left_roots.reshape(left_roots.shape[0], deep, size, part, width), me_s, 2)
    e_own, e_sent = embed_weight_call(
        patches, hot, tied(d_embed, own_rest, own_mid, scalars, left_part, *late_y.sent), d_gains
    )
    last_y = Sum(Sum(core_terms(e_own, e_sent), X).terms, Y)
    both_z = Sum(
        [jnp.concatenate([a.astype(wide), b.astype(wide)], axis=3) for a, b in zip(last_y.terms, late_y.terms)], Z
    )

    per = left_stats.shape[0]
    count = blocks.shape[0]
    own, *outgoing = collect_call(
        block_slot, scalars, own_rest, own_mid[0], both_z.terms, per,
        early * 2 * HEAD,
    )
    arrived = seq_parts(jnp.stack([swap(x, "fsdp", k) for k, x in enumerate(outgoing)]))
    slotted, notes, *directions = direction_call(left_part, right_roots, arrived)
    notes = jnp.sum(notes[:, :, :, 0].astype(wide), axis=(0, 1))
    loss_sum = notes[3] + notes[4] + notes[5]
    clip_norm = jnp.sqrt(notes[0] + notes[1] + notes[2])
    factor = jnp.minimum(1.0, clip_bound / clip_norm)
    back = select_call(block_slot, [swap(x, "fsdp", k) for k, x in enumerate(directions)])
    split = (count, size, part, width)
    block_grads, small_grad = finish_call(
        grads_kernel, factor, [], seq_parts(tied(own, slotted)), part, [split, (size, part // 3, width)]
    )
    blocks_new = finish_call(update_kernel, factor, [blocks.reshape(split)], seq_parts(back), part, [split])[0]
    blocks_new = blocks_new.reshape(blocks.shape)
    block_grads = block_grads.reshape(blocks.shape)
    slotted = tied(slotted, back)
    gram_left = product("sij,skj->sik", slotted, slotted)
    gram_right = product("sji,sjk->sik", slotted, slotted)
    left_new = stat_decay * left_stats + ((1 - stat_decay) * factor * factor) * gram_left
    right_new = stat_decay * right_stats + ((1 - stat_decay) * factor * factor) * gram_right

    small_grad = jnp.concatenate([small_grad[:, :, i * 256 : (i + 1) * 256] for i in range(3)], axis=1)
    small_grad = small_grad.reshape(lanes, 256).T
    table_grad = small_grad[: 2 * grid_rows].reshape(2, grid_rows, lanes)
    gain_grad = small_grad[2 * grid_rows : 2 * grid_rows + 5]
    pos_new, pos_first_new, pos_second_new = adam(
        pos_table, table_grad, pos_first, pos_second, table_rate, decay_rate
    )
    gains_new, gain_first_new, gain_second_new = adam(gains, gain_grad, gain_first, gain_second, gain_rate, 0.0)
    head_new, head_first_new, head_second_new = adam(
        head, tied(head_sum, back) * factor, head_first, head_second, adam_rate, decay_rate
    )
    return (
        blocks_new, block_grads, left_new, right_new, pos_new, pos_first_new, pos_second_new,
        gains_new, gain_first_new, gain_second_new, head_new, head_first_new, head_second_new,
        clip_norm, loss_sum, weight_sum,
    )


def solution(mesh):
    placed = (
        P(None, ("seq", "fsdp"), None, None),
        P(None, None, ("seq", "fsdp"), None),
        P(None, ("seq", "fsdp"), None),
        P(None, ("seq", "fsdp"), None),
        P(None, ("seq", "fsdp"), None),
        P(),
        P(None, "fsdp", None),
        P(None, None, "fsdp"),
        P(None, "fsdp"),
        P("fsdp", None),
        P("fsdp", None, None),
        P("fsdp", None, None),
        P("fsdp", None, None),
        P("fsdp", None, None),
        P(None, None, "fsdp"),
        P(None, None, "fsdp"),
        P(None, "fsdp"),
        P(None, "fsdp"),
        P("fsdp", None),
        P("fsdp", None),
    )
    return jax.shard_map(
        local,
        mesh=mesh,
        in_specs=placed,
        out_specs=(
            P(None, "fsdp", None),
            P(None, "fsdp", None),
            P("fsdp", None, None),
            P("fsdp", None, None),
            P(None, None, "fsdp"),
            P(None, None, "fsdp"),
            P(None, None, "fsdp"),
            P(None, "fsdp"),
            P(None, "fsdp"),
            P(None, "fsdp"),
            P("fsdp", None),
            P("fsdp", None),
            P("fsdp", None),
            P(),
            P(),
            P(),
        ),
        check_vma=False,
    )
```

```python
import functools
import math
import jax
import jax.numpy as jnp
from jax import lax
from jax.experimental import pallas as pl
from jax.experimental.pallas import tpu as pltpu
from jax.sharding import PartitionSpec as P

HEADS = 12
HEAD = 64
PACK = 1536
LONG = 1152
SHORT = 256
ROWS = LONG + SHORT
TILE = 352
STEP = 10
clip_bound = 0.01
stat_decay = 0.95
shampoo_rate = 0.1
decay_rate = 0.01
first_decay = 0.9
second_decay = 0.95
adam_rate = 0.04
table_rate = 0.5
gain_rate = 0.25
adam_eps = 1e-10
norm_eps = 1e-06
narrow = jnp.bfloat16
wide = jnp.float32
log2e = math.log2(math.e)
VM = 60 * 1024 * 1024


def params(limit=VM):
    return pltpu.CompilerParams(vmem_limit_bytes=limit)


def dot(a, b, ca=1, cb=0):
    return lax.dot_general(a, b, (((ca,), (cb,)), ((), ())), preferred_element_type=wide)


def norm_rows(v):
    c = v - jnp.mean(v, axis=-1, keepdims=True)
    r = lax.rsqrt(jnp.mean(c * c, axis=-1, keepdims=True) + norm_eps)
    return c * r, r


def back_rows(unit, r, scaled):
    return r * (
        scaled
        - jnp.mean(scaled, axis=-1, keepdims=True)
        - unit * jnp.mean(scaled * unit, axis=-1, keepdims=True)
    )


def spec(shape, index):
    return pl.BlockSpec(shape, index)


def beside(kernel, inputs, count):
    return lambda *refs: kernel(*refs[:inputs], *refs[inputs + count :])


def anywhere(arrays):
    return [pl.BlockSpec(memory_space=pl.ANY)] * len(arrays)


def held(shape):
    return pl.BlockSpec(shape, lambda *_: (0,) * len(shape), pipeline_mode=pl.Buffered(1))


def cost(flops, moved, trans=0):
    return pl.CostEstimate(flops=int(flops), bytes_accessed=int(moved), transcendentals=int(trans))


def embed_kernel(patch_ref, hot_ref, e_ref, gain_ref, embed_ref, first_ref):
    width = embed_ref.shape[2]
    v = dot(patch_ref[0, 0], e_ref[:, :width]) + dot(hot_ref[0], e_ref[:, width : width + 128], 1, 1)
    embed_ref[0] = v
    unit, _ = norm_rows(v)
    first_ref[0] = (unit * gain_ref[0:1]).astype(narrow)


def embed_call(patches, hot, e, gains):
    mb, width = patches.shape[0], gains.shape[1]
    steps = ROWS // TILE
    return pl.pallas_call(
        embed_kernel,
        grid=(mb, steps),
        in_specs=[
            spec((1, 1, TILE, patches.shape[3]), lambda m, i: (m, 0, i, 0)),
            spec((1, TILE, hot.shape[2]), lambda m, i: (m, i, 0)),
            held(e.shape),
            held(gains.shape),
        ],
        out_specs=[spec((1, TILE, width), lambda m, i: (m, i, 0))] * 2,
        out_shape=[
            jax.ShapeDtypeStruct((mb, ROWS, width), wide),
            jax.ShapeDtypeStruct((mb, ROWS, width), narrow),
        ],
        compiler_params=params(),
        cost_estimate=cost(2 * mb * ROWS * width * 896, 20e6),
    )(patches, hot, e, gains)


def group_mean(v, ones):
    return jnp.concatenate(
        [dot(v[:, at : at + 256].astype(narrow), ones) for at in range(0, v.shape[1], 256)], axis=1
    )


def project_kernel(first_ref, w_ref, gain_ref, ones_ref, q_ref, k_ref, v_ref, *kept):
    x = first_ref[0]
    width = x.shape[1]
    ones = ones_ref[...]
    for i, ref in enumerate((q_ref, k_ref)):
        raw = dot(x, w_ref[:, i * width : (i + 1) * width])
        c = raw - group_mean(raw, ones)
        r = lax.rsqrt(group_mean(c * c, ones) + norm_eps)
        unit = c * r
        kept[i][0] = unit.astype(narrow)
        kept[2 + i][0] = r.astype(narrow)
        out = (unit * gain_ref[1 + i : 2 + i]).astype(narrow)
        if i == 0:
            out = out * narrow(HEAD**-0.5)
        ref[0] = out
    v_ref[0] = dot(x, w_ref[:, 2 * width :]).astype(narrow)


def project_call(first, w, gains, ones):
    mb, _, width = first.shape
    rows = spec((1, TILE, width), lambda m, i: (m, i, 0))
    return pl.pallas_call(
        project_kernel,
        grid=(mb, ROWS // TILE),
        in_specs=[rows, held(w.shape), held(gains.shape), held(ones.shape)],
        out_specs=[rows] * 7,
        out_shape=[jax.ShapeDtypeStruct((mb, ROWS, width), narrow)] * 7,
        compiler_params=params(),
        cost_estimate=cost(2 * mb * ROWS * width * width * 3, 30e6),
    )(first, w, gains, ones)


ROWS_Q = 384


def attend_kernel(lengths_ref, q_ref, k_ref, v_ref, mixed_ref, stat_ref):
    pack, pair = pl.program_id(0), pl.program_id(1)
    lane = lax.broadcasted_iota(jnp.int32, (1, 2 * HEAD), 1)

    def part(start, count, tile, masked):
        k = k_ref[0, start : start + count]
        v = v_ref[0, start : start + count]
        zero = jnp.zeros_like(k)
        one = jnp.ones_like(k)
        k_both = [jnp.where(lane < HEAD, k, zero), jnp.where(lane < HEAD, zero, k)]
        ext = jnp.concatenate(
            [
                jnp.concatenate([jnp.where(lane < HEAD, v, zero), jnp.where(lane < HEAD, one, zero)], axis=1),
                jnp.concatenate([jnp.where(lane < HEAD, zero, v), jnp.where(lane < HEAD, zero, one)], axis=1),
            ],
            axis=0,
        )
        for at in range(start, start + count, tile):
            q = q_ref[0, at : at + tile]
            expos, peaks = [], []
            for h in range(2):
                s = dot(q, k_both[h], 1, 1)
                if masked:
                    limit = lengths_ref[pack, 1]
                    row = lax.broadcasted_iota(jnp.int32, s.shape, 0) + (at - start)
                    col = lax.broadcasted_iota(jnp.int32, s.shape, 1)
                    s = jnp.where((row < limit) == (col < limit), s, -1e30)
                peak = jnp.max(s, axis=1, keepdims=True)
                expos.append(jnp.exp2(s * log2e - peak * log2e).astype(narrow))
                peaks.append(peak)
            both = dot(jnp.concatenate(expos, axis=1), ext)
            total = both[:, 2 * HEAD :]
            mixed_ref[0, at : at + tile] = (both[:, : 2 * HEAD] / total).astype(narrow)
            lse = (jnp.where(lane < HEAD, peaks[0], peaks[1]) + jnp.log(total)) * log2e
            for h in range(2):
                column = jnp.sum(jnp.where(lane == h * HEAD, lse, 0.0), axis=1, keepdims=True)
                old = stat_ref[0, at : at + tile]
                stat_ref[0, at : at + tile] = jnp.where(lane == 2 * pair + h, column, old)

    part(0, LONG, ROWS_Q, False)
    part(LONG, SHORT, SHORT, True)


def attend_call(lengths, q, k, v):
    mb, _, width = q.shape
    block = pl.BlockSpec((1, ROWS, 2 * HEAD), lambda m, p, *_: (m, 0, p))
    pairs = width // (2 * HEAD)
    moved = mb * ROWS * width * 8
    return pl.pallas_call(
        attend_kernel,
        grid_spec=pltpu.PrefetchScalarGridSpec(
            num_scalar_prefetch=1,
            grid=(mb, pairs),
            in_specs=[block] * 3,
            out_specs=[block, pl.BlockSpec((1, ROWS, 128), lambda m, p, *_: (m, 0, 0))],
        ),
        out_shape=[
            jax.ShapeDtypeStruct((mb, ROWS, width), narrow),
            jax.ShapeDtypeStruct((mb, ROWS, 128), wide),
        ],
        compiler_params=params(),
        cost_estimate=cost(16 * mb * 2 * pairs * (LONG**2 + SHORT**2) * HEAD, moved),
    )(lengths, q, k, v)


def cdf_and_slope(up):
    cdf = 0.5 + 0.5 * lax.erf(up * 0.7071067811865476)
    slope = cdf + up * (jnp.exp2(up * up * (-0.5 * log2e)) * 0.3989422804014327)
    return cdf, slope


def forward_kernel(
    lengths_ref, embed_ref, mixed_ref, w_ref, gain_ref,
    second_ref, act_ref, slope_ref, unit2_ref, unit3_ref, stat_ref, pool_ref,
):
    pack, step = pl.program_id(0), pl.program_id(1)
    width = embed_ref.shape[2]
    resid = embed_ref[0] + dot(mixed_ref[0], w_ref[0])
    unit, r2 = norm_rows(resid)
    unit2_ref[0] = unit.astype(narrow)
    second = (unit * gain_ref[3:4]).astype(narrow)
    second_ref[0] = second
    outcome = resid
    for j in range(4):
        up = dot(second, w_ref[1 + j])
        cdf, slope = cdf_and_slope(up)
        act = (up * cdf).astype(narrow)
        act_ref[j, 0] = act
        slope_ref[j, 0] = slope.astype(narrow)
        outcome = outcome + dot(act, w_ref[5 + j])
    unit, r3 = norm_rows(outcome)
    unit3_ref[0] = unit.astype(narrow)
    lane = lax.broadcasted_iota(jnp.int32, (1, 128), 1)
    stat_ref[0] = jnp.where(lane == 0, r2, r3)
    final = unit * gain_ref[4:5]

    @pl.when(step == 0)
    def _():
        pool_ref[...] = jnp.zeros_like(pool_ref)

    row = lax.broadcasted_iota(jnp.int32, (TILE, 1), 0) + step * TILE
    first_len, second_len = lengths_ref[pack, 0], lengths_ref[pack, 1]
    inside = (row < first_len, (row >= first_len) & (row < first_len + second_len))
    for s in range(2):
        total = jnp.sum(jnp.where(inside[s], final, 0.0), axis=0, keepdims=True)
        pool_ref[0, s : s + 1] += total


def forward_call(lengths, embed, mixed, w, gains):
    mb, _, width = embed.shape
    rows = pl.BlockSpec((1, TILE, width), lambda m, i, *_: (m, i, 0))
    wider = pl.BlockSpec((4, 1, TILE, width), lambda m, i, *_: (0, m, i, 0))
    return pl.pallas_call(
        forward_kernel,
        grid_spec=pltpu.PrefetchScalarGridSpec(
            num_scalar_prefetch=1,
            grid=(mb, ROWS // TILE),
            in_specs=[rows, rows, held(w.shape), held(gains.shape)],
            out_specs=[
                rows, wider, wider, rows, rows,
                pl.BlockSpec((1, TILE, 128), lambda m, i, *_: (m, i, 0)),
                pl.BlockSpec((1, 8, width), lambda m, i, *_: (m, 0, 0)),
            ],
        ),
        out_shape=[
            jax.ShapeDtypeStruct((mb, ROWS, width), narrow),
            jax.ShapeDtypeStruct((4, mb, ROWS, width), narrow),
            jax.ShapeDtypeStruct((4, mb, ROWS, width), narrow),
            jax.ShapeDtypeStruct((mb, ROWS, width), narrow),
            jax.ShapeDtypeStruct((mb, ROWS, width), narrow),
            jax.ShapeDtypeStruct((mb, ROWS, 128), wide),
            jax.ShapeDtypeStruct((mb, 8, width), wide),
        ],
        compiler_params=params(),
        cost_estimate=cost(2 * mb * ROWS * width * width * 9, 80e6),
    )(lengths, embed, mixed, w, gains)


def head_kernel(pool_ref, scale_ref, weight_ref, label_ref, head_ref, loss_ref, dhead_ref, dpool_ref):
    pooled = (pool_ref[...] * scale_ref[:, 0:1]).astype(narrow)
    logits = dot(pooled, head_ref[...])
    peak = jnp.max(logits, axis=1, keepdims=True)
    expo = jnp.exp(logits - peak)
    total = jnp.sum(expo, axis=1, keepdims=True)
    hot = lax.broadcasted_iota(jnp.int32, logits.shape, 1) == label_ref[:, 0:1]
    picked = jnp.sum(jnp.where(hot, logits, 0.0), axis=1, keepdims=True)
    weight = weight_ref[:, 0:1].astype(wide)
    loss = jnp.where(weight > 0, weight * (peak + jnp.log(total) - picked), 0.0)
    loss_ref[...] = jnp.broadcast_to(jnp.sum(loss, axis=0, keepdims=True), loss_ref.shape)
    dlogits = (weight * (expo / total - hot.astype(wide))).astype(narrow)
    dhead_ref[...] = dot(pooled, dlogits, 0, 0).astype(dhead_ref.dtype)
    dpool_ref[...] = dot(dlogits, head_ref[...], 1, 1) * scale_ref[:, 0:1]


def head_call(pool, scale, weight, label, head, out=wide):
    rows, width = pool.shape
    return pl.pallas_call(
        head_kernel,
        out_shape=[
            jax.ShapeDtypeStruct((8, 128), wide),
            jax.ShapeDtypeStruct(head.shape, out),
            jax.ShapeDtypeStruct((rows, width), wide),
        ],
        compiler_params=params(),
        cost_estimate=cost(6 * rows * width * 1000, 8e6),
    )(pool, scale, weight, label, head)


def backward_kernel(
    lengths_ref, dpool_ref, unit3_ref, unit2_ref, stat_ref, slope_ref, mixed_ref, w_ref, gain_ref, pick_ref,
    dm_ref, dup_ref, dr_ref, dmixed_ref, delta_ref, dgain_ref,
):
    pack, step = pl.program_id(0), pl.program_id(1)
    row = lax.broadcasted_iota(jnp.int32, (TILE, 1), 0) + step * TILE
    first_len, second_len = lengths_ref[pack, 0], lengths_ref[pack, 1]
    dfinal = jnp.where(
        row < first_len,
        dpool_ref[0, 0:1],
        jnp.where(row < first_len + second_len, dpool_ref[0, 1:2], 0.0),
    )
    unit3 = unit3_ref[0].astype(wide)
    r2, r3 = stat_ref[0, :, 0:1], stat_ref[0, :, 1:2]
    doutcome = back_rows(unit3, r3, dfinal * gain_ref[4:5])
    dgf = jnp.sum(dfinal * unit3, axis=0, keepdims=True)
    dm = doutcome.astype(narrow)
    dm_ref[0] = dm
    dsecond = None
    for j in range(4):
        dact = dot(dm, w_ref[5 + j], 1, 1)
        dup = (dact * slope_ref[j, 0].astype(wide)).astype(narrow)
        dup_ref[j, 0] = dup
        term = dot(dup, w_ref[1 + j], 1, 1)
        dsecond = term if dsecond is None else dsecond + term
    unit2 = unit2_ref[0].astype(wide)
    dg2 = jnp.sum(dsecond * unit2, axis=0, keepdims=True)
    dresid = doutcome + back_rows(unit2, r2, dsecond * gain_ref[3:4])
    dr = dresid.astype(narrow)
    dr_ref[0] = dr
    dmixed = dot(dr, w_ref[0], 1, 1).astype(narrow)
    dmixed_ref[0] = dmixed
    delta_ref[0] = dot(dmixed * mixed_ref[0], pick_ref[...])

    @pl.when((pack == 0) & (step == 0))
    def _():
        dgain_ref[...] = jnp.zeros_like(dgain_ref)

    dgain_ref[3:4] += dg2
    dgain_ref[4:5] += dgf


def backward_call(lengths, dpool, unit3, unit2, stat, slope, mixed, w, gains, pick):
    mb, _, width = unit3.shape
    rows = pl.BlockSpec((1, TILE, width), lambda m, i, *_: (m, i, 0))
    lanes = pl.BlockSpec((1, TILE, 128), lambda m, i, *_: (m, i, 0))
    wider = pl.BlockSpec((4, 1, TILE, width), lambda m, i, *_: (0, m, i, 0))
    return pl.pallas_call(
        backward_kernel,
        grid_spec=pltpu.PrefetchScalarGridSpec(
            num_scalar_prefetch=1,
            grid=(mb, ROWS // TILE),
            in_specs=[
                pl.BlockSpec((1, 8, width), lambda m, i, *_: (m, 0, 0)),
                rows, rows, lanes, wider, rows,
                held(w.shape), held(gains.shape), held(pick.shape),
            ],
            out_specs=[rows, wider, rows, rows, lanes, pl.BlockSpec((8, width), lambda m, i, *_: (0, 0))],
        ),
        out_shape=[
            jax.ShapeDtypeStruct((mb, ROWS, width), narrow),
            jax.ShapeDtypeStruct((4, mb, ROWS, width), narrow),
            jax.ShapeDtypeStruct((mb, ROWS, width), narrow),
            jax.ShapeDtypeStruct((mb, ROWS, width), narrow),
            jax.ShapeDtypeStruct((mb, ROWS, 128), wide),
            jax.ShapeDtypeStruct((8, width), wide),
        ],
        compiler_params=params(),
        cost_estimate=cost(2 * mb * ROWS * width * width * 9, 70e6),
    )(lengths, dpool, unit3, unit2, stat, slope, mixed, w, gains, pick)


def attend_back_kernel(
    lengths_ref, q_ref, k_ref, v_ref, do_ref, qunit_ref, kunit_ref, qr_ref, kr_ref, stat_ref, gain_ref, ones_ref,
    dq_ref, dk_ref, dv_ref, dgain_ref, dq_acc, dk_acc, dv_acc,
):
    pack = pl.program_id(1)
    lane = lax.broadcasted_iota(jnp.int32, (1, 2 * HEAD), 1)

    def both(x, axis=0):
        zero = jnp.zeros_like(x)
        return jnp.concatenate([jnp.where(lane < HEAD, x, zero), jnp.where(lane < HEAD, zero, x)], axis=axis)

    def part(start, count, tile, chunk, masked):
        for ti in range(start, start + count, tile):
            q2 = both(q_ref[0, ti : ti + tile])
            do2 = both(do_ref[0, ti : ti + tile])
            lse = jnp.concatenate([stat_ref[0, h : h + 1, ti : ti + tile] for h in (0, 1)], axis=1)
            delta = jnp.concatenate([stat_ref[0, h : h + 1, ti : ti + tile] for h in (2, 3)], axis=1)
            for ui in range(start, start + count, chunk):
                k = k_ref[0, ui : ui + chunk]
                v = v_ref[0, ui : ui + chunk]
                s = dot(k, q2, 1, 1)
                p = jnp.exp2(s * log2e - lse)
                if masked:
                    limit = lengths_ref[pack, 1]
                    row = lax.broadcasted_iota(jnp.int32, s.shape, 0) + (ui - start)
                    col = lax.broadcasted_iota(jnp.int32, s.shape, 1)
                    col = jnp.where(col < tile, col, col - tile) + (ti - start)
                    p = jnp.where((row < limit) == (col < limit), p, 0.0)
                dp = dot(v, do2, 1, 1)
                ds = (p * (dp - delta)).astype(narrow)
                dv_new = dot(p.astype(narrow), do2)
                dk_new = dot(ds, q2)
                k2 = both(k)
                ds_rows = jnp.concatenate([ds[:, :tile], ds[:, tile:]], axis=0)
                dq_new = dot(ds_rows, k2, 0, 0)
                if ti == start:
                    dv_acc[ui : ui + chunk] = dv_new
                    dk_acc[ui : ui + chunk] = dk_new
                else:
                    dv_acc[ui : ui + chunk] += dv_new
                    dk_acc[ui : ui + chunk] += dk_new
                if ui == start:
                    dq_acc[ti : ti + tile] = dq_new
                else:
                    dq_acc[ti : ti + tile] += dq_new

    part(0, LONG, 384, 384, False)
    part(LONG, SHORT, SHORT, SHORT, True)
    dv_ref[0] = dv_acc[...].astype(narrow)
    ones = ones_ref[...]

    def mean(x):
        return dot(x.astype(narrow), ones)

    @pl.when(pack == 0)
    def _():
        dgain_ref[...] = jnp.zeros_like(dgain_ref)

    for i, (acc, unit_ref, r_ref, ref, factor) in enumerate(
        ((dq_acc, qunit_ref, qr_ref, dq_ref, HEAD**-0.5), (dk_acc, kunit_ref, kr_ref, dk_ref, 1.0))
    ):
        unit, r = unit_ref[0].astype(wide), r_ref[0].astype(wide)
        dy = acc[...] * factor
        dgain_ref[0, i : i + 1] += jnp.sum(dy * unit, axis=0, keepdims=True)
        scaled = dy * gain_ref[1 + i : 2 + i]
        ref[0] = (r * (scaled - mean(scaled) - unit * mean(scaled * unit))).astype(narrow)


def attend_back_call(lengths, q, k, v, do, kept, stat, gains, ones, first_pair, pairs, first=()):
    mb, _, width = q.shape
    block = pl.BlockSpec((1, ROWS, 2 * HEAD), lambda p, m, *_: (m, 0, p + first_pair))
    out = pl.BlockSpec((1, ROWS, 2 * HEAD), lambda p, m, *_: (m, 0, p))
    shape = jax.ShapeDtypeStruct((mb, ROWS, pairs * 2 * HEAD), narrow)
    return pl.pallas_call(
        beside(attend_back_kernel, 12, len(first)),
        grid_spec=pltpu.PrefetchScalarGridSpec(
            num_scalar_prefetch=1,
            grid=(pairs, mb),
            in_specs=[
                *[block] * 8,
                pl.BlockSpec((1, 8, ROWS), lambda p, m, *_: (m, p + first_pair, 0)),
                pl.BlockSpec((8, 2 * HEAD), lambda p, m, *_: (0, p + first_pair)),
                pl.BlockSpec((2 * HEAD, 2 * HEAD), lambda p, m, *_: (0, 0)),
                *anywhere(first),
            ],
            out_specs=[out, out, out, pl.BlockSpec((1, 8, 2 * HEAD), lambda p, m, *_: (p, 0, 0))],
            scratch_shapes=[pltpu.VMEM((ROWS, 2 * HEAD), wide)] * 3,
        ),
        out_shape=[shape, shape, shape, jax.ShapeDtypeStruct((pairs, 8, 2 * HEAD), wide)],
        compiler_params=params(),
        cost_estimate=cost(20 * mb * 2 * pairs * (LONG**2 + SHORT**2) * HEAD * 2, mb * ROWS * pairs * 128 * 18),
    )(lengths, q, k, v, do, *kept, stat, gains, ones, *first)


def first_kernel(*refs, parts):
    grads = refs[: 3 * parts]
    embed_ref, dr_ref, w_ref, gain_ref, out_ref, dgain_ref = refs[3 * parts :]
    step = pl.program_id(0) * pl.num_programs(1) + pl.program_id(1)
    width = embed_ref.shape[2]
    total = None
    for i in range(3):
        rows = jnp.concatenate([grads[3 * p + i][0] for p in range(parts)], axis=1)
        term = dot(rows, w_ref[:, i * width : (i + 1) * width], 1, 1)
        total = term if total is None else total + term
    unit, r = norm_rows(embed_ref[0])

    @pl.when(step == 0)
    def _():
        dgain_ref[...] = jnp.zeros_like(dgain_ref)

    dgain_ref[0:1] += jnp.sum(total * unit, axis=0, keepdims=True)
    out_ref[0] = (dr_ref[0].astype(wide) + back_rows(unit, r, total * gain_ref[0:1])).astype(narrow)


def first_call(grads, embed, dr, w, gains, first=()):
    mb, _, width = embed.shape
    rows = spec((1, TILE, width), lambda m, i: (m, i, 0))
    parts = len(grads) // 3
    return pl.pallas_call(
        beside(functools.partial(first_kernel, parts=parts), len(grads) + 4, len(first)),
        grid=(mb, ROWS // TILE),
        in_specs=[spec((1, TILE, g.shape[2]), lambda m, i: (m, i, 0)) for g in grads]
        + [rows, rows, held(w.shape), held(gains.shape)]
        + anywhere(first),
        out_specs=[rows, spec((8, width), lambda m, i: (0, 0))],
        out_shape=[
            jax.ShapeDtypeStruct((mb, ROWS, width), narrow),
            jax.ShapeDtypeStruct((8, width), wide),
        ],
        compiler_params=params(),
        cost_estimate=cost(2 * mb * ROWS * width * width * 3, 32e6),
    )(*grads, embed, dr, w, gains, *first)


def split_rows(value, own_ref, sent_ref, me, n):
    across, up, deep = own_ref.shape[:3]
    part = own_ref.shape[4]
    for x in range(across):
        for y in range(up):
            for z in range(deep):
                at = ((z * up + y) * across + x) * 2 * part
                first = value[at : at + part].astype(narrow)
                second = value[at + part : at + 2 * part].astype(narrow)
                own_ref[x, y, z, n] = jnp.where(me == 0, first, second)
                sent_ref[x, y, z, n] = jnp.where(me == 0, second, first)


def flat_rows(ref):
    return ref[...].reshape(-1, ref.shape[-1])


def weight_kernel(act_ref, dm_ref, second_ref, dup_ref, out_ref):
    step = pl.program_id(0)

    def write(a_ref, b_ref):
        value = dot(flat_rows(a_ref), flat_rows(b_ref), 0, 0)
        part = out_ref.shape[2]
        for to in range(out_ref.shape[0]):
            out_ref[to, 0] = value[to * part : (to + 1) * part].astype(narrow)

    pl.when(step < 4)(lambda: write(second_ref, dup_ref))
    pl.when(step >= 4)(lambda: write(act_ref, dm_ref))


def split_shape(rows):
    core, x, y, z = (level[2] for level in levels())
    return (x, y, z), rows // (core * x * y * z)


def core_at():
    return (lax.axis_index("seq") % 2).reshape(1).astype(jnp.int32)


def weight_call(act, dm, second, dup):
    width = dm.shape[2]
    parts = lax.axis_size("fsdp") * lax.axis_size("seq")
    rows = held(dm.shape)
    one = (1, *dm.shape)
    return pl.pallas_call(
        weight_kernel,
        grid=(8,),
        in_specs=[
            spec(one, lambda i: (jnp.maximum(i - 4, 0), 0, 0, 0)),
            rows,
            rows,
            spec(one, lambda i: (jnp.minimum(i, 3), 0, 0, 0)),
        ],
        out_specs=spec((parts, 1, width // parts, width), lambda i: (0, i, 0, 0)),
        out_shape=jax.ShapeDtypeStruct((parts, 8, width // parts, width), narrow),
        compiler_params=params(),
        cost_estimate=cost(2 * 8 * dm.size * width, 60e6),
    )(act, dm, second, dup)


def one_weight_kernel(at_ref, *refs, groups):
    count = len(groups) + sum(groups)
    own_ref, sent_ref, total = refs[count:]
    step = pl.program_id(0)
    last = step == pl.num_programs(0) - 1
    at, ref = 0, 0
    for members in groups:
        a = refs[ref][0]
        for b_ref in refs[ref + 1 : ref + 1 + members]:
            lanes = pl.ds(at, b_ref.shape[-1])
            at += b_ref.shape[-1]
            value = dot(a, b_ref[0], 0, 0)

            @pl.when(step == 0)
            def _(value=value, lanes=lanes):
                total[:, lanes] = value

            @pl.when((step > 0) & ~last)
            def _(value=value, lanes=lanes):
                total[:, lanes] += value

            @pl.when(last)
            def _(value=value, lanes=lanes):
                split_rows(total[:, lanes] + value, own_ref.at[..., lanes], sent_ref.at[..., lanes], at_ref[0], 0)

        ref += 1 + members


def one_weight_call(*groups, first=()):
    arrays = [array for group in groups for array in group]
    mb, rows, depth = arrays[0].shape
    width = sum(x.shape[-1] for group in groups for x in group[1:])
    (x, y, z), part = split_shape(depth)
    shape = (x, y, z, 1, part, width)
    out = pl.BlockSpec(shape, lambda m, *_: (0,) * 6)
    return pl.pallas_call(
        beside(
            functools.partial(one_weight_kernel, groups=[len(group) - 1 for group in groups]),
            1 + len(arrays),
            len(first),
        ),
        grid_spec=pltpu.PrefetchScalarGridSpec(
            num_scalar_prefetch=1,
            grid=(mb,),
            in_specs=[pl.BlockSpec((1, *v.shape[1:]), lambda m, *_: (m, 0, 0)) for v in arrays]
            + anywhere(first),
            out_specs=[out] * 2,
            scratch_shapes=[pltpu.VMEM((depth, width), wide)],
        ),
        out_shape=[jax.ShapeDtypeStruct(shape, narrow)] * 2,
        compiler_params=params(),
        cost_estimate=cost(2 * mb * rows * depth * width, 12e6),
    )(core_at(), *arrays, *first)


def embed_weight_kernel(at_ref, patch_ref, hot_ref, grad_ref, gain_ref, own_ref, sent_ref, total):
    step = pl.program_id(0)
    grad = grad_ref[0]
    width = grad.shape[1]
    value = dot(patch_ref[0, 0], grad, 0, 0)
    table = dot(grad, hot_ref[0], 0, 0)

    @pl.when(step == 0)
    def _():
        total[:, :width] = value
        total[:, width : width + 128] = table

    @pl.when(step > 0)
    def _():
        total[:, :width] += value
        total[:, width : width + 128] += table

    @pl.when(step == pl.num_programs(0) - 1)
    def _():
        total[:, width + 128 :] = gain_ref[...]
        split_rows(total[...], own_ref, sent_ref, at_ref[0], 0)


def embed_weight_call(patches, hot, grad, gain_columns, first=()):
    mb, _, width = grad.shape
    pixels = patches.shape[3]
    (x, y, z), part = split_shape(pixels)
    shape = (x, y, z, 1, part, width + 256)
    out = pl.BlockSpec(shape, lambda m, *_: (0,) * 6)
    return pl.pallas_call(
        beside(embed_weight_kernel, 5, len(first)),
        grid_spec=pltpu.PrefetchScalarGridSpec(
            num_scalar_prefetch=1,
            grid=(mb,),
            in_specs=[
                pl.BlockSpec((1, 1, ROWS, pixels), lambda m, *_: (m, 0, 0, 0)),
                pl.BlockSpec((1, ROWS, hot.shape[2]), lambda m, *_: (m, 0, 0)),
                pl.BlockSpec((1, ROWS, width), lambda m, *_: (m, 0, 0)),
                pl.BlockSpec((width, 128), lambda m, *_: (0, 0)),
                *anywhere(first),
            ],
            out_specs=[out, out],
            scratch_shapes=[pltpu.VMEM((pixels, width + 256), wide)],
        ),
        out_shape=[jax.ShapeDtypeStruct(shape, narrow)] * 2,
        compiler_params=params(),
        cost_estimate=cost(2 * grad.size * (pixels + 128), 12e6),
    )(core_at(), patches, hot, grad, gain_columns, *first)


def fold(parts):
    while len(parts) > 1:
        parts = [parts[i] + parts[i + 1] for i in range(0, len(parts), 2)]
    return parts[0]


def swap(x, axis, bits):
    if bits == 0:
        return x
    return lax.ppermute(x, axis, [(i, i ^ bits) for i in range(lax.axis_size(axis))])


def tied(x, *after):
    return lax.optimization_barrier((x, *after))[0]


def pick_index(x, index, dim):
    return lax.dynamic_index_in_dim(x, index, dim, keepdims=False)


def levels():
    across, deep = lax.axis_size("seq"), lax.axis_size("fsdp")
    y = 1 << ((deep.bit_length() - 1) // 2)
    return (("seq", 1, 2), ("seq", 2, across // 2), ("fsdp", 1, y), ("fsdp", y, deep // y))


CORE, X, Y, Z = range(4)


class Sum:
    def __init__(self, terms, which):
        axis, stride, size = levels()[which]
        at = lax.axis_index(axis) // stride % size

        def part(k):
            return fold([pick_index(term, at ^ k, 0).astype(wide) for term in terms])

        self.sent = [part(k).astype(narrow) for k in range(1, size)]
        self.terms = [part(0)] + [swap(x, axis, (k + 1) * stride) for k, x in enumerate(self.sent)]

    def after(self, *others):
        return [tied(self.terms[0], *others), *self.terms[1:]]

    def total(self):
        return fold([term.astype(wide) for term in self.terms])


def core_terms(own, sent):
    return [own, swap(sent, "seq", 1)]


def settle_kernel(at_ref, *refs, count, moves):
    sources, outs = refs[:count], refs[count:]
    for source, index, out, target in moves:
        outs[out][target(at_ref[0], at_ref[1])] = sources[source][index]


def mesh_at():
    return jnp.stack([lax.axis_index("fsdp"), lax.axis_index("seq")]).astype(jnp.int32)


def in_vmem(count):
    return [pl.BlockSpec(memory_space=pltpu.VMEM)] * count


def settled(parts, shapes, moves):
    size = sum(part.size for part in parts) * parts[0].dtype.itemsize
    return pl.pallas_call(
        functools.partial(settle_kernel, count=len(parts), moves=moves),
        in_specs=[pl.BlockSpec(memory_space=pltpu.SMEM)] + in_vmem(len(parts)),
        out_specs=in_vmem(len(shapes)),
        out_shape=[jax.ShapeDtypeStruct(shape, parts[0].dtype) for shape in shapes],
        compiler_params=params(),
        cost_estimate=cost(0, 2 * size),
    )(mesh_at(), *parts)


def seq_parts(x, *after):
    half = [swap(x, "seq", k) for k in range(0, lax.axis_size("seq"), 2)]
    if after:
        half = [half[0]] + [tied(y, *after) for y in half[1:]]
    return [part for y in half for part in (y, swap(y, "seq", 1))]


def settle_rows(parts, cuts, shapes):
    deep = parts[0].shape[0]
    moves = [
        (j, (k, slice(start, stop)), out, lambda f, s, j=j, k=k, index=index: (*index, k ^ f, j ^ s))
        for j in range(len(parts))
        for k in range(deep)
        for start, stop, out, index in cuts
    ]
    return settled(parts, shapes, moves)


def near_exchange(x):
    return jnp.stack([swap(x, "fsdp", k) for k in range(levels()[Y][2])])


def far_exchange(x):
    _, stride, far = levels()[Z]
    return [swap(x, "fsdp", k * stride) for k in range(far)]


def stacked(parts):
    return jnp.stack(parts).reshape(-1, *parts[0].shape[1:])


def my_rows(x):
    size = lax.axis_size("seq")
    return pick_index(x.reshape(x.shape[0], size, x.shape[1] // size, x.shape[2]), lax.axis_index("seq"), 1)


def grads_kernel(at_ref, factor_ref, *refs, count, part):
    parts, (out_ref, small_ref) = refs[:count], refs[count:]
    factor = factor_ref[0]
    for j, ref in enumerate(parts):
        to = at_ref[1] ^ j
        for b in range(out_ref.shape[0]):
            out_ref[b, to] = ref[b * part : (b + 1) * part].astype(wide) * factor
        small_ref[to] = ref[out_ref.shape[0] * part :].astype(wide) * factor


def collect_kernel(at_ref, slot_ref, scalar_ref, rest_ref, mid_ref, *refs, count, deep, per, columns):
    terms, (own_ref, *out_refs) = refs[:count], refs[count : count + 1 + deep]
    blocks = refs[-1]
    part, width = rest_ref.shape[1:]
    scale = 1.0 / scalar_ref[0]
    both = fold([ref[0].astype(wide) for ref in terms])
    late = both[:, width + 256 :]
    remain = width - columns
    pieces = [both[:, :width]]
    for i in range(3):
        first = mid_ref[:, width + i * columns : width + (i + 1) * columns]
        pieces.append(jnp.concatenate([first, late[:, i * remain : (i + 1) * remain]], axis=1))
    pieces.append(mid_ref[:, :width])
    pieces += [rest_ref[i].astype(wide) for i in range(rest_ref.shape[0])]
    squares = jnp.zeros((1, 1), wide)
    total = jnp.zeros((part, width), wide)
    for b, piece in enumerate(pieces):
        piece = (piece * scale).astype(narrow)
        blocks[b] = piece
        own_ref[b * part : (b + 1) * part] = piece
        total += jnp.square(piece.astype(wide))
    small = (both[:, width : width + 256] * scale).astype(narrow)
    third = part // 3
    small = small.astype(wide)
    squares = jnp.sum(total, keepdims=True) + jnp.sum(jnp.square(small), keepdims=True) + scalar_ref[1]
    small = jnp.concatenate([small[i * third : (i + 1) * third] for i in range(3)], axis=1)
    own_ref[len(pieces) * part :] = small.astype(narrow)
    row = lax.broadcasted_iota(jnp.int32, (8, width), 0)
    notes = jnp.zeros((8, width), wide)
    for at, value in ((0, squares), (3, jnp.full((1, 1), scalar_ref[2]))):
        for i in range(3):
            piece = value.astype(narrow).astype(wide)
            value = value - piece
            notes = jnp.where(row == at + i, piece, notes)
    notes = notes.astype(narrow)
    blocks[len(pieces)] = jnp.zeros((part, width), narrow)
    for k, out_ref in enumerate(out_refs):
        for i in range(per):
            slot = (at_ref[0] ^ k) * per + i
            found = len(pieces)
            for b in range(len(pieces)):
                found = jnp.where(slot_ref[b] == slot, b, found)
            out_ref[i * part : (i + 1) * part] = blocks[found]
        out_ref[per * part :] = notes


def collect_call(block_slot, scalars, rest, mid, terms, per, columns):
    part, width = rest.shape[1:]
    deep = lax.axis_size("fsdp")
    count = block_slot.shape[0]
    smem = pl.BlockSpec(memory_space=pltpu.SMEM)
    message = jax.ShapeDtypeStruct((per * part + 8, width), narrow)
    return pl.pallas_call(
        functools.partial(collect_kernel, count=len(terms), deep=deep, per=per, columns=columns),
        in_specs=[smem, smem, smem] + in_vmem(2 + len(terms)),
        out_specs=in_vmem(1 + deep),
        out_shape=[jax.ShapeDtypeStruct((count * part + part // 3, width), narrow)] + [message] * deep,
        scratch_shapes=[pltpu.VMEM((count + 1, part, width), narrow)],
        compiler_params=params(),
        cost_estimate=cost(0, 4e6),
    )(mesh_at(), block_slot, scalars, rest, mid, *terms)


def halves(x):
    high = x.astype(narrow)
    return high, (x - high.astype(wide)).astype(narrow)


def direction_kernel(at_ref, left_ref, right_ref, *refs, count, deep):
    parts, slotted_ref, notes_ref = refs[:count], refs[count], refs[count + 1]
    out_refs, rows, result = refs[count + 2 : count + 2 + deep], refs[-2], refs[-1]
    per, _, part, width = left_ref.shape
    for j, ref in enumerate(parts):
        for k in range(deep):
            f, s = at_ref[0] ^ k, at_ref[1] ^ j
            for i in range(per):
                rows[i, f * count + s] = ref[k, i * part : (i + 1) * part].astype(wide)
            notes_ref[f, s] = ref[k, per * part :]
    for i in range(per):
        grad = rows[i].reshape(deep * count * part, width).astype(narrow)
        slotted_ref[i] = grad
        left_high, left_low = halves(left_ref[i].reshape(deep * part, width))
        inner_high, inner_low = halves(dot(left_high, grad) + dot(left_low, grad))
        right_high, right_low = halves(right_ref[i])
        value = dot(inner_high, right_high) + dot(inner_low, right_high) + dot(inner_high, right_low)
        result[i] = value.reshape(deep, part, width)
    for k, out_ref in enumerate(out_refs):
        for i in range(per):
            out_ref[i] = result[i, at_ref[0] ^ k].astype(narrow)


def direction_call(left, right, parts):
    per, deep, part, width = left.shape
    count = len(parts)
    return pl.pallas_call(
        functools.partial(direction_kernel, count=count, deep=deep),
        in_specs=[pl.BlockSpec(memory_space=pltpu.SMEM)] + in_vmem(2 + count),
        out_specs=in_vmem(2 + deep),
        out_shape=[
            jax.ShapeDtypeStruct((per, width, width), narrow),
            jax.ShapeDtypeStruct((deep, count, 8, width), narrow),
        ]
        + [jax.ShapeDtypeStruct((per, part, width), narrow)] * deep,
        scratch_shapes=[
            pltpu.VMEM((per, deep * count, part, width), wide),
            pltpu.VMEM((per, deep, part, width), wide),
        ],
        compiler_params=params(),
        cost_estimate=cost(10 * per * deep * part * width * width, 16e6),
    )(mesh_at(), left, right, *parts)


def select_kernel(at_ref, slot_ref, *refs, deep):
    parts, out_ref, slots = refs[:deep], refs[deep], refs[deep + 1]
    per, part = parts[0].shape[:2]
    for k, ref in enumerate(parts):
        for i in range(per):
            slots[(at_ref[0] ^ k) * per + i] = ref[i]
    for b in range(out_ref.shape[0] // part):
        out_ref[b * part : (b + 1) * part] = slots[slot_ref[b]]


def select_call(block_slot, parts):
    per, part, width = parts[0].shape
    deep = len(parts)
    smem = pl.BlockSpec(memory_space=pltpu.SMEM)
    return pl.pallas_call(
        functools.partial(select_kernel, deep=deep),
        in_specs=[smem, smem] + in_vmem(deep),
        out_specs=pl.BlockSpec(memory_space=pltpu.VMEM),
        out_shape=jax.ShapeDtypeStruct((block_slot.shape[0] * part, width), narrow),
        scratch_shapes=[pltpu.VMEM((deep * per, part, width), narrow)],
        compiler_params=params(),
        cost_estimate=cost(0, 2e6),
    )(mesh_at(), block_slot, *parts)


def update_kernel(at_ref, factor_ref, block_ref, *refs, count, part):
    parts, out_ref = refs[:count], refs[count]
    factor = factor_ref[0]
    for j, ref in enumerate(parts):
        to = at_ref[1] ^ j
        for b in range(out_ref.shape[0]):
            old = block_ref[b, to]
            step = ref[b * part : (b + 1) * part].astype(wide) * factor
            out_ref[b, to] = old - shampoo_rate * (step + decay_rate * old)


def finish_call(kernel, factor, arrays, parts, part, shapes):
    smem = pl.BlockSpec(memory_space=pltpu.SMEM)
    return pl.pallas_call(
        functools.partial(kernel, count=len(parts), part=part),
        in_specs=[smem, smem] + in_vmem(len(arrays) + len(parts)),
        out_specs=in_vmem(len(shapes)),
        out_shape=[jax.ShapeDtypeStruct(shape, wide) for shape in shapes],
        compiler_params=params(),
        cost_estimate=cost(0, 12e6),
    )(mesh_at(), factor.reshape(1), *arrays, *parts)


def adam(weight, grad, first, second, rate, decay):
    first_new = first_decay * first + (1 - first_decay) * grad
    second_new = second_decay * second + (1 - second_decay) * grad * grad
    corrected = (
        first_new
        / (1 - first_decay**STEP)
        / (jnp.sqrt(second_new / (1 - second_decay**STEP)) + adam_eps)
    )
    return (weight - rate * (corrected + decay * weight), first_new, second_new)


def product(spec_text, a, b):
    return jnp.einsum(spec_text, a, b, preferred_element_type=wide)


def local(
    patches, positions, lengths, res_weights, labels, block_slot, blocks, pos_table, gains, head,
    left_stats, right_stats, left_roots, right_roots,
    pos_first, pos_second, gain_first, gain_second, head_first, head_second,
):
    mb = patches.shape[0]
    deep, size = lax.axis_size("fsdp"), lax.axis_size("seq")
    me_f, me_s = lax.axis_index("fsdp"), lax.axis_index("seq")
    lengths, res_weights, labels = (x[:, 0] for x in (lengths, res_weights, labels))
    lanes = pos_table.shape[2]
    width = lanes * deep
    grid_rows = pos_table.shape[1]

    part = blocks.shape[1] // size
    seen = jnp.broadcast_to(jnp.sum(res_weights).astype(wide), (lanes, 3))
    small = jnp.concatenate(
        [pos_table.reshape(2 * grid_rows, lanes).T, gains.T, seen, jnp.zeros((lanes, 120), wide)], axis=1
    ).astype(narrow)
    opening = my_rows(jnp.concatenate([blocks[0].astype(narrow), small], axis=1)[None])[0]
    project = my_rows(blocks[1:4]).astype(narrow).transpose(1, 0, 2).reshape(part, 3 * width)
    every = far_exchange(near_exchange(jnp.concatenate([opening, project], axis=1)))
    places = positions[:, :, 0, :ROWS]
    grid = jnp.arange(grid_rows)
    hot = jnp.concatenate([places[i][:, :, None] == grid for i in range(2)], axis=2).astype(narrow)
    index = jnp.arange(256)
    ones = jnp.where(index[:, None] // HEAD == index[None] // HEAD, 1 / HEAD, 0).astype(narrow)
    pick = (jnp.arange(width)[:, None] // HEAD == jnp.arange(128)[None]).astype(narrow)

    def column(x):
        x = jnp.pad(x, ((0, 0), (0, 6))).reshape(8 * mb, 1)
        return jnp.broadcast_to(x, (8 * mb, 128))

    seq_columns = [column(1.0 / lengths.astype(wide)), column(res_weights), column(labels)]
    rest_part = my_rows(blocks[4:13]).astype(narrow)
    head_part = my_rows(head[None])[0].astype(narrow)
    ahead = (hot, ones, pick, rest_part, head_part, *seq_columns)
    every = [every[0], tied(every[1], *ahead), *every[2:]]
    opening = seq_parts(stacked([x[:, :, : width + 256] for x in every]))
    project = stacked([x[:, :, width + 256 :] for x in every])
    w_embed = settle_rows(opening, [(0, part, 0, ())], [(deep, size, part, width + 256)])[0]
    w_embed = w_embed.reshape(width, width + 256)
    gains_full = w_embed[:, width + 128 :].T[:8].astype(wide)
    weight_sum = jnp.sum(gains_full[5].reshape(deep * size, part)[:, 0])
    w_rest = lax.all_gather(tied(rest_part, opening[-1]), ("fsdp", "seq"), axis=1, tiled=True)
    w_head = lax.all_gather(tied(head_part, opening[-1]), ("fsdp", "seq"), axis=0, tiled=True)

    embed, first = embed_call(patches, hot, tied(w_embed, project), gains_full)
    w_project = settle_rows(
        seq_parts(tied(project, opening[-1]), first), [(0, part, 0, ())], [(deep, size, part, 3 * width)]
    )[0].reshape(width, 3 * width)
    query, keys, values, *kept = project_call(first, w_project, gains_full, ones)
    mixed, stat = attend_call(lengths, query, keys, values)
    second, act, slope, unit2, unit3, row_stat, pool = forward_call(lengths, embed, mixed, w_rest, gains_full)

    loss, d_head, d_pool = head_call(pool.reshape(8 * mb, width), *seq_columns, w_head)
    head_sum = lax.psum_scatter(d_head, ("fsdp", "seq"), scatter_dimension=0, tiled=True)

    dm, d_up, dr, d_mixed, delta, d_gain_rest = backward_call(
        lengths, d_pool.reshape(mb, 8, width), unit3, unit2, row_stat, slope, mixed, w_rest, gains_full, pick
    )
    d_rest = weight_call(act, dm, second, d_up)
    own_rest = lax.psum_scatter(d_rest, ("fsdp", "seq"), scatter_dimension=0, tiled=True)[0]

    pairs = HEADS // 2
    early = 4
    stats = jnp.stack([s[:, :, :HEADS].reshape(mb, ROWS, pairs, 2) for s in (stat, delta)], axis=3)
    stats = jnp.pad(stats.transpose(0, 2, 3, 4, 1).reshape(mb, pairs, 4, ROWS), ((0, 0), (0, 0), (0, 4), (0, 0)))
    stats = stats.reshape(mb, 8 * pairs, ROWS)

    def heads_back(after, start, count):
        out = attend_back_call(
            lengths, query, keys, values, d_mixed, kept, stats, gains_full, ones, start, count, after,
        )
        return out[:3], out[3]

    grads_one, gain_one = heads_back([d_rest], 0, early)
    mid_core = core_terms(*one_weight_call((mixed, dr), (first, *grads_one), first=[head_sum]))
    mid_x = Sum(mid_core, X)
    grads_two, gain_two = heads_back(mid_x.sent, early, pairs - early)
    mid_y = Sum(mid_x.after(grads_two[0]), Y)
    late_core = core_terms(*one_weight_call((first, *grads_two), first=mid_y.sent))
    late_x = Sum(late_core, X)
    mid_z = Sum(mid_y.after(late_core[0]), Z)
    d_embed, d_gain_first = first_call(
        (*grads_one, *grads_two), embed, dr, w_project, gains_full, [own_rest, *late_x.sent, *mid_z.sent]
    )
    late_y = Sum(late_x.after(d_embed), Y)
    own_mid = fold([x.astype(wide) for x in mid_z.after(d_embed)])
    d_gain_heads = jnp.concatenate([gain_one, gain_two], axis=0).transpose(1, 0, 2).reshape(8, width)
    d_gains = jnp.concatenate(
        [d_gain_first[:1], d_gain_heads[:2], d_gain_rest[3:5], jnp.zeros((123, width), wide)], axis=0
    ).T
    e_own, e_sent = embed_weight_call(patches, hot, d_embed, d_gains, [own_mid, *late_y.sent])
    head_sum = tied(head_sum, e_own) / weight_sum
    scalars = jnp.stack([weight_sum, jnp.sum(jnp.square(head_sum)), loss[0, 0]])
    left_part = pick_index(
        tied(left_roots, e_own).reshape(left_roots.shape[0], deep, size, part, width), me_s, 2
    )
    last_y = Sum(Sum(core_terms(e_own, e_sent), X).terms, Y)
    both_z = Sum(
        [jnp.concatenate([a.astype(wide), b.astype(wide)], axis=3) for a, b in zip(last_y.terms, late_y.terms)], Z
    )

    per = left_stats.shape[0]
    count = blocks.shape[0]
    own, *outgoing = collect_call(
        block_slot, scalars, own_rest, own_mid[0], both_z.terms, per,
        early * 2 * HEAD,
    )
    arrived = seq_parts(jnp.stack([swap(x, "fsdp", k) for k, x in enumerate(outgoing)]))
    slotted, notes, *directions = direction_call(left_part, right_roots, arrived)
    notes = jnp.sum(notes[:, :, :, 0].astype(wide), axis=(0, 1))
    loss_sum = notes[3] + notes[4] + notes[5]
    clip_norm = jnp.sqrt(notes[0] + notes[1] + notes[2])
    factor = jnp.minimum(1.0, clip_bound / clip_norm)
    back = select_call(block_slot, [swap(x, "fsdp", k) for k, x in enumerate(directions)])
    split = (count, size, part, width)
    block_grads, small_grad = finish_call(
        grads_kernel, factor, [], seq_parts(tied(own, slotted)), part, [split, (size, part // 3, width)]
    )
    blocks_new = finish_call(update_kernel, factor, [blocks.reshape(split)], seq_parts(back), part, [split])[0]
    blocks_new = blocks_new.reshape(blocks.shape)
    block_grads = block_grads.reshape(blocks.shape)
    slotted = tied(slotted, back)
    head_all = settled(
        seq_parts(tied(head_sum, back)),
        [(size, *head_sum.shape)],
        [(j, (), 0, lambda f, s, j=j: j ^ s) for j in range(size)],
    )[0].reshape(head.shape)
    gram_left = product("sij,skj->sik", slotted, slotted)
    gram_right = product("sji,sjk->sik", slotted, slotted)
    left_new = stat_decay * left_stats + ((1 - stat_decay) * factor * factor) * gram_left
    right_new = stat_decay * right_stats + ((1 - stat_decay) * factor * factor) * gram_right

    small_grad = jnp.concatenate([small_grad[:, :, i * 256 : (i + 1) * 256] for i in range(3)], axis=1)
    small_grad = small_grad.reshape(lanes, 256).T
    table_grad = small_grad[: 2 * grid_rows].reshape(2, grid_rows, lanes)
    gain_grad = small_grad[2 * grid_rows : 2 * grid_rows + 5]
    pos_new, pos_first_new, pos_second_new = adam(
        pos_table, table_grad, pos_first, pos_second, table_rate, decay_rate
    )
    gains_new, gain_first_new, gain_second_new = adam(gains, gain_grad, gain_first, gain_second, gain_rate, 0.0)
    head_new, head_first_new, head_second_new = adam(
        head, head_all * factor, head_first, head_second, adam_rate, decay_rate
    )
    return (
        blocks_new, block_grads, left_new, right_new, pos_new, pos_first_new, pos_second_new,
        gains_new, gain_first_new, gain_second_new, head_new, head_first_new, head_second_new,
        clip_norm, loss_sum, weight_sum,
    )


def solution(mesh):
    placed = (
        P(None, ("seq", "fsdp"), None, None),
        P(None, None, ("seq", "fsdp"), None),
        P(None, ("seq", "fsdp"), None),
        P(None, ("seq", "fsdp"), None),
        P(None, ("seq", "fsdp"), None),
        P(),
        P(None, "fsdp", None),
        P(None, None, "fsdp"),
        P(None, "fsdp"),
        P("fsdp", None),
        P("fsdp", None, None),
        P("fsdp", None, None),
        P("fsdp", None, None),
        P("fsdp", None, None),
        P(None, None, "fsdp"),
        P(None, None, "fsdp"),
        P(None, "fsdp"),
        P(None, "fsdp"),
        P("fsdp", None),
        P("fsdp", None),
    )
    return jax.shard_map(
        local,
        mesh=mesh,
        in_specs=placed,
        out_specs=(
            P(None, "fsdp", None),
            P(None, "fsdp", None),
            P("fsdp", None, None),
            P("fsdp", None, None),
            P(None, None, "fsdp"),
            P(None, None, "fsdp"),
            P(None, None, "fsdp"),
            P(None, "fsdp"),
            P(None, "fsdp"),
            P(None, "fsdp"),
            P("fsdp", None),
            P("fsdp", None),
            P("fsdp", None),
            P(),
            P(),
            P(),
        ),
        check_vma=False,
    )
```

```python
import functools
import math
import jax
import jax.numpy as jnp
from jax import lax
from jax.experimental import pallas as pl
from jax.experimental.pallas import tpu as pltpu
from jax.sharding import PartitionSpec as P

HEADS = 12
HEAD = 64
PACK = 1536
LONG = 1152
SHORT = 256
ROWS = LONG + SHORT
TILE = 352
STEP = 10
clip_bound = 0.01
stat_decay = 0.95
shampoo_rate = 0.1
decay_rate = 0.01
first_decay = 0.9
second_decay = 0.95
adam_rate = 0.04
table_rate = 0.5
gain_rate = 0.25
adam_eps = 1e-10
norm_eps = 1e-06
narrow = jnp.bfloat16
wide = jnp.float32
log2e = math.log2(math.e)
VM = 60 * 1024 * 1024
SMALL_VM = 20 * 1024 * 1024


def params(limit=VM):
    return pltpu.CompilerParams(vmem_limit_bytes=limit)


def dot(a, b, ca=1, cb=0):
    return lax.dot_general(a, b, (((ca,), (cb,)), ((), ())), preferred_element_type=wide)


def norm_rows(v):
    c = v - jnp.mean(v, axis=-1, keepdims=True)
    r = lax.rsqrt(jnp.mean(c * c, axis=-1, keepdims=True) + norm_eps)
    return c * r, r


def back_rows(unit, r, scaled):
    return r * (
        scaled
        - jnp.mean(scaled, axis=-1, keepdims=True)
        - unit * jnp.mean(scaled * unit, axis=-1, keepdims=True)
    )


def spec(shape, index):
    return pl.BlockSpec(shape, index)


def beside(kernel, inputs, count):
    return lambda *refs: kernel(*refs[:inputs], *refs[inputs + count :])


def anywhere(arrays):
    return [pl.BlockSpec(memory_space=pl.ANY)] * len(arrays)


def held(shape):
    return pl.BlockSpec(shape, lambda *_: (0,) * len(shape), pipeline_mode=pl.Buffered(1))


def cost(flops, moved, trans=0):
    return pl.CostEstimate(flops=int(flops), bytes_accessed=int(moved), transcendentals=int(trans))


def embed_kernel(patch_ref, hot_ref, e_ref, gain_ref, embed_ref, first_ref):
    width = embed_ref.shape[2]
    v = dot(patch_ref[0, 0], e_ref[:, :width]) + dot(hot_ref[0], e_ref[:, width : width + 128], 1, 1)
    embed_ref[0] = v
    unit, _ = norm_rows(v)
    first_ref[0] = (unit * gain_ref[0:1]).astype(narrow)


def embed_call(patches, hot, e, gains):
    mb, width = patches.shape[0], gains.shape[1]
    steps = ROWS // TILE
    return pl.pallas_call(
        embed_kernel,
        grid=(mb, steps),
        in_specs=[
            spec((1, 1, TILE, patches.shape[3]), lambda m, i: (m, 0, i, 0)),
            spec((1, TILE, hot.shape[2]), lambda m, i: (m, i, 0)),
            held(e.shape),
            held(gains.shape),
        ],
        out_specs=[spec((1, TILE, width), lambda m, i: (m, i, 0))] * 2,
        out_shape=[
            jax.ShapeDtypeStruct((mb, ROWS, width), wide),
            jax.ShapeDtypeStruct((mb, ROWS, width), narrow),
        ],
        compiler_params=params(),
        cost_estimate=cost(2 * mb * ROWS * width * 896, 20e6),
    )(patches, hot, e, gains)


def group_mean(v, ones):
    return jnp.concatenate(
        [dot(v[:, at : at + 256].astype(narrow), ones) for at in range(0, v.shape[1], 256)], axis=1
    )


def project_kernel(first_ref, w_ref, gain_ref, ones_ref, q_ref, k_ref, v_ref, *kept):
    x = first_ref[0]
    width = x.shape[1]
    ones = ones_ref[...]
    for i, ref in enumerate((q_ref, k_ref)):
        raw = dot(x, w_ref[:, i * width : (i + 1) * width])
        c = raw - group_mean(raw, ones)
        r = lax.rsqrt(group_mean(c * c, ones) + norm_eps)
        unit = c * r
        kept[i][0] = unit.astype(narrow)
        kept[2 + i][0] = r.astype(narrow)
        out = (unit * gain_ref[1 + i : 2 + i]).astype(narrow)
        if i == 0:
            out = out * narrow(HEAD**-0.5)
        ref[0] = out
    v_ref[0] = dot(x, w_ref[:, 2 * width :]).astype(narrow)


def project_call(first, w, gains, ones):
    mb, _, width = first.shape
    rows = spec((1, TILE, width), lambda m, i: (m, i, 0))
    return pl.pallas_call(
        project_kernel,
        grid=(mb, ROWS // TILE),
        in_specs=[rows, held(w.shape), held(gains.shape), held(ones.shape)],
        out_specs=[rows] * 7,
        out_shape=[jax.ShapeDtypeStruct((mb, ROWS, width), narrow)] * 7,
        compiler_params=params(),
        cost_estimate=cost(2 * mb * ROWS * width * width * 3, 30e6),
    )(first, w, gains, ones)


ROWS_Q = 384


def attend_kernel(lengths_ref, q_ref, k_ref, v_ref, mixed_ref, stat_ref):
    pack, pair = pl.program_id(0), pl.program_id(1)
    lane = lax.broadcasted_iota(jnp.int32, (1, 2 * HEAD), 1)

    def part(start, count, tile, masked):
        k = k_ref[0, start : start + count]
        v = v_ref[0, start : start + count]
        zero = jnp.zeros_like(k)
        one = jnp.ones_like(k)
        k_both = [jnp.where(lane < HEAD, k, zero), jnp.where(lane < HEAD, zero, k)]
        ext = jnp.concatenate(
            [
                jnp.concatenate([jnp.where(lane < HEAD, v, zero), jnp.where(lane < HEAD, one, zero)], axis=1),
                jnp.concatenate([jnp.where(lane < HEAD, zero, v), jnp.where(lane < HEAD, zero, one)], axis=1),
            ],
            axis=0,
        )
        for at in range(start, start + count, tile):
            q = q_ref[0, at : at + tile]
            expos, peaks = [], []
            for h in range(2):
                s = dot(q, k_both[h], 1, 1)
                if masked:
                    limit = lengths_ref[pack, 1]
                    row = lax.broadcasted_iota(jnp.int32, s.shape, 0) + (at - start)
                    col = lax.broadcasted_iota(jnp.int32, s.shape, 1)
                    s = jnp.where((row < limit) == (col < limit), s, -1e30)
                peak = jnp.max(s, axis=1, keepdims=True)
                expos.append(jnp.exp2(s * log2e - peak * log2e).astype(narrow))
                peaks.append(peak)
            both = dot(jnp.concatenate(expos, axis=1), ext)
            total = both[:, 2 * HEAD :]
            mixed_ref[0, at : at + tile] = (both[:, : 2 * HEAD] / total).astype(narrow)
            lse = (jnp.where(lane < HEAD, peaks[0], peaks[1]) + jnp.log(total)) * log2e
            for h in range(2):
                column = jnp.sum(jnp.where(lane == h * HEAD, lse, 0.0), axis=1, keepdims=True)
                old = stat_ref[0, at : at + tile]
                stat_ref[0, at : at + tile] = jnp.where(lane == 2 * pair + h, column, old)

    part(0, LONG, ROWS_Q, False)
    part(LONG, SHORT, SHORT, True)


def attend_call(lengths, q, k, v):
    mb, _, width = q.shape
    block = pl.BlockSpec((1, ROWS, 2 * HEAD), lambda m, p, *_: (m, 0, p))
    pairs = width // (2 * HEAD)
    moved = mb * ROWS * width * 8
    return pl.pallas_call(
        attend_kernel,
        grid_spec=pltpu.PrefetchScalarGridSpec(
            num_scalar_prefetch=1,
            grid=(mb, pairs),
            in_specs=[block] * 3,
            out_specs=[block, pl.BlockSpec((1, ROWS, 128), lambda m, p, *_: (m, 0, 0))],
        ),
        out_shape=[
            jax.ShapeDtypeStruct((mb, ROWS, width), narrow),
            jax.ShapeDtypeStruct((mb, ROWS, 128), wide),
        ],
        compiler_params=params(),
        cost_estimate=cost(16 * mb * 2 * pairs * (LONG**2 + SHORT**2) * HEAD, moved),
    )(lengths, q, k, v)


def cdf_and_slope(up):
    cdf = 0.5 + 0.5 * lax.erf(up * 0.7071067811865476)
    slope = cdf + up * (jnp.exp2(up * up * (-0.5 * log2e)) * 0.3989422804014327)
    return cdf, slope


def forward_kernel(
    lengths_ref, embed_ref, mixed_ref, w_ref, gain_ref,
    second_ref, act_ref, slope_ref, unit2_ref, unit3_ref, stat_ref, pool_ref,
):
    pack, step = pl.program_id(0), pl.program_id(1)
    width = embed_ref.shape[2]
    resid = embed_ref[0] + dot(mixed_ref[0], w_ref[0])
    unit, r2 = norm_rows(resid)
    unit2_ref[0] = unit.astype(narrow)
    second = (unit * gain_ref[3:4]).astype(narrow)
    second_ref[0] = second
    outcome = resid
    for j in range(4):
        up = dot(second, w_ref[1 + j])
        cdf, slope = cdf_and_slope(up)
        act = (up * cdf).astype(narrow)
        act_ref[j, 0] = act
        slope_ref[j, 0] = slope.astype(narrow)
        outcome = outcome + dot(act, w_ref[5 + j])
    unit, r3 = norm_rows(outcome)
    unit3_ref[0] = unit.astype(narrow)
    lane = lax.broadcasted_iota(jnp.int32, (1, 128), 1)
    stat_ref[0] = jnp.where(lane == 0, r2, r3)
    final = unit * gain_ref[4:5]

    @pl.when(step == 0)
    def _():
        pool_ref[...] = jnp.zeros_like(pool_ref)

    row = lax.broadcasted_iota(jnp.int32, (TILE, 1), 0) + step * TILE
    first_len, second_len = lengths_ref[pack, 0], lengths_ref[pack, 1]
    inside = (row < first_len, (row >= first_len) & (row < first_len + second_len))
    for s in range(2):
        total = jnp.sum(jnp.where(inside[s], final, 0.0), axis=0, keepdims=True)
        pool_ref[0, s : s + 1] += total


def forward_call(lengths, embed, mixed, w, gains):
    mb, _, width = embed.shape
    rows = pl.BlockSpec((1, TILE, width), lambda m, i, *_: (m, i, 0))
    wider = pl.BlockSpec((4, 1, TILE, width), lambda m, i, *_: (0, m, i, 0))
    return pl.pallas_call(
        forward_kernel,
        grid_spec=pltpu.PrefetchScalarGridSpec(
            num_scalar_prefetch=1,
            grid=(mb, ROWS // TILE),
            in_specs=[rows, rows, held(w.shape), held(gains.shape)],
            out_specs=[
                rows, wider, wider, rows, rows,
                pl.BlockSpec((1, TILE, 128), lambda m, i, *_: (m, i, 0)),
                pl.BlockSpec((1, 8, width), lambda m, i, *_: (m, 0, 0)),
            ],
        ),
        out_shape=[
            jax.ShapeDtypeStruct((mb, ROWS, width), narrow),
            jax.ShapeDtypeStruct((4, mb, ROWS, width), narrow),
            jax.ShapeDtypeStruct((4, mb, ROWS, width), narrow),
            jax.ShapeDtypeStruct((mb, ROWS, width), narrow),
            jax.ShapeDtypeStruct((mb, ROWS, width), narrow),
            jax.ShapeDtypeStruct((mb, ROWS, 128), wide),
            jax.ShapeDtypeStruct((mb, 8, width), wide),
        ],
        compiler_params=params(),
        cost_estimate=cost(2 * mb * ROWS * width * width * 9, 80e6),
    )(lengths, embed, mixed, w, gains)


def head_kernel(pool_ref, scale_ref, weight_ref, label_ref, head_ref, loss_ref, dhead_ref, dpool_ref):
    pooled = (pool_ref[...] * scale_ref[:, 0:1]).astype(narrow)
    logits = dot(pooled, head_ref[...])
    peak = jnp.max(logits, axis=1, keepdims=True)
    expo = jnp.exp(logits - peak)
    total = jnp.sum(expo, axis=1, keepdims=True)
    hot = lax.broadcasted_iota(jnp.int32, logits.shape, 1) == label_ref[:, 0:1]
    picked = jnp.sum(jnp.where(hot, logits, 0.0), axis=1, keepdims=True)
    weight = weight_ref[:, 0:1].astype(wide)
    loss = jnp.where(weight > 0, weight * (peak + jnp.log(total) - picked), 0.0)
    loss_ref[...] = jnp.broadcast_to(jnp.sum(loss, axis=0, keepdims=True), loss_ref.shape)
    dlogits = (weight * (expo / total - hot.astype(wide))).astype(narrow)
    dhead_ref[...] = dot(pooled, dlogits, 0, 0).astype(dhead_ref.dtype)
    dpool_ref[...] = dot(dlogits, head_ref[...], 1, 1) * scale_ref[:, 0:1]


def head_call(pool, scale, weight, label, head, out=wide):
    rows, width = pool.shape
    return pl.pallas_call(
        head_kernel,
        out_shape=[
            jax.ShapeDtypeStruct((8, 128), wide),
            jax.ShapeDtypeStruct(head.shape, out),
            jax.ShapeDtypeStruct((rows, width), wide),
        ],
        compiler_params=params(),
        cost_estimate=cost(6 * rows * width * 1000, 8e6),
    )(pool, scale, weight, label, head)


def backward_kernel(
    lengths_ref, dpool_ref, unit3_ref, unit2_ref, stat_ref, slope_ref, mixed_ref, w_ref, gain_ref, pick_ref,
    dm_ref, dup_ref, dr_ref, dmixed_ref, delta_ref, dgain_ref,
):
    pack, step = pl.program_id(0), pl.program_id(1)
    row = lax.broadcasted_iota(jnp.int32, (TILE, 1), 0) + step * TILE
    first_len, second_len = lengths_ref[pack, 0], lengths_ref[pack, 1]
    dfinal = jnp.where(
        row < first_len,
        dpool_ref[0, 0:1],
        jnp.where(row < first_len + second_len, dpool_ref[0, 1:2], 0.0),
    )
    unit3 = unit3_ref[0].astype(wide)
    r2, r3 = stat_ref[0, :, 0:1], stat_ref[0, :, 1:2]
    doutcome = back_rows(unit3, r3, dfinal * gain_ref[4:5])
    dgf = jnp.sum(dfinal * unit3, axis=0, keepdims=True)
    dm = doutcome.astype(narrow)
    dm_ref[0] = dm
    dsecond = None
    for j in range(4):
        dact = dot(dm, w_ref[5 + j], 1, 1)
        dup = (dact * slope_ref[j, 0].astype(wide)).astype(narrow)
        dup_ref[j, 0] = dup
        term = dot(dup, w_ref[1 + j], 1, 1)
        dsecond = term if dsecond is None else dsecond + term
    unit2 = unit2_ref[0].astype(wide)
    dg2 = jnp.sum(dsecond * unit2, axis=0, keepdims=True)
    dresid = doutcome + back_rows(unit2, r2, dsecond * gain_ref[3:4])
    dr = dresid.astype(narrow)
    dr_ref[0] = dr
    dmixed = dot(dr, w_ref[0], 1, 1).astype(narrow)
    dmixed_ref[0] = dmixed
    delta_ref[0] = dot(dmixed * mixed_ref[0], pick_ref[...])

    @pl.when((pack == 0) & (step == 0))
    def _():
        dgain_ref[...] = jnp.zeros_like(dgain_ref)

    dgain_ref[3:4] += dg2
    dgain_ref[4:5] += dgf


def backward_call(lengths, dpool, unit3, unit2, stat, slope, mixed, w, gains, pick):
    mb, _, width = unit3.shape
    rows = pl.BlockSpec((1, TILE, width), lambda m, i, *_: (m, i, 0))
    lanes = pl.BlockSpec((1, TILE, 128), lambda m, i, *_: (m, i, 0))
    wider = pl.BlockSpec((4, 1, TILE, width), lambda m, i, *_: (0, m, i, 0))
    return pl.pallas_call(
        backward_kernel,
        grid_spec=pltpu.PrefetchScalarGridSpec(
            num_scalar_prefetch=1,
            grid=(mb, ROWS // TILE),
            in_specs=[
                pl.BlockSpec((1, 8, width), lambda m, i, *_: (m, 0, 0)),
                rows, rows, lanes, wider, rows,
                held(w.shape), held(gains.shape), held(pick.shape),
            ],
            out_specs=[rows, wider, rows, rows, lanes, pl.BlockSpec((8, width), lambda m, i, *_: (0, 0))],
        ),
        out_shape=[
            jax.ShapeDtypeStruct((mb, ROWS, width), narrow),
            jax.ShapeDtypeStruct((4, mb, ROWS, width), narrow),
            jax.ShapeDtypeStruct((mb, ROWS, width), narrow),
            jax.ShapeDtypeStruct((mb, ROWS, width), narrow),
            jax.ShapeDtypeStruct((mb, ROWS, 128), wide),
            jax.ShapeDtypeStruct((8, width), wide),
        ],
        compiler_params=params(),
        cost_estimate=cost(2 * mb * ROWS * width * width * 9, 70e6),
    )(lengths, dpool, unit3, unit2, stat, slope, mixed, w, gains, pick)


def attend_back_kernel(
    lengths_ref, q_ref, k_ref, v_ref, do_ref, qunit_ref, kunit_ref, qr_ref, kr_ref, stat_ref, gain_ref, ones_ref,
    dq_ref, dk_ref, dv_ref, dgain_ref, dq_acc, dk_acc, dv_acc,
):
    pack = pl.program_id(1)
    lane = lax.broadcasted_iota(jnp.int32, (1, 2 * HEAD), 1)

    def both(x, axis=0):
        zero = jnp.zeros_like(x)
        return jnp.concatenate([jnp.where(lane < HEAD, x, zero), jnp.where(lane < HEAD, zero, x)], axis=axis)

    def part(start, count, tile, chunk, masked):
        for ti in range(start, start + count, tile):
            q2 = both(q_ref[0, ti : ti + tile])
            do2 = both(do_ref[0, ti : ti + tile])
            lse = jnp.concatenate([stat_ref[0, h : h + 1, ti : ti + tile] for h in (0, 1)], axis=1)
            delta = jnp.concatenate([stat_ref[0, h : h + 1, ti : ti + tile] for h in (2, 3)], axis=1)
            for ui in range(start, start + count, chunk):
                k = k_ref[0, ui : ui + chunk]
                v = v_ref[0, ui : ui + chunk]
                s = dot(k, q2, 1, 1)
                p = jnp.exp2(s * log2e - lse)
                if masked:
                    limit = lengths_ref[pack, 1]
                    row = lax.broadcasted_iota(jnp.int32, s.shape, 0) + (ui - start)
                    col = lax.broadcasted_iota(jnp.int32, s.shape, 1)
                    col = jnp.where(col < tile, col, col - tile) + (ti - start)
                    p = jnp.where((row < limit) == (col < limit), p, 0.0)
                dp = dot(v, do2, 1, 1)
                ds = (p * (dp - delta)).astype(narrow)
                dv_new = dot(p.astype(narrow), do2)
                dk_new = dot(ds, q2)
                k2 = both(k)
                ds_rows = jnp.concatenate([ds[:, :tile], ds[:, tile:]], axis=0)
                dq_new = dot(ds_rows, k2, 0, 0)
                if ti == start:
                    dv_acc[ui : ui + chunk] = dv_new
                    dk_acc[ui : ui + chunk] = dk_new
                else:
                    dv_acc[ui : ui + chunk] += dv_new
                    dk_acc[ui : ui + chunk] += dk_new
                if ui == start:
                    dq_acc[ti : ti + tile] = dq_new
                else:
                    dq_acc[ti : ti + tile] += dq_new

    part(0, LONG, 384, 384, False)
    part(LONG, SHORT, SHORT, SHORT, True)
    dv_ref[0] = dv_acc[...].astype(narrow)
    ones = ones_ref[...]

    def mean(x):
        return dot(x.astype(narrow), ones)

    @pl.when(pack == 0)
    def _():
        dgain_ref[...] = jnp.zeros_like(dgain_ref)

    for i, (acc, unit_ref, r_ref, ref, factor) in enumerate(
        ((dq_acc, qunit_ref, qr_ref, dq_ref, HEAD**-0.5), (dk_acc, kunit_ref, kr_ref, dk_ref, 1.0))
    ):
        unit, r = unit_ref[0].astype(wide), r_ref[0].astype(wide)
        dy = acc[...] * factor
        dgain_ref[0, i : i + 1] += jnp.sum(dy * unit, axis=0, keepdims=True)
        scaled = dy * gain_ref[1 + i : 2 + i]
        ref[0] = (r * (scaled - mean(scaled) - unit * mean(scaled * unit))).astype(narrow)


def attend_back_call(lengths, q, k, v, do, kept, stat, gains, ones, first_pair, pairs, first=()):
    mb, _, width = q.shape
    block = pl.BlockSpec((1, ROWS, 2 * HEAD), lambda p, m, *_: (m, 0, p + first_pair))
    out = pl.BlockSpec((1, ROWS, 2 * HEAD), lambda p, m, *_: (m, 0, p))
    shape = jax.ShapeDtypeStruct((mb, ROWS, pairs * 2 * HEAD), narrow)
    return pl.pallas_call(
        beside(attend_back_kernel, 12, len(first)),
        grid_spec=pltpu.PrefetchScalarGridSpec(
            num_scalar_prefetch=1,
            grid=(pairs, mb),
            in_specs=[
                *[block] * 8,
                pl.BlockSpec((1, 8, ROWS), lambda p, m, *_: (m, p + first_pair, 0)),
                pl.BlockSpec((8, 2 * HEAD), lambda p, m, *_: (0, p + first_pair)),
                pl.BlockSpec((2 * HEAD, 2 * HEAD), lambda p, m, *_: (0, 0)),
                *anywhere(first),
            ],
            out_specs=[out, out, out, pl.BlockSpec((1, 8, 2 * HEAD), lambda p, m, *_: (p, 0, 0))],
            scratch_shapes=[pltpu.VMEM((ROWS, 2 * HEAD), wide)] * 3,
        ),
        out_shape=[shape, shape, shape, jax.ShapeDtypeStruct((pairs, 8, 2 * HEAD), wide)],
        compiler_params=params(),
        cost_estimate=cost(20 * mb * 2 * pairs * (LONG**2 + SHORT**2) * HEAD * 2, mb * ROWS * pairs * 128 * 18),
    )(lengths, q, k, v, do, *kept, stat, gains, ones, *first)


def first_kernel(*refs, parts):
    grads = refs[: 3 * parts]
    embed_ref, dr_ref, w_ref, gain_ref, out_ref, dgain_ref = refs[3 * parts :]
    step = pl.program_id(0) * pl.num_programs(1) + pl.program_id(1)
    width = embed_ref.shape[2]
    total = None
    for i in range(3):
        rows = jnp.concatenate([grads[3 * p + i][0] for p in range(parts)], axis=1)
        term = dot(rows, w_ref[:, i * width : (i + 1) * width], 1, 1)
        total = term if total is None else total + term
    unit, r = norm_rows(embed_ref[0])

    @pl.when(step == 0)
    def _():
        dgain_ref[...] = jnp.zeros_like(dgain_ref)

    dgain_ref[0:1] += jnp.sum(total * unit, axis=0, keepdims=True)
    out_ref[0] = (dr_ref[0].astype(wide) + back_rows(unit, r, total * gain_ref[0:1])).astype(narrow)


def first_call(grads, embed, dr, w, gains, first=()):
    mb, _, width = embed.shape
    rows = spec((1, TILE, width), lambda m, i: (m, i, 0))
    parts = len(grads) // 3
    return pl.pallas_call(
        beside(functools.partial(first_kernel, parts=parts), len(grads) + 4, len(first)),
        grid=(mb, ROWS // TILE),
        in_specs=[spec((1, TILE, g.shape[2]), lambda m, i: (m, i, 0)) for g in grads]
        + [rows, rows, held(w.shape), held(gains.shape)]
        + anywhere(first),
        out_specs=[rows, spec((8, width), lambda m, i: (0, 0))],
        out_shape=[
            jax.ShapeDtypeStruct((mb, ROWS, width), narrow),
            jax.ShapeDtypeStruct((8, width), wide),
        ],
        compiler_params=params(),
        cost_estimate=cost(2 * mb * ROWS * width * width * 3, 32e6),
    )(*grads, embed, dr, w, gains, *first)


def split_rows(value, own_ref, sent_ref, me, n):
    across, up, deep = own_ref.shape[:3]
    part = own_ref.shape[4]
    for x in range(across):
        for y in range(up):
            for z in range(deep):
                at = ((z * up + y) * across + x) * 2 * part
                first = value[at : at + part].astype(narrow)
                second = value[at + part : at + 2 * part].astype(narrow)
                own_ref[x, y, z, n] = jnp.where(me == 0, first, second)
                sent_ref[x, y, z, n] = jnp.where(me == 0, second, first)


def flat_rows(ref):
    return ref[...].reshape(-1, ref.shape[-1])


def weight_kernel(act_ref, dm_ref, second_ref, dup_ref, mixed_ref, dr_ref, out_ref):
    step = pl.program_id(0)

    def write(a_ref, b_ref):
        value = dot(flat_rows(a_ref), flat_rows(b_ref), 0, 0)
        part = out_ref.shape[2]
        for to in range(out_ref.shape[0]):
            out_ref[to, 0] = value[to * part : (to + 1) * part].astype(narrow)

    pl.when(step == 0)(lambda: write(mixed_ref, dr_ref))
    pl.when((step >= 1) & (step < 5))(lambda: write(second_ref, dup_ref))
    pl.when(step >= 5)(lambda: write(act_ref, dm_ref))


def split_shape(rows):
    core, x, y, z = (level[2] for level in levels())
    return (x, y, z), rows // (core * x * y * z)


def core_at():
    return (lax.axis_index("seq") % 2).reshape(1).astype(jnp.int32)


def weight_call(act, dm, second, dup, mixed, dr):
    width = dm.shape[2]
    parts = lax.axis_size("fsdp") * lax.axis_size("seq")
    rows = held(dm.shape)
    one = (1, *dm.shape)
    return pl.pallas_call(
        weight_kernel,
        grid=(9,),
        in_specs=[
            spec(one, lambda i: (jnp.maximum(i - 5, 0), 0, 0, 0)),
            rows,
            rows,
            spec(one, lambda i: (jnp.clip(i - 1, 0, 3), 0, 0, 0)),
            rows,
            rows,
        ],
        out_specs=spec((parts, 1, width // parts, width), lambda i: (0, i, 0, 0)),
        out_shape=jax.ShapeDtypeStruct((parts, 9, width // parts, width), narrow),
        compiler_params=params(),
        cost_estimate=cost(2 * 9 * dm.size * width, 70e6),
    )(act, dm, second, dup, mixed, dr)


def one_weight_kernel(at_ref, *refs, groups):
    count = len(groups) + sum(groups)
    own_ref, sent_ref, total = refs[count:]
    step = pl.program_id(0)
    last = step == pl.num_programs(0) - 1
    at, ref = 0, 0
    for members in groups:
        a = refs[ref][0]
        for b_ref in refs[ref + 1 : ref + 1 + members]:
            lanes = pl.ds(at, b_ref.shape[-1])
            at += b_ref.shape[-1]
            value = dot(a, b_ref[0], 0, 0)

            @pl.when(step == 0)
            def _(value=value, lanes=lanes):
                total[:, lanes] = value

            @pl.when((step > 0) & ~last)
            def _(value=value, lanes=lanes):
                total[:, lanes] += value

            @pl.when(last)
            def _(value=value, lanes=lanes):
                split_rows(total[:, lanes] + value, own_ref.at[..., lanes], sent_ref.at[..., lanes], at_ref[0], 0)

        ref += 1 + members


def one_weight_call(*groups, first=()):
    arrays = [array for group in groups for array in group]
    mb, rows, depth = arrays[0].shape
    width = sum(x.shape[-1] for group in groups for x in group[1:])
    (x, y, z), part = split_shape(depth)
    shape = (x, y, z, 1, part, width)
    out = pl.BlockSpec(shape, lambda m, *_: (0,) * 6)
    return pl.pallas_call(
        beside(
            functools.partial(one_weight_kernel, groups=[len(group) - 1 for group in groups]),
            1 + len(arrays),
            len(first),
        ),
        grid_spec=pltpu.PrefetchScalarGridSpec(
            num_scalar_prefetch=1,
            grid=(mb,),
            in_specs=[pl.BlockSpec((1, *v.shape[1:]), lambda m, *_: (m, 0, 0)) for v in arrays]
            + anywhere(first),
            out_specs=[out] * 2,
            scratch_shapes=[pltpu.VMEM((depth, width), wide)],
        ),
        out_shape=[jax.ShapeDtypeStruct(shape, narrow)] * 2,
        compiler_params=params(),
        cost_estimate=cost(2 * mb * rows * depth * width, 12e6),
    )(core_at(), *arrays, *first)


def embed_weight_kernel(at_ref, patch_ref, hot_ref, grad_ref, gain_ref, own_ref, sent_ref, total):
    step = pl.program_id(0)
    grad = grad_ref[0]
    width = grad.shape[1]
    value = dot(patch_ref[0, 0], grad, 0, 0)
    table = dot(grad, hot_ref[0], 0, 0)

    @pl.when(step == 0)
    def _():
        total[:, :width] = value
        total[:, width : width + 128] = table

    @pl.when(step > 0)
    def _():
        total[:, :width] += value
        total[:, width : width + 128] += table

    @pl.when(step == pl.num_programs(0) - 1)
    def _():
        total[:, width + 128 :] = gain_ref[...]
        split_rows(total[...], own_ref, sent_ref, at_ref[0], 0)


def embed_weight_call(patches, hot, grad, gain_columns, first=()):
    mb, _, width = grad.shape
    pixels = patches.shape[3]
    (x, y, z), part = split_shape(pixels)
    shape = (x, y, z, 1, part, width + 256)
    out = pl.BlockSpec(shape, lambda m, *_: (0,) * 6)
    return pl.pallas_call(
        beside(embed_weight_kernel, 5, len(first)),
        grid_spec=pltpu.PrefetchScalarGridSpec(
            num_scalar_prefetch=1,
            grid=(mb,),
            in_specs=[
                pl.BlockSpec((1, 1, ROWS, pixels), lambda m, *_: (m, 0, 0, 0)),
                pl.BlockSpec((1, ROWS, hot.shape[2]), lambda m, *_: (m, 0, 0)),
                pl.BlockSpec((1, ROWS, width), lambda m, *_: (m, 0, 0)),
                pl.BlockSpec((width, 128), lambda m, *_: (0, 0)),
                *anywhere(first),
            ],
            out_specs=[out, out],
            scratch_shapes=[pltpu.VMEM((pixels, width + 256), wide)],
        ),
        out_shape=[jax.ShapeDtypeStruct(shape, narrow)] * 2,
        compiler_params=params(),
        cost_estimate=cost(2 * grad.size * (pixels + 128), 12e6),
    )(core_at(), patches, hot, grad, gain_columns, *first)


def fold(parts):
    while len(parts) > 1:
        parts = [parts[i] + parts[i + 1] for i in range(0, len(parts), 2)]
    return parts[0]


def swap(x, axis, bits):
    if bits == 0:
        return x
    return lax.ppermute(x, axis, [(i, i ^ bits) for i in range(lax.axis_size(axis))])


def tied(x, *after):
    return lax.optimization_barrier((x, *after))[0]


def pick_index(x, index, dim):
    return lax.dynamic_index_in_dim(x, index, dim, keepdims=False)


def levels():
    across, deep = lax.axis_size("seq"), lax.axis_size("fsdp")
    y = 1 << ((deep.bit_length() - 1) // 2)
    return (("seq", 1, 2), ("seq", 2, across // 2), ("fsdp", 1, y), ("fsdp", y, deep // y))


CORE, X, Y, Z = range(4)


class Sum:
    def __init__(self, terms, which):
        axis, stride, size = levels()[which]
        at = lax.axis_index(axis) // stride % size

        def part(k):
            return fold([pick_index(term, at ^ k, 0).astype(wide) for term in terms])

        self.sent = [part(k).astype(narrow) for k in range(1, size)]
        self.terms = [part(0)] + [swap(x, axis, (k + 1) * stride) for k, x in enumerate(self.sent)]

    def after(self, *others):
        return [tied(self.terms[0], *others), *self.terms[1:]]

    def total(self):
        return fold([term.astype(wide) for term in self.terms])


def core_terms(own, sent):
    return [own, swap(sent, "seq", 1)]


def settle_kernel(at_ref, *refs, count, moves):
    sources, outs = refs[:count], refs[count:]
    for source, index, out, target in moves:
        outs[out][target(at_ref[0], at_ref[1])] = sources[source][index]


def mesh_at():
    return jnp.stack([lax.axis_index("fsdp"), lax.axis_index("seq")]).astype(jnp.int32)


def in_vmem(count):
    return [pl.BlockSpec(memory_space=pltpu.VMEM)] * count


def settled(parts, shapes, moves, first=()):
    size = sum(part.size for part in parts) * parts[0].dtype.itemsize
    return pl.pallas_call(
        beside(functools.partial(settle_kernel, count=len(parts), moves=moves), 1 + len(parts), len(first)),
        in_specs=[pl.BlockSpec(memory_space=pltpu.SMEM)] + in_vmem(len(parts)) + anywhere(first),
        out_specs=in_vmem(len(shapes)),
        out_shape=[jax.ShapeDtypeStruct(shape, parts[0].dtype) for shape in shapes],
        compiler_params=params(),
        cost_estimate=cost(0, 2 * size),
    )(mesh_at(), *parts, *first)


def seq_parts(x, *after):
    half = [swap(x, "seq", k) for k in range(0, lax.axis_size("seq"), 2)]
    if after:
        half = [half[0]] + [tied(y, *after) for y in half[1:]]
    return [part for y in half for part in (y, swap(y, "seq", 1))]


def settle_rows(parts, cuts, shapes):
    deep = parts[0].shape[0]
    moves = [
        (j, (k, slice(start, stop)), out, lambda f, s, j=j, k=k, index=index: (*index, k ^ f, j ^ s))
        for j in range(len(parts))
        for k in range(deep)
        for start, stop, out, index in cuts
    ]
    return settled(parts, shapes, moves)


def near_exchange(x):
    return jnp.stack([swap(x, "fsdp", k) for k in range(levels()[Y][2])])


def far_exchange(x):
    _, stride, far = levels()[Z]
    return [swap(x, "fsdp", k * stride) for k in range(far)]


def stacked(parts):
    return jnp.stack(parts).reshape(-1, *parts[0].shape[1:])


def my_rows(x):
    size = lax.axis_size("seq")
    return pick_index(x.reshape(x.shape[0], size, x.shape[1] // size, x.shape[2]), lax.axis_index("seq"), 1)


def grads_kernel(at_ref, factor_ref, *refs, count, part):
    parts, (out_ref, small_ref) = refs[:count], refs[count:]
    factor = factor_ref[0]
    for j, ref in enumerate(parts):
        to = at_ref[1] ^ j
        for b in range(out_ref.shape[0]):
            out_ref[b, to] = ref[b * part : (b + 1) * part].astype(wide) * factor
        small_ref[to] = ref[out_ref.shape[0] * part :].astype(wide) * factor


def collect_kernel(at_ref, slot_ref, scalar_ref, rest_ref, *refs, count, deep, per, columns):
    terms, (own_ref, *out_refs) = refs[:count], refs[count : count + 1 + deep]
    blocks = refs[-1]
    part, width = rest_ref.shape[1:]
    scale = 1.0 / scalar_ref[0]
    both = fold([ref[0].astype(wide) for ref in terms])
    remain = width - columns
    late, mid = both[:, width + 256 : width + 256 + 3 * remain], both[:, width + 256 + 3 * remain :]
    pieces = [both[:, :width]]
    for i in range(3):
        first = mid[:, i * columns : (i + 1) * columns]
        pieces.append(jnp.concatenate([first, late[:, i * remain : (i + 1) * remain]], axis=1))
    pieces += [rest_ref[i].astype(wide) for i in range(rest_ref.shape[0])]
    squares = jnp.zeros((1, 1), wide)
    total = jnp.zeros((part, width), wide)
    for b, piece in enumerate(pieces):
        piece = (piece * scale).astype(narrow)
        blocks[b] = piece
        own_ref[b * part : (b + 1) * part] = piece
        total += jnp.square(piece.astype(wide))
    small = (both[:, width : width + 256] * scale).astype(narrow)
    third = part // 3
    small = small.astype(wide)
    squares = jnp.sum(total, keepdims=True) + jnp.sum(jnp.square(small), keepdims=True) + scalar_ref[1]
    small = jnp.concatenate([small[i * third : (i + 1) * third] for i in range(3)], axis=1)
    own_ref[len(pieces) * part :] = small.astype(narrow)
    row = lax.broadcasted_iota(jnp.int32, (8, width), 0)
    notes = jnp.zeros((8, width), wide)
    for at, value in ((0, squares), (3, jnp.full((1, 1), scalar_ref[2]))):
        for i in range(3):
            piece = value.astype(narrow).astype(wide)
            value = value - piece
            notes = jnp.where(row == at + i, piece, notes)
    notes = notes.astype(narrow)
    blocks[len(pieces)] = jnp.zeros((part, width), narrow)
    for k, out_ref in enumerate(out_refs):
        for i in range(per):
            slot = (at_ref[0] ^ k) * per + i
            found = len(pieces)
            for b in range(len(pieces)):
                found = jnp.where(slot_ref[b] == slot, b, found)
            out_ref[i * part : (i + 1) * part] = blocks[found]
        out_ref[per * part :] = notes


def collect_call(block_slot, scalars, rest, terms, per, columns, first):
    part, width = rest.shape[1:]
    deep = lax.axis_size("fsdp")
    count = block_slot.shape[0]
    smem = pl.BlockSpec(memory_space=pltpu.SMEM)
    message = jax.ShapeDtypeStruct((per * part + 8, width), narrow)
    return pl.pallas_call(
        beside(
            functools.partial(collect_kernel, count=len(terms), deep=deep, per=per, columns=columns),
            4 + len(terms),
            len(first),
        ),
        in_specs=[smem, smem, smem] + in_vmem(1 + len(terms)) + anywhere(first),
        out_specs=in_vmem(1 + deep),
        out_shape=[jax.ShapeDtypeStruct((count * part + part // 3, width), narrow)] + [message] * deep,
        scratch_shapes=[pltpu.VMEM((count + 1, part, width), narrow)],
        compiler_params=params(),
        cost_estimate=cost(0, 4e6),
    )(mesh_at(), block_slot, scalars, rest, *terms, *first)


def direction_kernel(at_ref, left_ref, right_ref, *refs, count, deep):
    parts, slotted_ref, notes_ref = refs[:count], refs[count], refs[count + 1]
    out_ref, rows = refs[count + 2 :]
    per, _, part, width = left_ref.shape
    for j, ref in enumerate(parts):
        for k in range(deep):
            f, s = at_ref[0] ^ k, at_ref[1] ^ j
            for i in range(per):
                rows[i, f * count + s] = ref[k, i * part : (i + 1) * part].astype(wide)
            notes_ref[f, s] = ref[k, per * part :]
    for i in range(per):
        grad = rows[i].reshape(deep * count * part, width).astype(narrow)
        slotted_ref[i] = grad
        inner = dot(left_ref[i].astype(wide).reshape(deep * part, width).astype(narrow), grad)
        value = dot(inner.astype(narrow), right_ref[i])
        out_ref[:, i] = value.reshape(deep, part, width).astype(narrow)


def direction_call(left, right, parts):
    per, deep, part, width = left.shape
    count = len(parts)
    return pl.pallas_call(
        functools.partial(direction_kernel, count=count, deep=deep),
        in_specs=[pl.BlockSpec(memory_space=pltpu.SMEM)] + in_vmem(2 + count),
        out_specs=in_vmem(3),
        out_shape=[
            jax.ShapeDtypeStruct((per, width, width), narrow),
            jax.ShapeDtypeStruct((deep, count, 8, width), narrow),
            jax.ShapeDtypeStruct((deep, per, part, width), narrow),
        ],
        scratch_shapes=[pltpu.VMEM((per, deep * count, part, width), wide)],
        compiler_params=params(),
        cost_estimate=cost(10 * per * deep * part * width * width, 16e6),
    )(mesh_at(), left, right, *parts)


def select_kernel(slot_ref, slots_ref, out_ref):
    per, part = slots_ref.shape[1:3]
    for b in range(out_ref.shape[0] // part):
        slot = slot_ref[b]
        out_ref[b * part : (b + 1) * part] = slots_ref[slot // per, slot % per]


def select_call(block_slot, slots, first):
    part, width = slots.shape[2:]
    return pl.pallas_call(
        beside(select_kernel, 2, len(first)),
        in_specs=[pl.BlockSpec(memory_space=pltpu.SMEM)] + in_vmem(1) + anywhere(first),
        out_specs=pl.BlockSpec(memory_space=pltpu.VMEM),
        out_shape=jax.ShapeDtypeStruct((block_slot.shape[0] * part, width), narrow),
        compiler_params=params(),
        cost_estimate=cost(0, 2e6),
    )(block_slot, slots, *first)


def stats_kernel(factor_ref, grad_ref, left_ref, right_ref, left_out, right_out):
    grad = grad_ref[0]
    share = (1 - stat_decay) * factor_ref[0] * factor_ref[0]
    left_out[0] = stat_decay * left_ref[0] + share * dot(grad, grad, 1, 1)
    right_out[0] = stat_decay * right_ref[0] + share * dot(grad, grad, 0, 0)


def stats_call(factor, grads, left, right, first):
    per, width, _ = grads.shape
    one = spec((1, width, width), lambda i: (i, 0, 0))
    return pl.pallas_call(
        beside(stats_kernel, 4, len(first)),
        grid=(per,),
        in_specs=[pl.BlockSpec(memory_space=pltpu.SMEM), one, one, one] + anywhere(first),
        out_specs=[one, one],
        out_shape=[jax.ShapeDtypeStruct(left.shape, wide)] * 2,
        compiler_params=params(),
        cost_estimate=cost(4 * per * width**3, 20e6),
    )(factor.reshape(1), grads, left, right, *first)


def update_kernel(at_ref, factor_ref, block_ref, *refs, count, part):
    parts, out_ref = refs[:count], refs[count]
    factor = factor_ref[0]
    for j, ref in enumerate(parts):
        to = at_ref[1] ^ j
        for b in range(out_ref.shape[0]):
            old = block_ref[b, to]
            step = ref[b * part : (b + 1) * part].astype(wide) * factor
            out_ref[b, to] = old - shampoo_rate * (step + decay_rate * old)


def finish_call(kernel, factor, arrays, parts, part, shapes, first=()):
    smem = pl.BlockSpec(memory_space=pltpu.SMEM)
    return pl.pallas_call(
        beside(functools.partial(kernel, count=len(parts), part=part), 2 + len(arrays) + len(parts), len(first)),
        in_specs=[smem, smem] + in_vmem(len(arrays) + len(parts)) + anywhere(first),
        out_specs=in_vmem(len(shapes)),
        out_shape=[jax.ShapeDtypeStruct(shape, wide) for shape in shapes],
        compiler_params=params(),
        cost_estimate=cost(0, 12e6),
    )(mesh_at(), factor.reshape(1), *arrays, *parts, *first)


def adam(weight, grad, first, second, rate, decay):
    first_new = first_decay * first + (1 - first_decay) * grad
    second_new = second_decay * second + (1 - second_decay) * grad * grad
    corrected = (
        first_new
        / (1 - first_decay**STEP)
        / (jnp.sqrt(second_new / (1 - second_decay**STEP)) + adam_eps)
    )
    return (weight - rate * (corrected + decay * weight), first_new, second_new)


def product(spec_text, a, b):
    return jnp.einsum(spec_text, a, b, preferred_element_type=wide)


def local(
    patches, positions, lengths, res_weights, labels, block_slot, blocks, pos_table, gains, head,
    left_stats, right_stats, left_roots, right_roots,
    pos_first, pos_second, gain_first, gain_second, head_first, head_second,
):
    mb = patches.shape[0]
    deep, size = lax.axis_size("fsdp"), lax.axis_size("seq")
    me_f, me_s = lax.axis_index("fsdp"), lax.axis_index("seq")
    lengths, res_weights, labels = (x[:, 0] for x in (lengths, res_weights, labels))
    lanes = pos_table.shape[2]
    width = lanes * deep
    grid_rows = pos_table.shape[1]

    part = blocks.shape[1] // size
    seen = jnp.broadcast_to(jnp.sum(res_weights).astype(wide), (lanes, 3))
    small = jnp.concatenate(
        [pos_table.reshape(2 * grid_rows, lanes).T, gains.T, seen, jnp.zeros((lanes, 120), wide)], axis=1
    ).astype(narrow)
    opening = my_rows(jnp.concatenate([blocks[0].astype(narrow), small], axis=1)[None])[0]
    project = my_rows(blocks[1:4]).astype(narrow).transpose(1, 0, 2).reshape(part, 3 * width)
    near = near_exchange(jnp.concatenate([opening, project], axis=1))
    every = far_exchange(near)
    positions, lengths, res_weights, labels, later, later_head, left_part, right_part, _ = lax.optimization_barrier(
        (positions, lengths, res_weights, labels, blocks, head, left_roots, right_roots, near)
    )
    left_part = pick_index(left_part.reshape(left_roots.shape[0], deep, size, part, width), me_s, 2).astype(narrow)
    right_part = right_part.astype(narrow)
    places = positions[:, :, 0, :ROWS]
    grid = jnp.arange(grid_rows)
    hot = jnp.concatenate([places[i][:, :, None] == grid for i in range(2)], axis=2).astype(narrow)
    index = jnp.arange(256)
    ones = jnp.where(index[:, None] // HEAD == index[None] // HEAD, 1 / HEAD, 0).astype(narrow)
    pick = (jnp.arange(width)[:, None] // HEAD == jnp.arange(128)[None]).astype(narrow)

    def column(x):
        x = jnp.pad(x, ((0, 0), (0, 6))).reshape(8 * mb, 1)
        return jnp.broadcast_to(x, (8 * mb, 128))

    seq_columns = [column(1.0 / lengths.astype(wide)), column(res_weights), column(labels)]
    rest_part = my_rows(later[4:13]).astype(narrow)
    head_part = my_rows(later_head[None])[0].astype(narrow)
    ahead = (hot, ones, pick, rest_part, head_part, left_part, right_part, *seq_columns)
    every = [every[0], tied(every[1], *ahead), *every[2:]]
    opening = stacked([x[:, :, : width + 256] for x in every])
    project = tied(stacked([x[:, :, width + 256 :] for x in every]), opening)
    opening = seq_parts(opening)
    w_embed = settle_rows(opening, [(0, part, 0, ())], [(deep, size, part, width + 256)])[0]
    w_embed = w_embed.reshape(width, width + 256)
    gains_full = w_embed[:, width + 128 :].T[:8].astype(wide)
    weight_sum = jnp.sum(gains_full[5].reshape(deep * size, part)[:, 0])
    w_rest = lax.all_gather(tied(rest_part, opening[-1]), ("fsdp", "seq"), axis=1, tiled=True)
    w_head = lax.all_gather(tied(head_part, opening[-1]), ("fsdp", "seq"), axis=0, tiled=True)

    embed, first = embed_call(patches, hot, tied(w_embed, project), gains_full)
    w_project = settle_rows(
        seq_parts(project, first), [(0, part, 0, ())], [(deep, size, part, 3 * width)]
    )[0].reshape(width, 3 * width)
    query, keys, values, *kept = project_call(first, w_project, gains_full, ones)
    mixed, stat = attend_call(lengths, query, keys, values)
    second, act, slope, unit2, unit3, row_stat, pool = forward_call(lengths, embed, mixed, w_rest, gains_full)

    loss, d_head, d_pool = head_call(pool.reshape(8 * mb, width), *seq_columns, w_head)
    head_sum = lax.psum_scatter(d_head, ("fsdp", "seq"), scatter_dimension=0, tiled=True)

    dm, d_up, dr, d_mixed, delta, d_gain_rest = backward_call(
        lengths, d_pool.reshape(mb, 8, width), unit3, unit2, row_stat, slope, mixed, w_rest, gains_full, pick
    )
    d_rest = weight_call(act, dm, second, d_up, mixed, dr)
    own_rest = lax.psum_scatter(d_rest, ("fsdp", "seq"), scatter_dimension=0, tiled=True)[0]

    pairs = HEADS // 2
    early = 4
    stats = jnp.stack([s[:, :, :HEADS].reshape(mb, ROWS, pairs, 2) for s in (stat, delta)], axis=3)
    stats = jnp.pad(stats.transpose(0, 2, 3, 4, 1).reshape(mb, pairs, 4, ROWS), ((0, 0), (0, 0), (0, 4), (0, 0)))
    stats = stats.reshape(mb, 8 * pairs, ROWS)

    def heads_back(after, start, count):
        out = attend_back_call(
            lengths, query, keys, values, d_mixed, kept, stats, gains_full, ones, start, count, after,
        )
        return out[:3], out[3]

    grads_one, gain_one = heads_back([d_rest], 0, early)
    mid_core = core_terms(*one_weight_call((first, *grads_one), first=[head_sum]))
    mid_x = Sum(mid_core, X)
    grads_two, gain_two = heads_back(mid_x.sent, early, pairs - early)
    mid_y = Sum(mid_x.after(grads_two[0]), Y)
    late_core = core_terms(*one_weight_call((first, *grads_two), first=mid_y.sent))
    late_x = Sum(late_core, X)
    d_embed, d_gain_first = first_call(
        (*grads_one, *grads_two), embed, dr, w_project, gains_full, late_x.sent
    )
    late_y = Sum(late_x.after(d_embed), Y)
    d_gain_heads = jnp.concatenate([gain_one, gain_two], axis=0).transpose(1, 0, 2).reshape(8, width)
    d_gains = jnp.concatenate(
        [d_gain_first[:1], d_gain_heads[:2], d_gain_rest[3:5], jnp.zeros((123, width), wide)], axis=0
    ).T
    e_own, e_sent = embed_weight_call(patches, hot, d_embed, d_gains, [own_rest, *late_y.sent])
    head_sum = tied(head_sum, e_own) / weight_sum
    scalars = jnp.stack([weight_sum, jnp.sum(jnp.square(head_sum)), loss[0, 0]])
    last_y = Sum(Sum(core_terms(e_own, e_sent), X).terms, Y)
    both_z = Sum(
        [
            jnp.concatenate([x.astype(wide) for x in terms], axis=3)
            for terms in zip(last_y.terms, late_y.terms, mid_y.terms)
        ],
        Z,
    )

    per = left_stats.shape[0]
    count = blocks.shape[0]
    own, *outgoing = collect_call(
        block_slot, scalars, own_rest, both_z.terms, per,
        early * 2 * HEAD, [],
    )
    arrived = seq_parts(jnp.stack([swap(x, "fsdp", k) for k, x in enumerate(outgoing)]))
    slotted, notes, directions = direction_call(left_part, right_part, arrived)
    notes = jnp.sum(notes[:, :, :, 0].astype(wide), axis=(0, 1))
    loss_sum = notes[3] + notes[4] + notes[5]
    clip_norm = jnp.sqrt(notes[0] + notes[1] + notes[2])
    factor = jnp.minimum(1.0, clip_bound / clip_norm)
    came = lax.all_to_all(directions, "fsdp", split_axis=0, concat_axis=0, tiled=True)
    own_parts = seq_parts(tied(own, slotted))
    head_parts = seq_parts(tied(head_sum, slotted))
    left_new, right_new = stats_call(factor, slotted, left_stats, right_stats, [])
    back = select_call(block_slot, came, [own_parts[-1], head_parts[-1]])
    back_parts = seq_parts(back)
    split = (count, size, part, width)
    block_grads, small_grad = finish_call(
        grads_kernel, factor, [], own_parts, part, [split, (size, part // 3, width)], [back]
    )
    head_all = settled(
        head_parts,
        [(size, *head_sum.shape)],
        [(j, (), 0, lambda f, s, j=j: j ^ s) for j in range(size)],
        [back],
    )[0].reshape(head.shape)

    small_grad = jnp.concatenate([small_grad[:, :, i * 256 : (i + 1) * 256] for i in range(3)], axis=1)
    small_grad = small_grad.reshape(lanes, 256).T
    table_grad = small_grad[: 2 * grid_rows].reshape(2, grid_rows, lanes)
    gain_grad = small_grad[2 * grid_rows : 2 * grid_rows + 5]
    pos_new, pos_first_new, pos_second_new = adam(
        pos_table, table_grad, pos_first, pos_second, table_rate, decay_rate
    )
    gains_new, gain_first_new, gain_second_new = adam(gains, gain_grad, gain_first, gain_second, gain_rate, 0.0)
    head_new, head_first_new, head_second_new = adam(
        head, head_all * factor, head_first, head_second, adam_rate, decay_rate
    )
    blocks_new = finish_call(
        update_kernel, factor, [blocks.reshape(split)], back_parts, part, [split],
        [block_grads, right_new, pos_new, gains_new, head_new],
    )[0].reshape(blocks.shape)
    block_grads = block_grads.reshape(blocks.shape)
    return (
        blocks_new, block_grads, left_new, right_new, pos_new, pos_first_new, pos_second_new,
        gains_new, gain_first_new, gain_second_new, head_new, head_first_new, head_second_new,
        clip_norm, loss_sum, weight_sum,
    )


def solution(mesh):
    placed = (
        P(None, ("seq", "fsdp"), None, None),
        P(None, None, ("seq", "fsdp"), None),
        P(None, ("seq", "fsdp"), None),
        P(None, ("seq", "fsdp"), None),
        P(None, ("seq", "fsdp"), None),
        P(),
        P(None, "fsdp", None),
        P(None, None, "fsdp"),
        P(None, "fsdp"),
        P("fsdp", None),
        P("fsdp", None, None),
        P("fsdp", None, None),
        P("fsdp", None, None),
        P("fsdp", None, None),
        P(None, None, "fsdp"),
        P(None, None, "fsdp"),
        P(None, "fsdp"),
        P(None, "fsdp"),
        P("fsdp", None),
        P("fsdp", None),
    )
    return jax.shard_map(
        local,
        mesh=mesh,
        in_specs=placed,
        out_specs=(
            P(None, "fsdp", None),
            P(None, "fsdp", None),
            P("fsdp", None, None),
            P("fsdp", None, None),
            P(None, None, "fsdp"),
            P(None, None, "fsdp"),
            P(None, None, "fsdp"),
            P(None, "fsdp"),
            P(None, "fsdp"),
            P(None, "fsdp"),
            P("fsdp", None),
            P("fsdp", None),
            P("fsdp", None),
            P(),
            P(),
            P(),
        ),
        check_vma=False,
    )
```

```python
import functools
import math
import jax
import jax.numpy as jnp
from jax import lax
from jax.experimental import pallas as pl
from jax.experimental.pallas import tpu as pltpu
from jax.sharding import PartitionSpec as P

HEADS = 12
HEAD = 64
PACK = 1536
LONG = 1152
SHORT = 256
ROWS = LONG + SHORT
TILE = 352
STEP = 10
clip_bound = 0.01
stat_decay = 0.95
shampoo_rate = 0.1
decay_rate = 0.01
first_decay = 0.9
second_decay = 0.95
adam_rate = 0.04
table_rate = 0.5
gain_rate = 0.25
adam_eps = 1e-10
norm_eps = 1e-06
narrow = jnp.bfloat16
wide = jnp.float32
log2e = math.log2(math.e)
VM = 60 * 1024 * 1024
SMALL_VM = 20 * 1024 * 1024


def params(limit=VM):
    return pltpu.CompilerParams(vmem_limit_bytes=limit)


def dot(a, b, ca=1, cb=0):
    return lax.dot_general(a, b, (((ca,), (cb,)), ((), ())), preferred_element_type=wide)


def norm_rows(v):
    c = v - jnp.mean(v, axis=-1, keepdims=True)
    r = lax.rsqrt(jnp.mean(c * c, axis=-1, keepdims=True) + norm_eps)
    return c * r, r


def back_rows(unit, r, scaled):
    return r * (
        scaled
        - jnp.mean(scaled, axis=-1, keepdims=True)
        - unit * jnp.mean(scaled * unit, axis=-1, keepdims=True)
    )


def spec(shape, index):
    return pl.BlockSpec(shape, index)


def beside(kernel, inputs, count):
    return lambda *refs: kernel(*refs[:inputs], *refs[inputs + count :])


def anywhere(arrays):
    return [pl.BlockSpec(memory_space=pl.ANY)] * len(arrays)


def held(shape):
    return pl.BlockSpec(shape, lambda *_: (0,) * len(shape), pipeline_mode=pl.Buffered(1))


def cost(flops, moved, trans=0):
    return pl.CostEstimate(flops=int(flops), bytes_accessed=int(moved), transcendentals=int(trans))


def embed_kernel(patch_ref, hot_ref, e_ref, gain_ref, embed_ref, first_ref):
    width = embed_ref.shape[2]
    v = dot(patch_ref[0, 0], e_ref[:, :width]) + dot(hot_ref[0], e_ref[:, width : width + 128], 1, 1)
    embed_ref[0] = v
    unit, _ = norm_rows(v)
    first_ref[0] = (unit * gain_ref[0:1]).astype(narrow)


def embed_call(patches, hot, e, gains):
    mb, width = patches.shape[0], gains.shape[1]
    steps = ROWS // TILE
    return pl.pallas_call(
        embed_kernel,
        grid=(mb, steps),
        in_specs=[
            spec((1, 1, TILE, patches.shape[3]), lambda m, i: (m, 0, i, 0)),
            spec((1, TILE, hot.shape[2]), lambda m, i: (m, i, 0)),
            held(e.shape),
            held(gains.shape),
        ],
        out_specs=[spec((1, TILE, width), lambda m, i: (m, i, 0))] * 2,
        out_shape=[
            jax.ShapeDtypeStruct((mb, ROWS, width), wide),
            jax.ShapeDtypeStruct((mb, ROWS, width), narrow),
        ],
        compiler_params=params(),
        cost_estimate=cost(2 * mb * ROWS * width * 896, 20e6),
    )(patches, hot, e, gains)


def group_mean(v, ones):
    return jnp.concatenate(
        [dot(v[:, at : at + 256].astype(narrow), ones) for at in range(0, v.shape[1], 256)], axis=1
    )


def project_kernel(first_ref, w_ref, gain_ref, ones_ref, q_ref, k_ref, v_ref, *kept):
    x = first_ref[0]
    width = x.shape[1]
    ones = ones_ref[...]
    for i, ref in enumerate((q_ref, k_ref)):
        raw = dot(x, w_ref[:, i * width : (i + 1) * width])
        c = raw - group_mean(raw, ones)
        r = lax.rsqrt(group_mean(c * c, ones) + norm_eps)
        unit = c * r
        kept[i][0] = unit.astype(narrow)
        kept[2 + i][0] = r.astype(narrow)
        out = (unit * gain_ref[1 + i : 2 + i]).astype(narrow)
        if i == 0:
            out = out * narrow(HEAD**-0.5)
        ref[0] = out
    v_ref[0] = dot(x, w_ref[:, 2 * width :]).astype(narrow)


def project_call(first, w, gains, ones):
    mb, _, width = first.shape
    rows = spec((1, TILE, width), lambda m, i: (m, i, 0))
    return pl.pallas_call(
        project_kernel,
        grid=(mb, ROWS // TILE),
        in_specs=[rows, held(w.shape), held(gains.shape), held(ones.shape)],
        out_specs=[rows] * 7,
        out_shape=[jax.ShapeDtypeStruct((mb, ROWS, width), narrow)] * 7,
        compiler_params=params(),
        cost_estimate=cost(2 * mb * ROWS * width * width * 3, 30e6),
    )(first, w, gains, ones)


ROWS_Q = 384


def attend_kernel(lengths_ref, q_ref, k_ref, v_ref, mixed_ref, stat_ref):
    pack, pair = pl.program_id(0), pl.program_id(1)
    lane = lax.broadcasted_iota(jnp.int32, (1, 2 * HEAD), 1)

    def part(start, count, tile, masked):
        k = k_ref[0, start : start + count]
        v = v_ref[0, start : start + count]
        zero = jnp.zeros_like(k)
        one = jnp.ones_like(k)
        k_both = [jnp.where(lane < HEAD, k, zero), jnp.where(lane < HEAD, zero, k)]
        ext = jnp.concatenate(
            [
                jnp.concatenate([jnp.where(lane < HEAD, v, zero), jnp.where(lane < HEAD, one, zero)], axis=1),
                jnp.concatenate([jnp.where(lane < HEAD, zero, v), jnp.where(lane < HEAD, zero, one)], axis=1),
            ],
            axis=0,
        )
        for at in range(start, start + count, tile):
            q = q_ref[0, at : at + tile]
            expos, peaks = [], []
            for h in range(2):
                s = dot(q, k_both[h], 1, 1)
                if masked:
                    limit = lengths_ref[pack, 1]
                    row = lax.broadcasted_iota(jnp.int32, s.shape, 0) + (at - start)
                    col = lax.broadcasted_iota(jnp.int32, s.shape, 1)
                    s = jnp.where((row < limit) == (col < limit), s, -1e30)
                peak = jnp.max(s, axis=1, keepdims=True)
                expos.append(jnp.exp2(s * log2e - peak * log2e).astype(narrow))
                peaks.append(peak)
            both = dot(jnp.concatenate(expos, axis=1), ext)
            total = both[:, 2 * HEAD :]
            mixed_ref[0, at : at + tile] = (both[:, : 2 * HEAD] / total).astype(narrow)
            lse = (jnp.where(lane < HEAD, peaks[0], peaks[1]) + jnp.log(total)) * log2e
            for h in range(2):
                column = jnp.sum(jnp.where(lane == h * HEAD, lse, 0.0), axis=1, keepdims=True)
                old = stat_ref[0, at : at + tile]
                stat_ref[0, at : at + tile] = jnp.where(lane == 2 * pair + h, column, old)

    part(0, LONG, ROWS_Q, False)
    part(LONG, SHORT, SHORT, True)


def attend_call(lengths, q, k, v):
    mb, _, width = q.shape
    block = pl.BlockSpec((1, ROWS, 2 * HEAD), lambda m, p, *_: (m, 0, p))
    pairs = width // (2 * HEAD)
    moved = mb * ROWS * width * 8
    return pl.pallas_call(
        attend_kernel,
        grid_spec=pltpu.PrefetchScalarGridSpec(
            num_scalar_prefetch=1,
            grid=(mb, pairs),
            in_specs=[block] * 3,
            out_specs=[block, pl.BlockSpec((1, ROWS, 128), lambda m, p, *_: (m, 0, 0))],
        ),
        out_shape=[
            jax.ShapeDtypeStruct((mb, ROWS, width), narrow),
            jax.ShapeDtypeStruct((mb, ROWS, 128), wide),
        ],
        compiler_params=params(),
        cost_estimate=cost(16 * mb * 2 * pairs * (LONG**2 + SHORT**2) * HEAD, moved),
    )(lengths, q, k, v)


def cdf_and_slope(up):
    cdf = 0.5 + 0.5 * lax.erf(up * 0.7071067811865476)
    slope = cdf + up * (jnp.exp2(up * up * (-0.5 * log2e)) * 0.3989422804014327)
    return cdf, slope


def forward_kernel(
    lengths_ref, embed_ref, mixed_ref, w_ref, gain_ref,
    second_ref, act_ref, slope_ref, unit2_ref, unit3_ref, stat_ref, pool_ref,
):
    pack, step = pl.program_id(0), pl.program_id(1)
    width = embed_ref.shape[2]
    resid = embed_ref[0] + dot(mixed_ref[0], w_ref[0])
    unit, r2 = norm_rows(resid)
    unit2_ref[0] = unit.astype(narrow)
    second = (unit * gain_ref[3:4]).astype(narrow)
    second_ref[0] = second
    outcome = resid
    for j in range(4):
        up = dot(second, w_ref[1 + j])
        cdf, slope = cdf_and_slope(up)
        act = (up * cdf).astype(narrow)
        act_ref[j, 0] = act
        slope_ref[j, 0] = slope.astype(narrow)
        outcome = outcome + dot(act, w_ref[5 + j])
    unit, r3 = norm_rows(outcome)
    unit3_ref[0] = unit.astype(narrow)
    lane = lax.broadcasted_iota(jnp.int32, (1, 128), 1)
    stat_ref[0] = jnp.where(lane == 0, r2, r3)
    final = unit * gain_ref[4:5]

    @pl.when(step == 0)
    def _():
        pool_ref[...] = jnp.zeros_like(pool_ref)

    row = lax.broadcasted_iota(jnp.int32, (TILE, 1), 0) + step * TILE
    first_len, second_len = lengths_ref[pack, 0], lengths_ref[pack, 1]
    inside = (row < first_len, (row >= first_len) & (row < first_len + second_len))
    for s in range(2):
        total = jnp.sum(jnp.where(inside[s], final, 0.0), axis=0, keepdims=True)
        pool_ref[0, s : s + 1] += total


def forward_call(lengths, embed, mixed, w, gains):
    mb, _, width = embed.shape
    rows = pl.BlockSpec((1, TILE, width), lambda m, i, *_: (m, i, 0))
    wider = pl.BlockSpec((4, 1, TILE, width), lambda m, i, *_: (0, m, i, 0))
    return pl.pallas_call(
        forward_kernel,
        grid_spec=pltpu.PrefetchScalarGridSpec(
            num_scalar_prefetch=1,
            grid=(mb, ROWS // TILE),
            in_specs=[rows, rows, held(w.shape), held(gains.shape)],
            out_specs=[
                rows, wider, wider, rows, rows,
                pl.BlockSpec((1, TILE, 128), lambda m, i, *_: (m, i, 0)),
                pl.BlockSpec((1, 8, width), lambda m, i, *_: (m, 0, 0)),
            ],
        ),
        out_shape=[
            jax.ShapeDtypeStruct((mb, ROWS, width), narrow),
            jax.ShapeDtypeStruct((4, mb, ROWS, width), narrow),
            jax.ShapeDtypeStruct((4, mb, ROWS, width), narrow),
            jax.ShapeDtypeStruct((mb, ROWS, width), narrow),
            jax.ShapeDtypeStruct((mb, ROWS, width), narrow),
            jax.ShapeDtypeStruct((mb, ROWS, 128), wide),
            jax.ShapeDtypeStruct((mb, 8, width), wide),
        ],
        compiler_params=params(),
        cost_estimate=cost(2 * mb * ROWS * width * width * 9, 80e6),
    )(lengths, embed, mixed, w, gains)


def head_kernel(pool_ref, scale_ref, weight_ref, label_ref, head_ref, loss_ref, dhead_ref, dpool_ref):
    pooled = (pool_ref[...] * scale_ref[:, 0:1]).astype(narrow)
    logits = dot(pooled, head_ref[...])
    peak = jnp.max(logits, axis=1, keepdims=True)
    expo = jnp.exp(logits - peak)
    total = jnp.sum(expo, axis=1, keepdims=True)
    hot = lax.broadcasted_iota(jnp.int32, logits.shape, 1) == label_ref[:, 0:1]
    picked = jnp.sum(jnp.where(hot, logits, 0.0), axis=1, keepdims=True)
    weight = weight_ref[:, 0:1].astype(wide)
    loss = jnp.where(weight > 0, weight * (peak + jnp.log(total) - picked), 0.0)
    loss_ref[...] = jnp.broadcast_to(jnp.sum(loss, axis=0, keepdims=True), loss_ref.shape)
    dlogits = (weight * (expo / total - hot.astype(wide))).astype(narrow)
    dhead_ref[...] = dot(pooled, dlogits, 0, 0).astype(dhead_ref.dtype)
    dpool_ref[...] = dot(dlogits, head_ref[...], 1, 1) * scale_ref[:, 0:1]


def head_call(pool, scale, weight, label, head, out=wide):
    rows, width = pool.shape
    return pl.pallas_call(
        head_kernel,
        out_shape=[
            jax.ShapeDtypeStruct((8, 128), wide),
            jax.ShapeDtypeStruct(head.shape, out),
            jax.ShapeDtypeStruct((rows, width), wide),
        ],
        compiler_params=params(),
        cost_estimate=cost(6 * rows * width * 1000, 8e6),
    )(pool, scale, weight, label, head)


def backward_kernel(
    lengths_ref, dpool_ref, unit3_ref, unit2_ref, stat_ref, slope_ref, mixed_ref, w_ref, gain_ref, pick_ref,
    dm_ref, dup_ref, dr_ref, dmixed_ref, delta_ref, dgain_ref,
):
    pack, step = pl.program_id(0), pl.program_id(1)
    row = lax.broadcasted_iota(jnp.int32, (TILE, 1), 0) + step * TILE
    first_len, second_len = lengths_ref[pack, 0], lengths_ref[pack, 1]
    dfinal = jnp.where(
        row < first_len,
        dpool_ref[0, 0:1],
        jnp.where(row < first_len + second_len, dpool_ref[0, 1:2], 0.0),
    )
    unit3 = unit3_ref[0].astype(wide)
    r2, r3 = stat_ref[0, :, 0:1], stat_ref[0, :, 1:2]
    doutcome = back_rows(unit3, r3, dfinal * gain_ref[4:5])
    dgf = jnp.sum(dfinal * unit3, axis=0, keepdims=True)
    dm = doutcome.astype(narrow)
    dm_ref[0] = dm
    dsecond = None
    for j in range(4):
        dact = dot(dm, w_ref[5 + j], 1, 1)
        dup = (dact * slope_ref[j, 0].astype(wide)).astype(narrow)
        dup_ref[j, 0] = dup
        term = dot(dup, w_ref[1 + j], 1, 1)
        dsecond = term if dsecond is None else dsecond + term
    unit2 = unit2_ref[0].astype(wide)
    dg2 = jnp.sum(dsecond * unit2, axis=0, keepdims=True)
    dresid = doutcome + back_rows(unit2, r2, dsecond * gain_ref[3:4])
    dr = dresid.astype(narrow)
    dr_ref[0] = dr
    dmixed = dot(dr, w_ref[0], 1, 1).astype(narrow)
    dmixed_ref[0] = dmixed
    delta_ref[0] = dot(dmixed * mixed_ref[0], pick_ref[...])

    @pl.when((pack == 0) & (step == 0))
    def _():
        dgain_ref[...] = jnp.zeros_like(dgain_ref)

    dgain_ref[3:4] += dg2
    dgain_ref[4:5] += dgf


def backward_call(lengths, dpool, unit3, unit2, stat, slope, mixed, w, gains, pick):
    mb, _, width = unit3.shape
    rows = pl.BlockSpec((1, TILE, width), lambda m, i, *_: (m, i, 0))
    lanes = pl.BlockSpec((1, TILE, 128), lambda m, i, *_: (m, i, 0))
    wider = pl.BlockSpec((4, 1, TILE, width), lambda m, i, *_: (0, m, i, 0))
    return pl.pallas_call(
        backward_kernel,
        grid_spec=pltpu.PrefetchScalarGridSpec(
            num_scalar_prefetch=1,
            grid=(mb, ROWS // TILE),
            in_specs=[
                pl.BlockSpec((1, 8, width), lambda m, i, *_: (m, 0, 0)),
                rows, rows, lanes, wider, rows,
                held(w.shape), held(gains.shape), held(pick.shape),
            ],
            out_specs=[rows, wider, rows, rows, lanes, pl.BlockSpec((8, width), lambda m, i, *_: (0, 0))],
        ),
        out_shape=[
            jax.ShapeDtypeStruct((mb, ROWS, width), narrow),
            jax.ShapeDtypeStruct((4, mb, ROWS, width), narrow),
            jax.ShapeDtypeStruct((mb, ROWS, width), narrow),
            jax.ShapeDtypeStruct((mb, ROWS, width), narrow),
            jax.ShapeDtypeStruct((mb, ROWS, 128), wide),
            jax.ShapeDtypeStruct((8, width), wide),
        ],
        compiler_params=params(),
        cost_estimate=cost(2 * mb * ROWS * width * width * 9, 70e6),
    )(lengths, dpool, unit3, unit2, stat, slope, mixed, w, gains, pick)


def attend_back_kernel(
    lengths_ref, q_ref, k_ref, v_ref, do_ref, qunit_ref, kunit_ref, qr_ref, kr_ref, stat_ref, gain_ref, ones_ref,
    dq_ref, dk_ref, dv_ref, dgain_ref, dq_acc, dk_acc, dv_acc,
):
    pack = pl.program_id(1)
    lane = lax.broadcasted_iota(jnp.int32, (1, 2 * HEAD), 1)

    def both(x, axis=0):
        zero = jnp.zeros_like(x)
        return jnp.concatenate([jnp.where(lane < HEAD, x, zero), jnp.where(lane < HEAD, zero, x)], axis=axis)

    def part(start, count, tile, chunk, masked):
        for ti in range(start, start + count, tile):
            q2 = both(q_ref[0, ti : ti + tile])
            do2 = both(do_ref[0, ti : ti + tile])
            lse = jnp.concatenate([stat_ref[0, h : h + 1, ti : ti + tile] for h in (0, 1)], axis=1)
            delta = jnp.concatenate([stat_ref[0, h : h + 1, ti : ti + tile] for h in (2, 3)], axis=1)
            for ui in range(start, start + count, chunk):
                k = k_ref[0, ui : ui + chunk]
                v = v_ref[0, ui : ui + chunk]
                s = dot(k, q2, 1, 1)
                p = jnp.exp2(s * log2e - lse)
                if masked:
                    limit = lengths_ref[pack, 1]
                    row = lax.broadcasted_iota(jnp.int32, s.shape, 0) + (ui - start)
                    col = lax.broadcasted_iota(jnp.int32, s.shape, 1)
                    col = jnp.where(col < tile, col, col - tile) + (ti - start)
                    p = jnp.where((row < limit) == (col < limit), p, 0.0)
                dp = dot(v, do2, 1, 1)
                ds = (p * (dp - delta)).astype(narrow)
                dv_new = dot(p.astype(narrow), do2)
                dk_new = dot(ds, q2)
                k2 = both(k)
                ds_rows = jnp.concatenate([ds[:, :tile], ds[:, tile:]], axis=0)
                dq_new = dot(ds_rows, k2, 0, 0)
                if ti == start:
                    dv_acc[ui : ui + chunk] = dv_new
                    dk_acc[ui : ui + chunk] = dk_new
                else:
                    dv_acc[ui : ui + chunk] += dv_new
                    dk_acc[ui : ui + chunk] += dk_new
                if ui == start:
                    dq_acc[ti : ti + tile] = dq_new
                else:
                    dq_acc[ti : ti + tile] += dq_new

    part(0, LONG, 384, 384, False)
    part(LONG, SHORT, SHORT, SHORT, True)
    dv_ref[0] = dv_acc[...].astype(narrow)
    ones = ones_ref[...]

    def mean(x):
        return dot(x.astype(narrow), ones)

    @pl.when(pack == 0)
    def _():
        dgain_ref[...] = jnp.zeros_like(dgain_ref)

    for i, (acc, unit_ref, r_ref, ref, factor) in enumerate(
        ((dq_acc, qunit_ref, qr_ref, dq_ref, HEAD**-0.5), (dk_acc, kunit_ref, kr_ref, dk_ref, 1.0))
    ):
        unit, r = unit_ref[0].astype(wide), r_ref[0].astype(wide)
        dy = acc[...] * factor
        dgain_ref[0, i : i + 1] += jnp.sum(dy * unit, axis=0, keepdims=True)
        scaled = dy * gain_ref[1 + i : 2 + i]
        ref[0] = (r * (scaled - mean(scaled) - unit * mean(scaled * unit))).astype(narrow)


def attend_back_call(lengths, q, k, v, do, kept, stat, gains, ones, first_pair, pairs, first=()):
    mb, _, width = q.shape
    block = pl.BlockSpec((1, ROWS, 2 * HEAD), lambda p, m, *_: (m, 0, p + first_pair))
    out = pl.BlockSpec((1, ROWS, 2 * HEAD), lambda p, m, *_: (m, 0, p))
    shape = jax.ShapeDtypeStruct((mb, ROWS, pairs * 2 * HEAD), narrow)
    return pl.pallas_call(
        beside(attend_back_kernel, 12, len(first)),
        grid_spec=pltpu.PrefetchScalarGridSpec(
            num_scalar_prefetch=1,
            grid=(pairs, mb),
            in_specs=[
                *[block] * 8,
                pl.BlockSpec((1, 8, ROWS), lambda p, m, *_: (m, p + first_pair, 0)),
                pl.BlockSpec((8, 2 * HEAD), lambda p, m, *_: (0, p + first_pair)),
                pl.BlockSpec((2 * HEAD, 2 * HEAD), lambda p, m, *_: (0, 0)),
                *anywhere(first),
            ],
            out_specs=[out, out, out, pl.BlockSpec((1, 8, 2 * HEAD), lambda p, m, *_: (p, 0, 0))],
            scratch_shapes=[pltpu.VMEM((ROWS, 2 * HEAD), wide)] * 3,
        ),
        out_shape=[shape, shape, shape, jax.ShapeDtypeStruct((pairs, 8, 2 * HEAD), wide)],
        compiler_params=params(),
        cost_estimate=cost(20 * mb * 2 * pairs * (LONG**2 + SHORT**2) * HEAD * 2, mb * ROWS * pairs * 128 * 18),
    )(lengths, q, k, v, do, *kept, stat, gains, ones, *first)


def first_kernel(*refs, parts):
    grads = refs[: 3 * parts]
    embed_ref, dr_ref, w_ref, gain_ref, out_ref, dgain_ref = refs[3 * parts :]
    step = pl.program_id(0) * pl.num_programs(1) + pl.program_id(1)
    width = embed_ref.shape[2]
    total = None
    for i in range(3):
        rows = jnp.concatenate([grads[3 * p + i][0] for p in range(parts)], axis=1)
        term = dot(rows, w_ref[:, i * width : (i + 1) * width], 1, 1)
        total = term if total is None else total + term
    unit, r = norm_rows(embed_ref[0])

    @pl.when(step == 0)
    def _():
        dgain_ref[...] = jnp.zeros_like(dgain_ref)

    dgain_ref[0:1] += jnp.sum(total * unit, axis=0, keepdims=True)
    out_ref[0] = (dr_ref[0].astype(wide) + back_rows(unit, r, total * gain_ref[0:1])).astype(narrow)


def first_call(grads, embed, dr, w, gains, first=()):
    mb, _, width = embed.shape
    rows = spec((1, TILE, width), lambda m, i: (m, i, 0))
    parts = len(grads) // 3
    return pl.pallas_call(
        beside(functools.partial(first_kernel, parts=parts), len(grads) + 4, len(first)),
        grid=(mb, ROWS // TILE),
        in_specs=[spec((1, TILE, g.shape[2]), lambda m, i: (m, i, 0)) for g in grads]
        + [rows, rows, held(w.shape), held(gains.shape)]
        + anywhere(first),
        out_specs=[rows, spec((8, width), lambda m, i: (0, 0))],
        out_shape=[
            jax.ShapeDtypeStruct((mb, ROWS, width), narrow),
            jax.ShapeDtypeStruct((8, width), wide),
        ],
        compiler_params=params(),
        cost_estimate=cost(2 * mb * ROWS * width * width * 3, 32e6),
    )(*grads, embed, dr, w, gains, *first)


def split_rows(value, own_ref, sent_ref, me, n):
    across, up, deep = own_ref.shape[:3]
    part = own_ref.shape[4]
    for x in range(across):
        for y in range(up):
            for z in range(deep):
                at = ((z * up + y) * across + x) * 2 * part
                first = value[at : at + part].astype(narrow)
                second = value[at + part : at + 2 * part].astype(narrow)
                own_ref[x, y, z, n] = jnp.where(me == 0, first, second)
                sent_ref[x, y, z, n] = jnp.where(me == 0, second, first)


def flat_rows(ref):
    return ref[...].reshape(-1, ref.shape[-1])


def weight_kernel(act_ref, dm_ref, second_ref, dup_ref, mixed_ref, dr_ref, out_ref):
    step = pl.program_id(0)

    def write(a_ref, b_ref):
        value = dot(flat_rows(a_ref), flat_rows(b_ref), 0, 0)
        part = out_ref.shape[2]
        for to in range(out_ref.shape[0]):
            out_ref[to, 0] = value[to * part : (to + 1) * part].astype(narrow)

    pl.when(step == 0)(lambda: write(mixed_ref, dr_ref))
    pl.when((step >= 1) & (step < 5))(lambda: write(second_ref, dup_ref))
    pl.when(step >= 5)(lambda: write(act_ref, dm_ref))


def split_shape(rows):
    core, x, y, z = (level[2] for level in levels())
    return (x, y, z), rows // (core * x * y * z)


def core_at():
    return (lax.axis_index("seq") % 2).reshape(1).astype(jnp.int32)


def weight_call(act, dm, second, dup, mixed, dr):
    width = dm.shape[2]
    parts = lax.axis_size("fsdp") * lax.axis_size("seq")
    rows = held(dm.shape)
    one = (1, *dm.shape)
    return pl.pallas_call(
        weight_kernel,
        grid=(9,),
        in_specs=[
            spec(one, lambda i: (jnp.maximum(i - 5, 0), 0, 0, 0)),
            rows,
            rows,
            spec(one, lambda i: (jnp.clip(i - 1, 0, 3), 0, 0, 0)),
            rows,
            rows,
        ],
        out_specs=spec((parts, 1, width // parts, width), lambda i: (0, i, 0, 0)),
        out_shape=jax.ShapeDtypeStruct((parts, 9, width // parts, width), narrow),
        compiler_params=params(),
        cost_estimate=cost(2 * 9 * dm.size * width, 70e6),
    )(act, dm, second, dup, mixed, dr)


def one_weight_kernel(at_ref, *refs, groups):
    count = len(groups) + sum(groups)
    own_ref, sent_ref, total = refs[count:]
    step = pl.program_id(0)
    last = step == pl.num_programs(0) - 1
    at, ref = 0, 0
    for members in groups:
        a = refs[ref][0]
        for b_ref in refs[ref + 1 : ref + 1 + members]:
            lanes = pl.ds(at, b_ref.shape[-1])
            at += b_ref.shape[-1]
            value = dot(a, b_ref[0], 0, 0)

            @pl.when(step == 0)
            def _(value=value, lanes=lanes):
                total[:, lanes] = value

            @pl.when((step > 0) & ~last)
            def _(value=value, lanes=lanes):
                total[:, lanes] += value

            @pl.when(last)
            def _(value=value, lanes=lanes):
                split_rows(total[:, lanes] + value, own_ref.at[..., lanes], sent_ref.at[..., lanes], at_ref[0], 0)

        ref += 1 + members


def one_weight_call(*groups, first=()):
    arrays = [array for group in groups for array in group]
    mb, rows, depth = arrays[0].shape
    width = sum(x.shape[-1] for group in groups for x in group[1:])
    (x, y, z), part = split_shape(depth)
    shape = (x, y, z, 1, part, width)
    out = pl.BlockSpec(shape, lambda m, *_: (0,) * 6)
    return pl.pallas_call(
        beside(
            functools.partial(one_weight_kernel, groups=[len(group) - 1 for group in groups]),
            1 + len(arrays),
            len(first),
        ),
        grid_spec=pltpu.PrefetchScalarGridSpec(
            num_scalar_prefetch=1,
            grid=(mb,),
            in_specs=[pl.BlockSpec((1, *v.shape[1:]), lambda m, *_: (m, 0, 0)) for v in arrays]
            + anywhere(first),
            out_specs=[out] * 2,
            scratch_shapes=[pltpu.VMEM((depth, width), wide)],
        ),
        out_shape=[jax.ShapeDtypeStruct(shape, narrow)] * 2,
        compiler_params=params(),
        cost_estimate=cost(2 * mb * rows * depth * width, 12e6),
    )(core_at(), *arrays, *first)


def embed_weight_kernel(at_ref, patch_ref, hot_ref, grad_ref, gain_ref, own_ref, sent_ref, total):
    step = pl.program_id(0)
    grad = grad_ref[0]
    width = grad.shape[1]
    value = dot(patch_ref[0, 0], grad, 0, 0)
    table = dot(grad, hot_ref[0], 0, 0)

    @pl.when(step == 0)
    def _():
        total[:, :width] = value
        total[:, width : width + 128] = table

    @pl.when(step > 0)
    def _():
        total[:, :width] += value
        total[:, width : width + 128] += table

    @pl.when(step == pl.num_programs(0) - 1)
    def _():
        total[:, width + 128 :] = gain_ref[...]
        split_rows(total[...], own_ref, sent_ref, at_ref[0], 0)


def embed_weight_call(patches, hot, grad, gain_columns, first=()):
    mb, _, width = grad.shape
    pixels = patches.shape[3]
    (x, y, z), part = split_shape(pixels)
    shape = (x, y, z, 1, part, width + 256)
    out = pl.BlockSpec(shape, lambda m, *_: (0,) * 6)
    return pl.pallas_call(
        beside(embed_weight_kernel, 5, len(first)),
        grid_spec=pltpu.PrefetchScalarGridSpec(
            num_scalar_prefetch=1,
            grid=(mb,),
            in_specs=[
                pl.BlockSpec((1, 1, ROWS, pixels), lambda m, *_: (m, 0, 0, 0)),
                pl.BlockSpec((1, ROWS, hot.shape[2]), lambda m, *_: (m, 0, 0)),
                pl.BlockSpec((1, ROWS, width), lambda m, *_: (m, 0, 0)),
                pl.BlockSpec((width, 128), lambda m, *_: (0, 0)),
                *anywhere(first),
            ],
            out_specs=[out, out],
            scratch_shapes=[pltpu.VMEM((pixels, width + 256), wide)],
        ),
        out_shape=[jax.ShapeDtypeStruct(shape, narrow)] * 2,
        compiler_params=params(),
        cost_estimate=cost(2 * grad.size * (pixels + 128), 12e6),
    )(core_at(), patches, hot, grad, gain_columns, *first)


def fold(parts):
    while len(parts) > 1:
        parts = [parts[i] + parts[i + 1] for i in range(0, len(parts), 2)]
    return parts[0]


def swap(x, axis, bits):
    if bits == 0:
        return x
    return lax.ppermute(x, axis, [(i, i ^ bits) for i in range(lax.axis_size(axis))])


def tied(x, *after):
    return lax.optimization_barrier((x, *after))[0]


def pick_index(x, index, dim):
    return lax.dynamic_index_in_dim(x, index, dim, keepdims=False)


def levels():
    across, deep = lax.axis_size("seq"), lax.axis_size("fsdp")
    y = 1 << ((deep.bit_length() - 1) // 2)
    return (("seq", 1, 2), ("seq", 2, across // 2), ("fsdp", 1, y), ("fsdp", y, deep // y))


CORE, X, Y, Z = range(4)


class Sum:
    def __init__(self, terms, which):
        axis, stride, size = levels()[which]
        at = lax.axis_index(axis) // stride % size

        def part(k):
            return fold([pick_index(term, at ^ k, 0).astype(wide) for term in terms])

        self.sent = [part(k).astype(narrow) for k in range(1, size)]
        self.terms = [part(0)] + [swap(x, axis, (k + 1) * stride) for k, x in enumerate(self.sent)]

    def after(self, *others):
        return [tied(self.terms[0], *others), *self.terms[1:]]

    def total(self):
        return fold([term.astype(wide) for term in self.terms])


def core_terms(own, sent):
    return [own, swap(sent, "seq", 1)]


def settle_kernel(at_ref, *refs, count, moves):
    sources, outs = refs[:count], refs[count:]
    for source, index, out, target in moves:
        outs[out][target(at_ref[0], at_ref[1])] = sources[source][index]


def mesh_at():
    return jnp.stack([lax.axis_index("fsdp"), lax.axis_index("seq")]).astype(jnp.int32)


def in_vmem(count):
    return [pl.BlockSpec(memory_space=pltpu.VMEM)] * count


def settled(parts, shapes, moves, first=()):
    size = sum(part.size for part in parts) * parts[0].dtype.itemsize
    return pl.pallas_call(
        beside(functools.partial(settle_kernel, count=len(parts), moves=moves), 1 + len(parts), len(first)),
        in_specs=[pl.BlockSpec(memory_space=pltpu.SMEM)] + in_vmem(len(parts)) + anywhere(first),
        out_specs=in_vmem(len(shapes)),
        out_shape=[jax.ShapeDtypeStruct(shape, parts[0].dtype) for shape in shapes],
        compiler_params=params(),
        cost_estimate=cost(0, 2 * size),
    )(mesh_at(), *parts, *first)


def seq_parts(x, *after):
    half = [swap(x, "seq", k) for k in range(0, lax.axis_size("seq"), 2)]
    if after:
        half = [half[0]] + [tied(y, *after) for y in half[1:]]
    return [part for y in half for part in (y, swap(y, "seq", 1))]


def settle_rows(parts, cuts, shapes):
    deep = parts[0].shape[0]
    moves = [
        (j, (k, slice(start, stop)), out, lambda f, s, j=j, k=k, index=index: (*index, k ^ f, j ^ s))
        for j in range(len(parts))
        for k in range(deep)
        for start, stop, out, index in cuts
    ]
    return settled(parts, shapes, moves)


def near_exchange(x):
    return jnp.stack([swap(x, "fsdp", k) for k in range(levels()[Y][2])])


def far_exchange(x):
    _, stride, far = levels()[Z]
    return [swap(x, "fsdp", k * stride) for k in range(far)]


def stacked(parts):
    return jnp.stack(parts).reshape(-1, *parts[0].shape[1:])


def my_rows(x):
    size = lax.axis_size("seq")
    return pick_index(x.reshape(x.shape[0], size, x.shape[1] // size, x.shape[2]), lax.axis_index("seq"), 1)


def grads_kernel(at_ref, factor_ref, *refs, count, part):
    parts, (out_ref, small_ref) = refs[:count], refs[count:]
    factor = factor_ref[0]
    for j, ref in enumerate(parts):
        to = at_ref[1] ^ j
        for b in range(out_ref.shape[0]):
            out_ref[b, to] = ref[b * part : (b + 1) * part].astype(wide) * factor
        small_ref[to] = ref[out_ref.shape[0] * part :].astype(wide) * factor


def join_kernel(at_ref, *refs, counts, size):
    ins, outs = refs[: sum(counts)], refs[sum(counts) :]
    for k in range(size):
        at = 0
        ref = 0
        for count in counts:
            value = fold([r[at_ref[0] ^ k].astype(wide) for r in ins[ref : ref + count]])
            ref += count
            lanes = value.shape[-1]
            outs[k][:, :, at : at + lanes] = value.astype(outs[k].dtype)
            at += lanes


def join_call(groups, first):
    axis, stride, size = levels()[Z]
    at = (lax.axis_index(axis) // stride % size).reshape(1).astype(jnp.int32)
    arrays = [term for terms in groups for term in terms]
    counts = [len(terms) for terms in groups]
    shape = (*arrays[0].shape[1:-1], sum(terms[0].shape[-1] for terms in groups))
    own, *sent = pl.pallas_call(
        beside(functools.partial(join_kernel, counts=counts, size=size), 1 + len(arrays), len(first)),
        in_specs=[pl.BlockSpec(memory_space=pltpu.SMEM)] + in_vmem(len(arrays)) + anywhere(first),
        out_specs=in_vmem(size),
        out_shape=[jax.ShapeDtypeStruct(shape, wide)] + [jax.ShapeDtypeStruct(shape, narrow)] * (size - 1),
        compiler_params=params(),
        cost_estimate=cost(0, 3e6),
    )(at, *arrays, *first)
    return [own] + [swap(x, axis, (k + 1) * stride) for k, x in enumerate(sent)]


def collect_kernel(at_ref, slot_ref, scalar_ref, rest_ref, *refs, count, deep, per, columns):
    terms, mid_terms = refs[:count], refs[count : 2 * count]
    own_ref, *out_refs = refs[2 * count : 2 * count + 1 + deep]
    blocks = refs[-1]
    part, width = rest_ref.shape[1:]
    scale = 1.0 / scalar_ref[0]
    both = fold([ref[0].astype(wide) for ref in terms])
    remain = width - columns
    late = both[:, width + 256 :]
    mid = fold([ref[0].astype(wide) for ref in mid_terms])
    pieces = [both[:, :width]]
    for i in range(3):
        first = mid[:, i * columns : (i + 1) * columns]
        pieces.append(jnp.concatenate([first, late[:, i * remain : (i + 1) * remain]], axis=1))
    pieces += [rest_ref[i].astype(wide) for i in range(rest_ref.shape[0])]
    squares = jnp.zeros((1, 1), wide)
    total = jnp.zeros((part, width), wide)
    for b, piece in enumerate(pieces):
        piece = (piece * scale).astype(narrow)
        blocks[b] = piece
        own_ref[b * part : (b + 1) * part] = piece
        total += jnp.square(piece.astype(wide))
    small = (both[:, width : width + 256] * scale).astype(narrow)
    third = part // 3
    small = small.astype(wide)
    squares = jnp.sum(total, keepdims=True) + jnp.sum(jnp.square(small), keepdims=True) + scalar_ref[1]
    small = jnp.concatenate([small[i * third : (i + 1) * third] for i in range(3)], axis=1)
    own_ref[len(pieces) * part :] = small.astype(narrow)
    row = lax.broadcasted_iota(jnp.int32, (8, width), 0)
    notes = jnp.zeros((8, width), wide)
    for at, value in ((0, squares), (3, jnp.full((1, 1), scalar_ref[2]))):
        for i in range(3):
            piece = value.astype(narrow).astype(wide)
            value = value - piece
            notes = jnp.where(row == at + i, piece, notes)
    notes = notes.astype(narrow)
    blocks[len(pieces)] = jnp.zeros((part, width), narrow)
    for k, out_ref in enumerate(out_refs):
        for i in range(per):
            slot = (at_ref[0] ^ k) * per + i
            found = len(pieces)
            for b in range(len(pieces)):
                found = jnp.where(slot_ref[b] == slot, b, found)
            out_ref[i * part : (i + 1) * part] = blocks[found]
        out_ref[per * part :] = notes


def collect_call(block_slot, scalars, rest, terms, mid_terms, per, columns, first):
    part, width = rest.shape[1:]
    deep = lax.axis_size("fsdp")
    count = block_slot.shape[0]
    smem = pl.BlockSpec(memory_space=pltpu.SMEM)
    message = jax.ShapeDtypeStruct((per * part + 8, width), narrow)
    return pl.pallas_call(
        beside(
            functools.partial(collect_kernel, count=len(terms), deep=deep, per=per, columns=columns),
            4 + 2 * len(terms),
            len(first),
        ),
        in_specs=[smem, smem, smem] + in_vmem(1 + 2 * len(terms)) + anywhere(first),
        out_specs=in_vmem(1 + deep),
        out_shape=[jax.ShapeDtypeStruct((count * part + part // 3, width), narrow)] + [message] * deep,
        scratch_shapes=[pltpu.VMEM((count + 1, part, width), narrow)],
        compiler_params=params(),
        cost_estimate=cost(0, 4e6),
    )(mesh_at(), block_slot, scalars, rest, *terms, *mid_terms, *first)


def direction_kernel(at_ref, left_ref, right_ref, *refs, count, deep):
    parts, slotted_ref, notes_ref = refs[:count], refs[count], refs[count + 1]
    out_ref, rows = refs[count + 2 :]
    per, _, part, width = left_ref.shape
    for j, ref in enumerate(parts):
        for k in range(deep):
            f, s = at_ref[0] ^ k, at_ref[1] ^ j
            for i in range(per):
                rows[i, f * count + s] = ref[k, i * part : (i + 1) * part].astype(wide)
            notes_ref[f, s] = ref[k, per * part :]
    for i in range(per):
        grad = rows[i].reshape(deep * count * part, width).astype(narrow)
        slotted_ref[i] = grad
        inner = dot(left_ref[i].astype(wide).reshape(deep * part, width).astype(narrow), grad)
        value = dot(inner.astype(narrow), right_ref[i])
        out_ref[:, i] = value.reshape(deep, part, width).astype(narrow)


def direction_call(left, right, parts):
    per, deep, part, width = left.shape
    count = len(parts)
    return pl.pallas_call(
        functools.partial(direction_kernel, count=count, deep=deep),
        in_specs=[pl.BlockSpec(memory_space=pltpu.SMEM)] + in_vmem(2 + count),
        out_specs=in_vmem(3),
        out_shape=[
            jax.ShapeDtypeStruct((per, width, width), narrow),
            jax.ShapeDtypeStruct((deep, count, 8, width), narrow),
            jax.ShapeDtypeStruct((deep, per, part, width), narrow),
        ],
        scratch_shapes=[pltpu.VMEM((per, deep * count, part, width), wide)],
        compiler_params=params(),
        cost_estimate=cost(10 * per * deep * part * width * width, 16e6),
    )(mesh_at(), left, right, *parts)


def select_kernel(slot_ref, slots_ref, out_ref):
    per, part = slots_ref.shape[1:3]
    for b in range(out_ref.shape[0] // part):
        slot = slot_ref[b]
        out_ref[b * part : (b + 1) * part] = slots_ref[slot // per, slot % per]


def select_call(block_slot, slots, first):
    part, width = slots.shape[2:]
    return pl.pallas_call(
        beside(select_kernel, 2, len(first)),
        in_specs=[pl.BlockSpec(memory_space=pltpu.SMEM)] + in_vmem(1) + anywhere(first),
        out_specs=pl.BlockSpec(memory_space=pltpu.VMEM),
        out_shape=jax.ShapeDtypeStruct((block_slot.shape[0] * part, width), narrow),
        compiler_params=params(),
        cost_estimate=cost(0, 2e6),
    )(block_slot, slots, *first)


def stats_kernel(factor_ref, grad_ref, left_ref, right_ref, left_out, right_out):
    grad = grad_ref[0]
    share = (1 - stat_decay) * factor_ref[0] * factor_ref[0]
    left_out[0] = stat_decay * left_ref[0] + share * dot(grad, grad, 1, 1)
    right_out[0] = stat_decay * right_ref[0] + share * dot(grad, grad, 0, 0)


def stats_call(factor, grads, left, right, first):
    per, width, _ = grads.shape
    one = spec((1, width, width), lambda i: (i, 0, 0))
    return pl.pallas_call(
        beside(stats_kernel, 4, len(first)),
        grid=(per,),
        in_specs=[pl.BlockSpec(memory_space=pltpu.SMEM), one, one, one] + anywhere(first),
        out_specs=[one, one],
        out_shape=[jax.ShapeDtypeStruct(left.shape, wide)] * 2,
        compiler_params=params(),
        cost_estimate=cost(4 * per * width**3, 20e6),
    )(factor.reshape(1), grads, left, right, *first)


def update_kernel(at_ref, factor_ref, block_ref, *refs, count, part):
    parts, out_ref = refs[:count], refs[count]
    factor = factor_ref[0]
    for j, ref in enumerate(parts):
        to = at_ref[1] ^ j
        for b in range(out_ref.shape[0]):
            old = block_ref[b, to]
            step = ref[b * part : (b + 1) * part].astype(wide) * factor
            out_ref[b, to] = old - shampoo_rate * (step + decay_rate * old)


def finish_call(kernel, factor, arrays, parts, part, shapes, first=()):
    smem = pl.BlockSpec(memory_space=pltpu.SMEM)
    return pl.pallas_call(
        beside(functools.partial(kernel, count=len(parts), part=part), 2 + len(arrays) + len(parts), len(first)),
        in_specs=[smem, smem] + in_vmem(len(arrays) + len(parts)) + anywhere(first),
        out_specs=in_vmem(len(shapes)),
        out_shape=[jax.ShapeDtypeStruct(shape, wide) for shape in shapes],
        compiler_params=params(),
        cost_estimate=cost(0, 12e6),
    )(mesh_at(), factor.reshape(1), *arrays, *parts, *first)


def adam(weight, grad, first, second, rate, decay):
    first_new = first_decay * first + (1 - first_decay) * grad
    second_new = second_decay * second + (1 - second_decay) * grad * grad
    corrected = (
        first_new
        / (1 - first_decay**STEP)
        / (jnp.sqrt(second_new / (1 - second_decay**STEP)) + adam_eps)
    )
    return (weight - rate * (corrected + decay * weight), first_new, second_new)


def product(spec_text, a, b):
    return jnp.einsum(spec_text, a, b, preferred_element_type=wide)


def local(
    patches, positions, lengths, res_weights, labels, block_slot, blocks, pos_table, gains, head,
    left_stats, right_stats, left_roots, right_roots,
    pos_first, pos_second, gain_first, gain_second, head_first, head_second,
):
    mb = patches.shape[0]
    deep, size = lax.axis_size("fsdp"), lax.axis_size("seq")
    me_f, me_s = lax.axis_index("fsdp"), lax.axis_index("seq")
    lengths, res_weights, labels = (x[:, 0] for x in (lengths, res_weights, labels))
    lanes = pos_table.shape[2]
    width = lanes * deep
    grid_rows = pos_table.shape[1]

    part = blocks.shape[1] // size
    seen = jnp.broadcast_to(jnp.sum(res_weights).astype(wide), (lanes, 3))
    small = jnp.concatenate(
        [pos_table.reshape(2 * grid_rows, lanes).T, gains.T, seen, jnp.zeros((lanes, 120), wide)], axis=1
    ).astype(narrow)
    opening = my_rows(jnp.concatenate([blocks[0].astype(narrow), small], axis=1)[None])[0]
    project = my_rows(blocks[1:4]).astype(narrow).transpose(1, 0, 2).reshape(part, 3 * width)
    near = near_exchange(jnp.concatenate([opening, project], axis=1))
    every = far_exchange(near)
    positions, lengths, res_weights, labels, later, later_head, left_part, right_part, _ = lax.optimization_barrier(
        (positions, lengths, res_weights, labels, blocks, head, left_roots, right_roots, near)
    )
    left_part = pick_index(left_part.reshape(left_roots.shape[0], deep, size, part, width), me_s, 2).astype(narrow)
    right_part = right_part.astype(narrow)
    places = positions[:, :, 0, :ROWS]
    grid = jnp.arange(grid_rows)
    hot = jnp.concatenate([places[i][:, :, None] == grid for i in range(2)], axis=2).astype(narrow)
    index = jnp.arange(256)
    ones = jnp.where(index[:, None] // HEAD == index[None] // HEAD, 1 / HEAD, 0).astype(narrow)
    pick = (jnp.arange(width)[:, None] // HEAD == jnp.arange(128)[None]).astype(narrow)

    def column(x):
        x = jnp.pad(x, ((0, 0), (0, 6))).reshape(8 * mb, 1)
        return jnp.broadcast_to(x, (8 * mb, 128))

    seq_columns = [column(1.0 / lengths.astype(wide)), column(res_weights), column(labels)]
    rest_part = my_rows(later[4:13]).astype(narrow)
    head_part = my_rows(later_head[None])[0].astype(narrow)
    ahead = (hot, ones, pick, rest_part, head_part, left_part, right_part, *seq_columns)
    every = [every[0], tied(every[1], *ahead), *every[2:]]
    opening = stacked([x[:, :, : width + 256] for x in every])
    project = tied(stacked([x[:, :, width + 256 :] for x in every]), opening)
    opening = seq_parts(opening)
    w_embed = settle_rows(opening, [(0, part, 0, ())], [(deep, size, part, width + 256)])[0]
    w_embed = w_embed.reshape(width, width + 256)
    gains_full = w_embed[:, width + 128 :].T[:8].astype(wide)
    weight_sum = jnp.sum(gains_full[5].reshape(deep * size, part)[:, 0])
    w_rest = lax.all_gather(tied(rest_part, opening[-1]), ("fsdp", "seq"), axis=1, tiled=True)
    w_head = lax.all_gather(tied(head_part, opening[-1]), ("fsdp", "seq"), axis=0, tiled=True)

    embed, first = embed_call(patches, hot, tied(w_embed, project), gains_full)
    w_project = settle_rows(
        seq_parts(project, first), [(0, part, 0, ())], [(deep, size, part, 3 * width)]
    )[0].reshape(width, 3 * width)
    query, keys, values, *kept = project_call(first, w_project, gains_full, ones)
    mixed, stat = attend_call(lengths, query, keys, values)
    second, act, slope, unit2, unit3, row_stat, pool = forward_call(lengths, embed, mixed, w_rest, gains_full)

    loss, d_head, d_pool = head_call(pool.reshape(8 * mb, width), *seq_columns, w_head)
    head_sum = lax.psum_scatter(d_head, ("fsdp", "seq"), scatter_dimension=0, tiled=True)

    dm, d_up, dr, d_mixed, delta, d_gain_rest = backward_call(
        lengths, d_pool.reshape(mb, 8, width), unit3, unit2, row_stat, slope, mixed, w_rest, gains_full, pick
    )
    d_rest = weight_call(act, dm, second, d_up, mixed, dr)
    own_rest = lax.psum_scatter(d_rest, ("fsdp", "seq"), scatter_dimension=0, tiled=True)[0]

    pairs = HEADS // 2
    early = 4
    stats = jnp.stack([s[:, :, :HEADS].reshape(mb, ROWS, pairs, 2) for s in (stat, delta)], axis=3)
    stats = jnp.pad(stats.transpose(0, 2, 3, 4, 1).reshape(mb, pairs, 4, ROWS), ((0, 0), (0, 0), (0, 4), (0, 0)))
    stats = stats.reshape(mb, 8 * pairs, ROWS)

    def heads_back(after, start, count):
        out = attend_back_call(
            lengths, query, keys, values, d_mixed, kept, stats, gains_full, ones, start, count, after,
        )
        return out[:3], out[3]

    grads_one, gain_one = heads_back([d_rest], 0, early)
    mid_core = core_terms(*one_weight_call((first, *grads_one), first=[head_sum]))
    mid_x = Sum(mid_core, X)
    grads_two, gain_two = heads_back(mid_x.sent, early, pairs - early)
    mid_y = Sum(mid_x.after(grads_two[0]), Y)
    late_core = core_terms(*one_weight_call((first, *grads_two), first=mid_y.sent))
    late_x = Sum(late_core, X)
    d_embed, d_gain_first = first_call(
        (*grads_one, *grads_two), embed, dr, w_project, gains_full, late_x.sent
    )
    late_y = Sum(late_x.after(d_embed), Y)
    d_gain_heads = jnp.concatenate([gain_one, gain_two], axis=0).transpose(1, 0, 2).reshape(8, width)
    d_gains = jnp.concatenate(
        [d_gain_first[:1], d_gain_heads[:2], d_gain_rest[3:5], jnp.zeros((123, width), wide)], axis=0
    ).T
    e_own, e_sent = embed_weight_call(
        patches, hot, d_embed, d_gains, [own_rest, *late_y.sent, *mid_y.terms[1:]]
    )
    head_sum = tied(head_sum, e_own) / weight_sum
    scalars = jnp.stack([weight_sum, jnp.sum(jnp.square(head_sum)), loss[0, 0]])
    last_y = Sum(Sum(core_terms(e_own, e_sent), X).terms, Y)
    mid_z = Sum(mid_y.after(e_own), Z)
    z_terms = join_call([last_y.terms, late_y.terms], mid_z.terms[1:])

    per = left_stats.shape[0]
    count = blocks.shape[0]
    own, *outgoing = collect_call(
        block_slot, scalars, own_rest, z_terms, mid_z.terms, per,
        early * 2 * HEAD, [],
    )
    arrived = seq_parts(jnp.stack([swap(x, "fsdp", k) for k, x in enumerate(outgoing)]))
    slotted, notes, directions = direction_call(left_part, right_part, arrived)
    notes = jnp.sum(notes[:, :, :, 0].astype(wide), axis=(0, 1))
    loss_sum = notes[3] + notes[4] + notes[5]
    clip_norm = jnp.sqrt(notes[0] + notes[1] + notes[2])
    factor = jnp.minimum(1.0, clip_bound / clip_norm)
    came = lax.all_to_all(directions, "fsdp", split_axis=0, concat_axis=0, tiled=True)
    own_parts = seq_parts(tied(own, slotted))
    head_parts = seq_parts(tied(head_sum, slotted))
    left_new, right_new = stats_call(factor, slotted, left_stats, right_stats, [])
    back = select_call(block_slot, came, [own_parts[-1], head_parts[-1]])
    back_parts = seq_parts(back)
    split = (count, size, part, width)
    block_grads, small_grad = finish_call(
        grads_kernel, factor, [], own_parts, part, [split, (size, part // 3, width)], [back]
    )
    head_all = settled(
        head_parts,
        [(size, *head_sum.shape)],
        [(j, (), 0, lambda f, s, j=j: j ^ s) for j in range(size)],
        [back],
    )[0].reshape(head.shape)

    small_grad = jnp.concatenate([small_grad[:, :, i * 256 : (i + 1) * 256] for i in range(3)], axis=1)
    small_grad = small_grad.reshape(lanes, 256).T
    table_grad = small_grad[: 2 * grid_rows].reshape(2, grid_rows, lanes)
    gain_grad = small_grad[2 * grid_rows : 2 * grid_rows + 5]
    pos_new, pos_first_new, pos_second_new = adam(
        pos_table, table_grad, pos_first, pos_second, table_rate, decay_rate
    )
    gains_new, gain_first_new, gain_second_new = adam(gains, gain_grad, gain_first, gain_second, gain_rate, 0.0)
    head_new, head_first_new, head_second_new = adam(
        head, head_all * factor, head_first, head_second, adam_rate, decay_rate
    )
    blocks_new = finish_call(
        update_kernel, factor, [blocks.reshape(split)], back_parts, part, [split],
        [block_grads, right_new, pos_new, gains_new, head_new],
    )[0].reshape(blocks.shape)
    block_grads = block_grads.reshape(blocks.shape)
    return (
        blocks_new, block_grads, left_new, right_new, pos_new, pos_first_new, pos_second_new,
        gains_new, gain_first_new, gain_second_new, head_new, head_first_new, head_second_new,
        clip_norm, loss_sum, weight_sum,
    )


def solution(mesh):
    placed = (
        P(None, ("seq", "fsdp"), None, None),
        P(None, None, ("seq", "fsdp"), None),
        P(None, ("seq", "fsdp"), None),
        P(None, ("seq", "fsdp"), None),
        P(None, ("seq", "fsdp"), None),
        P(),
        P(None, "fsdp", None),
        P(None, None, "fsdp"),
        P(None, "fsdp"),
        P("fsdp", None),
        P("fsdp", None, None),
        P("fsdp", None, None),
        P("fsdp", None, None),
        P("fsdp", None, None),
        P(None, None, "fsdp"),
        P(None, None, "fsdp"),
        P(None, "fsdp"),
        P(None, "fsdp"),
        P("fsdp", None),
        P("fsdp", None),
    )
    return jax.shard_map(
        local,
        mesh=mesh,
        in_specs=placed,
        out_specs=(
            P(None, "fsdp", None),
            P(None, "fsdp", None),
            P("fsdp", None, None),
            P("fsdp", None, None),
            P(None, None, "fsdp"),
            P(None, None, "fsdp"),
            P(None, None, "fsdp"),
            P(None, "fsdp"),
            P(None, "fsdp"),
            P(None, "fsdp"),
            P("fsdp", None),
            P("fsdp", None),
            P("fsdp", None),
            P(),
            P(),
            P(),
        ),
        check_vma=False,
    )
```

```python
import functools
import math
import jax
import jax.numpy as jnp
from jax import lax
from jax.experimental import pallas as pl
from jax.experimental.pallas import tpu as pltpu
from jax.sharding import PartitionSpec as P

HEADS = 12
HEAD = 64
PACK = 1536
LONG = 1152
SHORT = 256
ROWS = LONG + SHORT
TILE = 352
STEP = 10
clip_bound = 0.01
stat_decay = 0.95
shampoo_rate = 0.1
decay_rate = 0.01
first_decay = 0.9
second_decay = 0.95
adam_rate = 0.04
table_rate = 0.5
gain_rate = 0.25
adam_eps = 1e-10
norm_eps = 1e-06
narrow = jnp.bfloat16
wide = jnp.float32
log2e = math.log2(math.e)
VM = 60 * 1024 * 1024
SMALL_VM = 20 * 1024 * 1024


def params(limit=VM):
    return pltpu.CompilerParams(vmem_limit_bytes=limit)


def dot(a, b, ca=1, cb=0):
    return lax.dot_general(a, b, (((ca,), (cb,)), ((), ())), preferred_element_type=wide)


def norm_rows(v):
    c = v - jnp.mean(v, axis=-1, keepdims=True)
    r = lax.rsqrt(jnp.mean(c * c, axis=-1, keepdims=True) + norm_eps)
    return c * r, r


def back_rows(unit, r, scaled):
    return r * (
        scaled
        - jnp.mean(scaled, axis=-1, keepdims=True)
        - unit * jnp.mean(scaled * unit, axis=-1, keepdims=True)
    )


def spec(shape, index):
    return pl.BlockSpec(shape, index)


def beside(kernel, inputs, count):
    return lambda *refs: kernel(*refs[:inputs], *refs[inputs + count :])


def anywhere(arrays):
    return [pl.BlockSpec(memory_space=pl.ANY)] * len(arrays)


def held(shape):
    return pl.BlockSpec(shape, lambda *_: (0,) * len(shape), pipeline_mode=pl.Buffered(1))


def cost(flops, moved, trans=0):
    return pl.CostEstimate(flops=int(flops), bytes_accessed=int(moved), transcendentals=int(trans))


def embed_kernel(patch_ref, hot_ref, e_ref, gain_ref, embed_ref, first_ref):
    width = embed_ref.shape[2]
    v = dot(patch_ref[0, 0], e_ref[:, :width]) + dot(hot_ref[0], e_ref[:, width : width + 128], 1, 1)
    embed_ref[0] = v
    unit, _ = norm_rows(v)
    first_ref[0] = (unit * gain_ref[0:1]).astype(narrow)


def embed_call(patches, hot, e, gains):
    mb, width = patches.shape[0], gains.shape[1]
    steps = ROWS // TILE
    return pl.pallas_call(
        embed_kernel,
        grid=(mb, steps),
        in_specs=[
            spec((1, 1, TILE, patches.shape[3]), lambda m, i: (m, 0, i, 0)),
            spec((1, TILE, hot.shape[2]), lambda m, i: (m, i, 0)),
            held(e.shape),
            held(gains.shape),
        ],
        out_specs=[spec((1, TILE, width), lambda m, i: (m, i, 0))] * 2,
        out_shape=[
            jax.ShapeDtypeStruct((mb, ROWS, width), wide),
            jax.ShapeDtypeStruct((mb, ROWS, width), narrow),
        ],
        compiler_params=params(),
        cost_estimate=cost(2 * mb * ROWS * width * 896, 20e6),
    )(patches, hot, e, gains)


def group_mean(v, ones):
    return jnp.concatenate(
        [dot(v[:, at : at + 256].astype(narrow), ones) for at in range(0, v.shape[1], 256)], axis=1
    )


def project_kernel(first_ref, w_ref, gain_ref, ones_ref, q_ref, k_ref, v_ref, *kept):
    x = first_ref[0]
    width = x.shape[1]
    ones = ones_ref[...]
    for i, ref in enumerate((q_ref, k_ref)):
        raw = dot(x, w_ref[:, i * width : (i + 1) * width])
        c = raw - group_mean(raw, ones)
        r = lax.rsqrt(group_mean(c * c, ones) + norm_eps)
        unit = c * r
        kept[i][0] = unit.astype(narrow)
        kept[2 + i][0] = r.astype(narrow)
        out = (unit * gain_ref[1 + i : 2 + i]).astype(narrow)
        if i == 0:
            out = out * narrow(HEAD**-0.5)
        ref[0] = out
    v_ref[0] = dot(x, w_ref[:, 2 * width :]).astype(narrow)


def project_call(first, w, gains, ones):
    mb, _, width = first.shape
    rows = spec((1, TILE, width), lambda m, i: (m, i, 0))
    return pl.pallas_call(
        project_kernel,
        grid=(mb, ROWS // TILE),
        in_specs=[rows, held(w.shape), held(gains.shape), held(ones.shape)],
        out_specs=[rows] * 7,
        out_shape=[jax.ShapeDtypeStruct((mb, ROWS, width), narrow)] * 7,
        compiler_params=params(),
        cost_estimate=cost(2 * mb * ROWS * width * width * 3, 30e6),
    )(first, w, gains, ones)


ROWS_Q = 384


def attend_kernel(lengths_ref, q_ref, k_ref, v_ref, mixed_ref, stat_ref):
    pack, pair = pl.program_id(0), pl.program_id(1)
    lane = lax.broadcasted_iota(jnp.int32, (1, 2 * HEAD), 1)

    def part(start, count, tile, masked):
        k = k_ref[0, start : start + count]
        v = v_ref[0, start : start + count]
        zero = jnp.zeros_like(k)
        one = jnp.ones_like(k)
        k_both = [jnp.where(lane < HEAD, k, zero), jnp.where(lane < HEAD, zero, k)]
        ext = jnp.concatenate(
            [
                jnp.concatenate([jnp.where(lane < HEAD, v, zero), jnp.where(lane < HEAD, one, zero)], axis=1),
                jnp.concatenate([jnp.where(lane < HEAD, zero, v), jnp.where(lane < HEAD, zero, one)], axis=1),
            ],
            axis=0,
        )
        for at in range(start, start + count, tile):
            q = q_ref[0, at : at + tile]
            expos, peaks = [], []
            for h in range(2):
                s = dot(q, k_both[h], 1, 1)
                if masked:
                    limit = lengths_ref[pack, 1]
                    row = lax.broadcasted_iota(jnp.int32, s.shape, 0) + (at - start)
                    col = lax.broadcasted_iota(jnp.int32, s.shape, 1)
                    s = jnp.where((row < limit) == (col < limit), s, -1e30)
                peak = jnp.max(s, axis=1, keepdims=True)
                expos.append(jnp.exp2(s * log2e - peak * log2e).astype(narrow))
                peaks.append(peak)
            both = dot(jnp.concatenate(expos, axis=1), ext)
            total = both[:, 2 * HEAD :]
            mixed_ref[0, at : at + tile] = (both[:, : 2 * HEAD] / total).astype(narrow)
            lse = (jnp.where(lane < HEAD, peaks[0], peaks[1]) + jnp.log(total)) * log2e
            for h in range(2):
                column = jnp.sum(jnp.where(lane == h * HEAD, lse, 0.0), axis=1, keepdims=True)
                old = stat_ref[0, at : at + tile]
                stat_ref[0, at : at + tile] = jnp.where(lane == 2 * pair + h, column, old)

    part(0, LONG, ROWS_Q, False)
    part(LONG, SHORT, SHORT, True)


def attend_call(lengths, q, k, v):
    mb, _, width = q.shape
    block = pl.BlockSpec((1, ROWS, 2 * HEAD), lambda m, p, *_: (m, 0, p))
    pairs = width // (2 * HEAD)
    moved = mb * ROWS * width * 8
    return pl.pallas_call(
        attend_kernel,
        grid_spec=pltpu.PrefetchScalarGridSpec(
            num_scalar_prefetch=1,
            grid=(mb, pairs),
            in_specs=[block] * 3,
            out_specs=[block, pl.BlockSpec((1, ROWS, 128), lambda m, p, *_: (m, 0, 0))],
        ),
        out_shape=[
            jax.ShapeDtypeStruct((mb, ROWS, width), narrow),
            jax.ShapeDtypeStruct((mb, ROWS, 128), wide),
        ],
        compiler_params=params(),
        cost_estimate=cost(16 * mb * 2 * pairs * (LONG**2 + SHORT**2) * HEAD, moved),
    )(lengths, q, k, v)


def cdf_and_slope(up):
    cdf = 0.5 + 0.5 * lax.erf(up * 0.7071067811865476)
    slope = cdf + up * (jnp.exp2(up * up * (-0.5 * log2e)) * 0.3989422804014327)
    return cdf, slope


def forward_kernel(
    lengths_ref, embed_ref, mixed_ref, w_ref, gain_ref,
    second_ref, act_ref, slope_ref, unit2_ref, unit3_ref, stat_ref, pool_ref,
):
    pack, step = pl.program_id(0), pl.program_id(1)
    width = embed_ref.shape[2]
    resid = embed_ref[0] + dot(mixed_ref[0], w_ref[0])
    unit, r2 = norm_rows(resid)
    unit2_ref[0] = unit.astype(narrow)
    second = (unit * gain_ref[3:4]).astype(narrow)
    second_ref[0] = second
    outcome = resid
    for j in range(4):
        up = dot(second, w_ref[1 + j])
        cdf, slope = cdf_and_slope(up)
        act = (up * cdf).astype(narrow)
        act_ref[j, 0] = act
        slope_ref[j, 0] = slope.astype(narrow)
        outcome = outcome + dot(act, w_ref[5 + j])
    unit, r3 = norm_rows(outcome)
    unit3_ref[0] = unit.astype(narrow)
    lane = lax.broadcasted_iota(jnp.int32, (1, 128), 1)
    stat_ref[0] = jnp.where(lane == 0, r2, r3)
    final = unit * gain_ref[4:5]

    @pl.when(step == 0)
    def _():
        pool_ref[...] = jnp.zeros_like(pool_ref)

    row = lax.broadcasted_iota(jnp.int32, (TILE, 1), 0) + step * TILE
    first_len, second_len = lengths_ref[pack, 0], lengths_ref[pack, 1]
    inside = (row < first_len, (row >= first_len) & (row < first_len + second_len))
    for s in range(2):
        total = jnp.sum(jnp.where(inside[s], final, 0.0), axis=0, keepdims=True)
        pool_ref[0, s : s + 1] += total


def forward_call(lengths, embed, mixed, w, gains):
    mb, _, width = embed.shape
    rows = pl.BlockSpec((1, TILE, width), lambda m, i, *_: (m, i, 0))
    wider = pl.BlockSpec((4, 1, TILE, width), lambda m, i, *_: (0, m, i, 0))
    return pl.pallas_call(
        forward_kernel,
        grid_spec=pltpu.PrefetchScalarGridSpec(
            num_scalar_prefetch=1,
            grid=(mb, ROWS // TILE),
            in_specs=[rows, rows, held(w.shape), held(gains.shape)],
            out_specs=[
                rows, wider, wider, rows, rows,
                pl.BlockSpec((1, TILE, 128), lambda m, i, *_: (m, i, 0)),
                pl.BlockSpec((1, 8, width), lambda m, i, *_: (m, 0, 0)),
            ],
        ),
        out_shape=[
            jax.ShapeDtypeStruct((mb, ROWS, width), narrow),
            jax.ShapeDtypeStruct((4, mb, ROWS, width), narrow),
            jax.ShapeDtypeStruct((4, mb, ROWS, width), narrow),
            jax.ShapeDtypeStruct((mb, ROWS, width), narrow),
            jax.ShapeDtypeStruct((mb, ROWS, width), narrow),
            jax.ShapeDtypeStruct((mb, ROWS, 128), wide),
            jax.ShapeDtypeStruct((mb, 8, width), wide),
        ],
        compiler_params=params(),
        cost_estimate=cost(2 * mb * ROWS * width * width * 9, 80e6),
    )(lengths, embed, mixed, w, gains)


def head_kernel(pool_ref, scale_ref, weight_ref, label_ref, head_ref, loss_ref, dhead_ref, dpool_ref):
    pooled = (pool_ref[...] * scale_ref[:, 0:1]).astype(narrow)
    logits = dot(pooled, head_ref[...])
    peak = jnp.max(logits, axis=1, keepdims=True)
    expo = jnp.exp(logits - peak)
    total = jnp.sum(expo, axis=1, keepdims=True)
    hot = lax.broadcasted_iota(jnp.int32, logits.shape, 1) == label_ref[:, 0:1]
    picked = jnp.sum(jnp.where(hot, logits, 0.0), axis=1, keepdims=True)
    weight = weight_ref[:, 0:1].astype(wide)
    loss = jnp.where(weight > 0, weight * (peak + jnp.log(total) - picked), 0.0)
    loss_ref[...] = jnp.broadcast_to(jnp.sum(loss, axis=0, keepdims=True), loss_ref.shape)
    dlogits = (weight * (expo / total - hot.astype(wide))).astype(narrow)
    dhead_ref[...] = dot(pooled, dlogits, 0, 0).astype(dhead_ref.dtype)
    dpool_ref[...] = dot(dlogits, head_ref[...], 1, 1) * scale_ref[:, 0:1]


def head_call(pool, scale, weight, label, head, out=wide):
    rows, width = pool.shape
    return pl.pallas_call(
        head_kernel,
        out_shape=[
            jax.ShapeDtypeStruct((8, 128), wide),
            jax.ShapeDtypeStruct(head.shape, out),
            jax.ShapeDtypeStruct((rows, width), wide),
        ],
        compiler_params=params(),
        cost_estimate=cost(6 * rows * width * 1000, 8e6),
    )(pool, scale, weight, label, head)


def backward_kernel(
    lengths_ref, dpool_ref, unit3_ref, unit2_ref, stat_ref, slope_ref, mixed_ref, w_ref, gain_ref, pick_ref,
    dm_ref, dup_ref, dr_ref, dmixed_ref, delta_ref, dgain_ref,
):
    pack, step = pl.program_id(0), pl.program_id(1)
    row = lax.broadcasted_iota(jnp.int32, (TILE, 1), 0) + step * TILE
    first_len, second_len = lengths_ref[pack, 0], lengths_ref[pack, 1]
    dfinal = jnp.where(
        row < first_len,
        dpool_ref[0, 0:1],
        jnp.where(row < first_len + second_len, dpool_ref[0, 1:2], 0.0),
    )
    unit3 = unit3_ref[0].astype(wide)
    r2, r3 = stat_ref[0, :, 0:1], stat_ref[0, :, 1:2]
    doutcome = back_rows(unit3, r3, dfinal * gain_ref[4:5])
    dgf = jnp.sum(dfinal * unit3, axis=0, keepdims=True)
    dm = doutcome.astype(narrow)
    dm_ref[0] = dm
    dsecond = None
    for j in range(4):
        dact = dot(dm, w_ref[5 + j], 1, 1)
        dup = (dact * slope_ref[j, 0].astype(wide)).astype(narrow)
        dup_ref[j, 0] = dup
        term = dot(dup, w_ref[1 + j], 1, 1)
        dsecond = term if dsecond is None else dsecond + term
    unit2 = unit2_ref[0].astype(wide)
    dg2 = jnp.sum(dsecond * unit2, axis=0, keepdims=True)
    dresid = doutcome + back_rows(unit2, r2, dsecond * gain_ref[3:4])
    dr = dresid.astype(narrow)
    dr_ref[0] = dr
    dmixed = dot(dr, w_ref[0], 1, 1).astype(narrow)
    dmixed_ref[0] = dmixed
    delta_ref[0] = dot(dmixed * mixed_ref[0], pick_ref[...])

    @pl.when((pack == 0) & (step == 0))
    def _():
        dgain_ref[...] = jnp.zeros_like(dgain_ref)

    dgain_ref[3:4] += dg2
    dgain_ref[4:5] += dgf


def backward_call(lengths, dpool, unit3, unit2, stat, slope, mixed, w, gains, pick):
    mb, _, width = unit3.shape
    rows = pl.BlockSpec((1, TILE, width), lambda m, i, *_: (m, i, 0))
    lanes = pl.BlockSpec((1, TILE, 128), lambda m, i, *_: (m, i, 0))
    wider = pl.BlockSpec((4, 1, TILE, width), lambda m, i, *_: (0, m, i, 0))
    return pl.pallas_call(
        backward_kernel,
        grid_spec=pltpu.PrefetchScalarGridSpec(
            num_scalar_prefetch=1,
            grid=(mb, ROWS // TILE),
            in_specs=[
                pl.BlockSpec((1, 8, width), lambda m, i, *_: (m, 0, 0)),
                rows, rows, lanes, wider, rows,
                held(w.shape), held(gains.shape), held(pick.shape),
            ],
            out_specs=[rows, wider, rows, rows, lanes, pl.BlockSpec((8, width), lambda m, i, *_: (0, 0))],
        ),
        out_shape=[
            jax.ShapeDtypeStruct((mb, ROWS, width), narrow),
            jax.ShapeDtypeStruct((4, mb, ROWS, width), narrow),
            jax.ShapeDtypeStruct((mb, ROWS, width), narrow),
            jax.ShapeDtypeStruct((mb, ROWS, width), narrow),
            jax.ShapeDtypeStruct((mb, ROWS, 128), wide),
            jax.ShapeDtypeStruct((8, width), wide),
        ],
        compiler_params=params(),
        cost_estimate=cost(2 * mb * ROWS * width * width * 9, 70e6),
    )(lengths, dpool, unit3, unit2, stat, slope, mixed, w, gains, pick)


def attend_back_kernel(
    lengths_ref, q_ref, k_ref, v_ref, do_ref, qunit_ref, kunit_ref, qr_ref, kr_ref, stat_ref, gain_ref, ones_ref,
    dq_ref, dk_ref, dv_ref, dgain_ref, dq_acc, dk_acc, dv_acc,
):
    pack = pl.program_id(1)
    lane = lax.broadcasted_iota(jnp.int32, (1, 2 * HEAD), 1)

    def both(x, axis=0):
        zero = jnp.zeros_like(x)
        return jnp.concatenate([jnp.where(lane < HEAD, x, zero), jnp.where(lane < HEAD, zero, x)], axis=axis)

    def part(start, count, tile, chunk, masked):
        for ti in range(start, start + count, tile):
            q2 = both(q_ref[0, ti : ti + tile])
            do2 = both(do_ref[0, ti : ti + tile])
            lse = jnp.concatenate([stat_ref[0, h : h + 1, ti : ti + tile] for h in (0, 1)], axis=1)
            delta = jnp.concatenate([stat_ref[0, h : h + 1, ti : ti + tile] for h in (2, 3)], axis=1)
            for ui in range(start, start + count, chunk):
                k = k_ref[0, ui : ui + chunk]
                v = v_ref[0, ui : ui + chunk]
                s = dot(k, q2, 1, 1)
                p = jnp.exp2(s * log2e - lse)
                if masked:
                    limit = lengths_ref[pack, 1]
                    row = lax.broadcasted_iota(jnp.int32, s.shape, 0) + (ui - start)
                    col = lax.broadcasted_iota(jnp.int32, s.shape, 1)
                    col = jnp.where(col < tile, col, col - tile) + (ti - start)
                    p = jnp.where((row < limit) == (col < limit), p, 0.0)
                dp = dot(v, do2, 1, 1)
                ds = (p * (dp - delta)).astype(narrow)
                dv_new = dot(p.astype(narrow), do2)
                dk_new = dot(ds, q2)
                k2 = both(k)
                ds_rows = jnp.concatenate([ds[:, :tile], ds[:, tile:]], axis=0)
                dq_new = dot(ds_rows, k2, 0, 0)
                if ti == start:
                    dv_acc[ui : ui + chunk] = dv_new
                    dk_acc[ui : ui + chunk] = dk_new
                else:
                    dv_acc[ui : ui + chunk] += dv_new
                    dk_acc[ui : ui + chunk] += dk_new
                if ui == start:
                    dq_acc[ti : ti + tile] = dq_new
                else:
                    dq_acc[ti : ti + tile] += dq_new

    part(0, LONG, 384, 384, False)
    part(LONG, SHORT, SHORT, SHORT, True)
    dv_ref[0] = dv_acc[...].astype(narrow)
    ones = ones_ref[...]

    def mean(x):
        return dot(x.astype(narrow), ones)

    @pl.when(pack == 0)
    def _():
        dgain_ref[...] = jnp.zeros_like(dgain_ref)

    for i, (acc, unit_ref, r_ref, ref, factor) in enumerate(
        ((dq_acc, qunit_ref, qr_ref, dq_ref, HEAD**-0.5), (dk_acc, kunit_ref, kr_ref, dk_ref, 1.0))
    ):
        unit, r = unit_ref[0].astype(wide), r_ref[0].astype(wide)
        dy = acc[...] * factor
        dgain_ref[0, i : i + 1] += jnp.sum(dy * unit, axis=0, keepdims=True)
        scaled = dy * gain_ref[1 + i : 2 + i]
        ref[0] = (r * (scaled - mean(scaled) - unit * mean(scaled * unit))).astype(narrow)


def attend_back_call(lengths, q, k, v, do, kept, stat, gains, ones, first_pair, pairs, first=()):
    mb, _, width = q.shape
    block = pl.BlockSpec((1, ROWS, 2 * HEAD), lambda p, m, *_: (m, 0, p + first_pair))
    out = pl.BlockSpec((1, ROWS, 2 * HEAD), lambda p, m, *_: (m, 0, p))
    shape = jax.ShapeDtypeStruct((mb, ROWS, pairs * 2 * HEAD), narrow)
    return pl.pallas_call(
        beside(attend_back_kernel, 12, len(first)),
        grid_spec=pltpu.PrefetchScalarGridSpec(
            num_scalar_prefetch=1,
            grid=(pairs, mb),
            in_specs=[
                *[block] * 8,
                pl.BlockSpec((1, 8, ROWS), lambda p, m, *_: (m, p + first_pair, 0)),
                pl.BlockSpec((8, 2 * HEAD), lambda p, m, *_: (0, p + first_pair)),
                pl.BlockSpec((2 * HEAD, 2 * HEAD), lambda p, m, *_: (0, 0)),
                *anywhere(first),
            ],
            out_specs=[out, out, out, pl.BlockSpec((1, 8, 2 * HEAD), lambda p, m, *_: (p, 0, 0))],
            scratch_shapes=[pltpu.VMEM((ROWS, 2 * HEAD), wide)] * 3,
        ),
        out_shape=[shape, shape, shape, jax.ShapeDtypeStruct((pairs, 8, 2 * HEAD), wide)],
        compiler_params=params(),
        cost_estimate=cost(20 * mb * 2 * pairs * (LONG**2 + SHORT**2) * HEAD * 2, mb * ROWS * pairs * 128 * 18),
    )(lengths, q, k, v, do, *kept, stat, gains, ones, *first)


def first_kernel(*refs, parts):
    grads = refs[: 3 * parts]
    embed_ref, dr_ref, w_ref, gain_ref, out_ref, dgain_ref = refs[3 * parts :]
    step = pl.program_id(0) * pl.num_programs(1) + pl.program_id(1)
    width = embed_ref.shape[2]
    total = None
    for i in range(3):
        rows = jnp.concatenate([grads[3 * p + i][0] for p in range(parts)], axis=1)
        term = dot(rows, w_ref[:, i * width : (i + 1) * width], 1, 1)
        total = term if total is None else total + term
    unit, r = norm_rows(embed_ref[0])

    @pl.when(step == 0)
    def _():
        dgain_ref[...] = jnp.zeros_like(dgain_ref)

    dgain_ref[0:1] += jnp.sum(total * unit, axis=0, keepdims=True)
    out_ref[0] = (dr_ref[0].astype(wide) + back_rows(unit, r, total * gain_ref[0:1])).astype(narrow)


def first_call(grads, embed, dr, w, gains, first=()):
    mb, _, width = embed.shape
    rows = spec((1, TILE, width), lambda m, i: (m, i, 0))
    parts = len(grads) // 3
    return pl.pallas_call(
        beside(functools.partial(first_kernel, parts=parts), len(grads) + 4, len(first)),
        grid=(mb, ROWS // TILE),
        in_specs=[spec((1, TILE, g.shape[2]), lambda m, i: (m, i, 0)) for g in grads]
        + [rows, rows, held(w.shape), held(gains.shape)]
        + anywhere(first),
        out_specs=[rows, spec((8, width), lambda m, i: (0, 0))],
        out_shape=[
            jax.ShapeDtypeStruct((mb, ROWS, width), narrow),
            jax.ShapeDtypeStruct((8, width), wide),
        ],
        compiler_params=params(),
        cost_estimate=cost(2 * mb * ROWS * width * width * 3, 32e6),
    )(*grads, embed, dr, w, gains, *first)


def split_rows(value, own_ref, sent_ref, me, n):
    across, up, deep = own_ref.shape[:3]
    part = own_ref.shape[4]
    for x in range(across):
        for y in range(up):
            for z in range(deep):
                at = ((z * up + y) * across + x) * 2 * part
                first = value[at : at + part].astype(narrow)
                second = value[at + part : at + 2 * part].astype(narrow)
                own_ref[x, y, z, n] = jnp.where(me == 0, first, second)
                sent_ref[x, y, z, n] = jnp.where(me == 0, second, first)


def flat_rows(ref):
    return ref[...].reshape(-1, ref.shape[-1])


def weight_kernel(act_ref, dm_ref, second_ref, dup_ref, mixed_ref, dr_ref, out_ref):
    step = pl.program_id(0)

    def write(a_ref, b_ref):
        value = dot(flat_rows(a_ref), flat_rows(b_ref), 0, 0)
        part = out_ref.shape[2]
        for to in range(out_ref.shape[0]):
            out_ref[to, 0] = value[to * part : (to + 1) * part].astype(narrow)

    pl.when(step == 0)(lambda: write(mixed_ref, dr_ref))
    pl.when((step >= 1) & (step < 5))(lambda: write(second_ref, dup_ref))
    pl.when(step >= 5)(lambda: write(act_ref, dm_ref))


def split_shape(rows):
    core, x, y, z = (level[2] for level in levels())
    return (x, y, z), rows // (core * x * y * z)


def core_at():
    return (lax.axis_index("seq") % 2).reshape(1).astype(jnp.int32)


def weight_call(act, dm, second, dup, mixed, dr):
    width = dm.shape[2]
    parts = lax.axis_size("fsdp") * lax.axis_size("seq")
    rows = held(dm.shape)
    one = (1, *dm.shape)
    return pl.pallas_call(
        weight_kernel,
        grid=(9,),
        in_specs=[
            spec(one, lambda i: (jnp.maximum(i - 5, 0), 0, 0, 0)),
            rows,
            rows,
            spec(one, lambda i: (jnp.clip(i - 1, 0, 3), 0, 0, 0)),
            rows,
            rows,
        ],
        out_specs=spec((parts, 1, width // parts, width), lambda i: (0, i, 0, 0)),
        out_shape=jax.ShapeDtypeStruct((parts, 9, width // parts, width), narrow),
        compiler_params=params(),
        cost_estimate=cost(2 * 9 * dm.size * width, 70e6),
    )(act, dm, second, dup, mixed, dr)


def one_weight_kernel(at_ref, *refs, groups):
    count = len(groups) + sum(groups)
    own_ref, sent_ref, total = refs[count:]
    step = pl.program_id(0)
    last = step == pl.num_programs(0) - 1
    at, ref = 0, 0
    for members in groups:
        a = refs[ref][0]
        for b_ref in refs[ref + 1 : ref + 1 + members]:
            lanes = pl.ds(at, b_ref.shape[-1])
            at += b_ref.shape[-1]
            value = dot(a, b_ref[0], 0, 0)

            @pl.when(step == 0)
            def _(value=value, lanes=lanes):
                total[:, lanes] = value

            @pl.when((step > 0) & ~last)
            def _(value=value, lanes=lanes):
                total[:, lanes] += value

            @pl.when(last)
            def _(value=value, lanes=lanes):
                split_rows(total[:, lanes] + value, own_ref.at[..., lanes], sent_ref.at[..., lanes], at_ref[0], 0)

        ref += 1 + members


def one_weight_call(*groups, first=()):
    arrays = [array for group in groups for array in group]
    mb, rows, depth = arrays[0].shape
    width = sum(x.shape[-1] for group in groups for x in group[1:])
    (x, y, z), part = split_shape(depth)
    shape = (x, y, z, 1, part, width)
    out = pl.BlockSpec(shape, lambda m, *_: (0,) * 6)
    return pl.pallas_call(
        beside(
            functools.partial(one_weight_kernel, groups=[len(group) - 1 for group in groups]),
            1 + len(arrays),
            len(first),
        ),
        grid_spec=pltpu.PrefetchScalarGridSpec(
            num_scalar_prefetch=1,
            grid=(mb,),
            in_specs=[pl.BlockSpec((1, *v.shape[1:]), lambda m, *_: (m, 0, 0)) for v in arrays]
            + anywhere(first),
            out_specs=[out] * 2,
            scratch_shapes=[pltpu.VMEM((depth, width), wide)],
        ),
        out_shape=[jax.ShapeDtypeStruct(shape, narrow)] * 2,
        compiler_params=params(),
        cost_estimate=cost(2 * mb * rows * depth * width, 12e6),
    )(core_at(), *arrays, *first)


def embed_weight_kernel(at_ref, patch_ref, hot_ref, grad_ref, norm_ref, gain_ref, own_ref, sent_ref, total):
    step = pl.program_id(0)
    grad = grad_ref[0]
    width = grad.shape[1]
    value = dot(patch_ref[0, 0], grad, 0, 0)
    table = dot(grad, hot_ref[0], 0, 0)

    @pl.when(step == 0)
    def _():
        total[:, :width] = value
        total[:, width : width + 128] = table

    @pl.when(step > 0)
    def _():
        total[:, :width] += value
        total[:, width : width + 128] += table

    @pl.when(step == pl.num_programs(0) - 1)
    def _():
        gains = norm_ref[...] + gain_ref[...]
        total[:, width + 128 :] = jnp.concatenate([gains, jnp.zeros((120, width), wide)], axis=0).T
        split_rows(total[...], own_ref, sent_ref, at_ref[0], 0)


def embed_weight_call(patches, hot, grad, norm_gain, gain_rows, first=()):
    mb, _, width = grad.shape
    pixels = patches.shape[3]
    (x, y, z), part = split_shape(pixels)
    shape = (x, y, z, 1, part, width + 256)
    out = pl.BlockSpec(shape, lambda m, *_: (0,) * 6)
    return pl.pallas_call(
        beside(embed_weight_kernel, 6, len(first)),
        grid_spec=pltpu.PrefetchScalarGridSpec(
            num_scalar_prefetch=1,
            grid=(mb,),
            in_specs=[
                pl.BlockSpec((1, 1, ROWS, pixels), lambda m, *_: (m, 0, 0, 0)),
                pl.BlockSpec((1, ROWS, hot.shape[2]), lambda m, *_: (m, 0, 0)),
                pl.BlockSpec((1, ROWS, width), lambda m, *_: (m, 0, 0)),
                pl.BlockSpec((8, width), lambda m, *_: (0, 0)),
                pl.BlockSpec((8, width), lambda m, *_: (0, 0)),
                *anywhere(first),
            ],
            out_specs=[out, out],
            scratch_shapes=[pltpu.VMEM((pixels, width + 256), wide)],
        ),
        out_shape=[jax.ShapeDtypeStruct(shape, narrow)] * 2,
        compiler_params=params(),
        cost_estimate=cost(2 * grad.size * (pixels + 128), 12e6),
    )(core_at(), patches, hot, grad, norm_gain, gain_rows, *first)


def fold(parts):
    while len(parts) > 1:
        parts = [parts[i] + parts[i + 1] for i in range(0, len(parts), 2)]
    return parts[0]


def swap(x, axis, bits):
    if bits == 0:
        return x
    return lax.ppermute(x, axis, [(i, i ^ bits) for i in range(lax.axis_size(axis))])


def tied(x, *after):
    return lax.optimization_barrier((x, *after))[0]


def pick_index(x, index, dim):
    return lax.dynamic_index_in_dim(x, index, dim, keepdims=False)


def levels():
    across, deep = lax.axis_size("seq"), lax.axis_size("fsdp")
    y = 1 << ((deep.bit_length() - 1) // 2)
    return (("seq", 1, 2), ("seq", 2, across // 2), ("fsdp", 1, y), ("fsdp", y, deep // y))


CORE, X, Y, Z = range(4)


class Sum:
    def __init__(self, terms, which):
        axis, stride, size = levels()[which]
        at = lax.axis_index(axis) // stride % size

        def part(k):
            return fold([pick_index(term, at ^ k, 0).astype(wide) for term in terms])

        self.sent = [part(k).astype(narrow) for k in range(1, size)]
        self.terms = [part(0)] + [swap(x, axis, (k + 1) * stride) for k, x in enumerate(self.sent)]

    def after(self, *others):
        return [tied(self.terms[0], *others), *self.terms[1:]]

    def total(self):
        return fold([term.astype(wide) for term in self.terms])


def core_terms(own, sent):
    return [own, swap(sent, "seq", 1)]


def settle_kernel(at_ref, *refs, count, moves):
    sources, outs = refs[:count], refs[count:]
    for source, index, out, target in moves:
        outs[out][target(at_ref[0], at_ref[1])] = sources[source][index]


def mesh_at():
    return jnp.stack([lax.axis_index("fsdp"), lax.axis_index("seq")]).astype(jnp.int32)


def in_vmem(count):
    return [pl.BlockSpec(memory_space=pltpu.VMEM)] * count


def settled(parts, shapes, moves, first=()):
    size = sum(part.size for part in parts) * parts[0].dtype.itemsize
    return pl.pallas_call(
        beside(functools.partial(settle_kernel, count=len(parts), moves=moves), 1 + len(parts), len(first)),
        in_specs=[pl.BlockSpec(memory_space=pltpu.SMEM)] + in_vmem(len(parts)) + anywhere(first),
        out_specs=in_vmem(len(shapes)),
        out_shape=[jax.ShapeDtypeStruct(shape, parts[0].dtype) for shape in shapes],
        compiler_params=params(),
        cost_estimate=cost(0, 2 * size),
    )(mesh_at(), *parts, *first)


def seq_parts(x, *after):
    half = [swap(x, "seq", k) for k in range(0, lax.axis_size("seq"), 2)]
    if after:
        half = [half[0]] + [tied(y, *after) for y in half[1:]]
    return [part for y in half for part in (y, swap(y, "seq", 1))]


def settle_rows(parts, cuts, shapes):
    deep = parts[0].shape[0]
    moves = [
        (j, (k, slice(start, stop)), out, lambda f, s, j=j, k=k, index=index: (*index, k ^ f, j ^ s))
        for j in range(len(parts))
        for k in range(deep)
        for start, stop, out, index in cuts
    ]
    return settled(parts, shapes, moves)


def near_exchange(x):
    return jnp.stack([swap(x, "fsdp", k) for k in range(levels()[Y][2])])


def far_exchange(x):
    _, stride, far = levels()[Z]
    return [swap(x, "fsdp", k * stride) for k in range(far)]


def stacked(parts):
    return jnp.stack(parts).reshape(-1, *parts[0].shape[1:])


def my_rows(x):
    size = lax.axis_size("seq")
    return pick_index(x.reshape(x.shape[0], size, x.shape[1] // size, x.shape[2]), lax.axis_index("seq"), 1)


def grads_kernel(at_ref, factor_ref, *refs, count, part):
    parts, (out_ref, small_ref) = refs[:count], refs[count:]
    factor = factor_ref[0]
    for j, ref in enumerate(parts):
        to = at_ref[1] ^ j
        for b in range(out_ref.shape[0]):
            out_ref[b, to] = ref[b * part : (b + 1) * part].astype(wide) * factor
        small_ref[to] = ref[out_ref.shape[0] * part :].astype(wide) * factor


def join_kernel(at_ref, *refs, counts, size):
    ins, outs = refs[: sum(counts)], refs[sum(counts) :]
    for k in range(size):
        at = 0
        ref = 0
        for count in counts:
            value = fold([r[at_ref[0] ^ k].astype(wide) for r in ins[ref : ref + count]])
            ref += count
            lanes = value.shape[-1]
            outs[k][:, :, at : at + lanes] = value.astype(outs[k].dtype)
            at += lanes


def join_call(groups, first):
    axis, stride, size = levels()[Z]
    at = (lax.axis_index(axis) // stride % size).reshape(1).astype(jnp.int32)
    arrays = [term for terms in groups for term in terms]
    counts = [len(terms) for terms in groups]
    shape = (*arrays[0].shape[1:-1], sum(terms[0].shape[-1] for terms in groups))
    own, *sent = pl.pallas_call(
        beside(functools.partial(join_kernel, counts=counts, size=size), 1 + len(arrays), len(first)),
        in_specs=[pl.BlockSpec(memory_space=pltpu.SMEM)] + in_vmem(len(arrays)) + anywhere(first),
        out_specs=in_vmem(size),
        out_shape=[jax.ShapeDtypeStruct(shape, wide)] + [jax.ShapeDtypeStruct(shape, narrow)] * (size - 1),
        compiler_params=params(),
        cost_estimate=cost(0, 3e6),
    )(at, *arrays, *first)
    return [own] + [swap(x, axis, (k + 1) * stride) for k, x in enumerate(sent)]


def collect_kernel(at_ref, slot_ref, scalar_ref, rest_ref, *refs, count, deep, per, columns):
    terms, mid_terms = refs[:count], refs[count : 2 * count]
    own_ref, *out_refs = refs[2 * count : 2 * count + 1 + deep]
    blocks = refs[-1]
    part, width = rest_ref.shape[1:]
    scale = 1.0 / scalar_ref[0]
    both = fold([ref[0].astype(wide) for ref in terms])
    remain = width - columns
    late = both[:, width + 256 :]
    mid = fold([ref[0].astype(wide) for ref in mid_terms])
    pieces = [both[:, :width]]
    for i in range(3):
        first = mid[:, i * columns : (i + 1) * columns]
        pieces.append(jnp.concatenate([first, late[:, i * remain : (i + 1) * remain]], axis=1))
    pieces += [rest_ref[i].astype(wide) for i in range(rest_ref.shape[0])]
    squares = jnp.zeros((1, 1), wide)
    total = jnp.zeros((part, width), wide)
    for b, piece in enumerate(pieces):
        piece = (piece * scale).astype(narrow)
        blocks[b] = piece
        own_ref[b * part : (b + 1) * part] = piece
        total += jnp.square(piece.astype(wide))
    small = (both[:, width : width + 256] * scale).astype(narrow)
    third = part // 3
    small = small.astype(wide)
    squares = jnp.sum(total, keepdims=True) + jnp.sum(jnp.square(small), keepdims=True) + scalar_ref[1]
    small = jnp.concatenate([small[i * third : (i + 1) * third] for i in range(3)], axis=1)
    own_ref[len(pieces) * part :] = small.astype(narrow)
    row = lax.broadcasted_iota(jnp.int32, (8, width), 0)
    notes = jnp.zeros((8, width), wide)
    for at, value in ((0, squares), (3, jnp.full((1, 1), scalar_ref[2]))):
        for i in range(3):
            piece = value.astype(narrow).astype(wide)
            value = value - piece
            notes = jnp.where(row == at + i, piece, notes)
    notes = notes.astype(narrow)
    blocks[len(pieces)] = jnp.zeros((part, width), narrow)
    for k, out_ref in enumerate(out_refs):
        for i in range(per):
            slot = (at_ref[0] ^ k) * per + i
            found = len(pieces)
            for b in range(len(pieces)):
                found = jnp.where(slot_ref[b] == slot, b, found)
            out_ref[i * part : (i + 1) * part] = blocks[found]
        out_ref[per * part :] = notes


def collect_call(block_slot, scalars, rest, terms, mid_terms, per, columns, first):
    part, width = rest.shape[1:]
    deep = lax.axis_size("fsdp")
    count = block_slot.shape[0]
    smem = pl.BlockSpec(memory_space=pltpu.SMEM)
    message = jax.ShapeDtypeStruct((per * part + 8, width), narrow)
    return pl.pallas_call(
        beside(
            functools.partial(collect_kernel, count=len(terms), deep=deep, per=per, columns=columns),
            4 + 2 * len(terms),
            len(first),
        ),
        in_specs=[smem, smem, smem] + in_vmem(1 + 2 * len(terms)) + anywhere(first),
        out_specs=in_vmem(1 + deep),
        out_shape=[jax.ShapeDtypeStruct((count * part + part // 3, width), narrow)] + [message] * deep,
        scratch_shapes=[pltpu.VMEM((count + 1, part, width), narrow)],
        compiler_params=params(),
        cost_estimate=cost(0, 4e6),
    )(mesh_at(), block_slot, scalars, rest, *terms, *mid_terms, *first)


def direction_kernel(at_ref, left_ref, right_ref, *refs, count, deep):
    parts, slotted_ref, notes_ref = refs[:count], refs[count], refs[count + 1]
    out_ref, rows = refs[count + 2 :]
    per, _, part, width = left_ref.shape
    for j, ref in enumerate(parts):
        for k in range(deep):
            f, s = at_ref[0] ^ k, at_ref[1] ^ j
            for i in range(per):
                rows[i, f * count + s] = ref[k, i * part : (i + 1) * part].astype(wide)
            notes_ref[f, s] = ref[k, per * part :]
    for i in range(per):
        grad = rows[i].reshape(deep * count * part, width).astype(narrow)
        slotted_ref[i] = grad
        inner = dot(left_ref[i].astype(wide).reshape(deep * part, width).astype(narrow), grad)
        value = dot(inner.astype(narrow), right_ref[i])
        out_ref[:, i] = value.reshape(deep, part, width).astype(narrow)


def direction_call(left, right, parts):
    per, deep, part, width = left.shape
    count = len(parts)
    return pl.pallas_call(
        functools.partial(direction_kernel, count=count, deep=deep),
        in_specs=[pl.BlockSpec(memory_space=pltpu.SMEM)] + in_vmem(2 + count),
        out_specs=in_vmem(3),
        out_shape=[
            jax.ShapeDtypeStruct((per, width, width), narrow),
            jax.ShapeDtypeStruct((deep, count, 8, width), narrow),
            jax.ShapeDtypeStruct((deep, per, part, width), narrow),
        ],
        scratch_shapes=[pltpu.VMEM((per, deep * count, part, width), wide)],
        compiler_params=params(),
        cost_estimate=cost(10 * per * deep * part * width * width, 16e6),
    )(mesh_at(), left, right, *parts)


def select_kernel(slot_ref, slots_ref, out_ref):
    per, part = slots_ref.shape[1:3]
    for b in range(out_ref.shape[0] // part):
        slot = slot_ref[b]
        out_ref[b * part : (b + 1) * part] = slots_ref[slot // per, slot % per]


def select_call(block_slot, slots, first):
    part, width = slots.shape[2:]
    return pl.pallas_call(
        beside(select_kernel, 2, len(first)),
        in_specs=[pl.BlockSpec(memory_space=pltpu.SMEM)] + in_vmem(1) + anywhere(first),
        out_specs=pl.BlockSpec(memory_space=pltpu.VMEM),
        out_shape=jax.ShapeDtypeStruct((block_slot.shape[0] * part, width), narrow),
        compiler_params=params(),
        cost_estimate=cost(0, 2e6),
    )(block_slot, slots, *first)


def stats_kernel(factor_ref, grad_ref, left_ref, right_ref, left_out, right_out):
    grad = grad_ref[0]
    share = (1 - stat_decay) * factor_ref[0] * factor_ref[0]
    left_out[0] = stat_decay * left_ref[0] + share * dot(grad, grad, 1, 1)
    right_out[0] = stat_decay * right_ref[0] + share * dot(grad, grad, 0, 0)


def stats_call(factor, grads, left, right, first):
    per, width, _ = grads.shape
    one = spec((1, width, width), lambda i: (i, 0, 0))
    return pl.pallas_call(
        beside(stats_kernel, 4, len(first)),
        grid=(per,),
        in_specs=[pl.BlockSpec(memory_space=pltpu.SMEM), one, one, one] + anywhere(first),
        out_specs=[one, one],
        out_shape=[jax.ShapeDtypeStruct(left.shape, wide)] * 2,
        compiler_params=params(),
        cost_estimate=cost(4 * per * width**3, 20e6),
    )(factor.reshape(1), grads, left, right, *first)


def classifier_kernel(at_ref, factor_ref, weight_ref, first_ref, second_ref, *refs, count, part):
    parts, outs = refs[:count], refs[count:]
    for j, ref in enumerate(parts):
        to = at_ref[1] ^ j
        new = adam(
            weight_ref[to], ref[...] * factor_ref[0], first_ref[to], second_ref[to], adam_rate, decay_rate
        )
        for out_ref, value in zip(outs, new):
            out_ref[to] = value


def update_kernel(at_ref, factor_ref, block_ref, *refs, count, part):
    parts, out_ref = refs[:count], refs[count]
    factor = factor_ref[0]
    for j, ref in enumerate(parts):
        to = at_ref[1] ^ j
        for b in range(out_ref.shape[0]):
            old = block_ref[b, to]
            step = ref[b * part : (b + 1) * part].astype(wide) * factor
            out_ref[b, to] = old - shampoo_rate * (step + decay_rate * old)


def finish_call(kernel, factor, arrays, parts, part, shapes, first=()):
    smem = pl.BlockSpec(memory_space=pltpu.SMEM)
    return pl.pallas_call(
        beside(functools.partial(kernel, count=len(parts), part=part), 2 + len(arrays) + len(parts), len(first)),
        in_specs=[smem, smem] + in_vmem(len(arrays) + len(parts)) + anywhere(first),
        out_specs=in_vmem(len(shapes)),
        out_shape=[jax.ShapeDtypeStruct(shape, wide) for shape in shapes],
        compiler_params=params(),
        cost_estimate=cost(0, 12e6),
    )(mesh_at(), factor.reshape(1), *arrays, *parts, *first)


def adam(weight, grad, first, second, rate, decay):
    first_new = first_decay * first + (1 - first_decay) * grad
    second_new = second_decay * second + (1 - second_decay) * grad * grad
    corrected = (
        first_new
        / (1 - first_decay**STEP)
        / (jnp.sqrt(second_new / (1 - second_decay**STEP)) + adam_eps)
    )
    return (weight - rate * (corrected + decay * weight), first_new, second_new)


def product(spec_text, a, b):
    return jnp.einsum(spec_text, a, b, preferred_element_type=wide)


def local(
    patches, positions, lengths, res_weights, labels, block_slot, blocks, pos_table, gains, head,
    left_stats, right_stats, left_roots, right_roots,
    pos_first, pos_second, gain_first, gain_second, head_first, head_second,
):
    mb = patches.shape[0]
    deep, size = lax.axis_size("fsdp"), lax.axis_size("seq")
    me_f, me_s = lax.axis_index("fsdp"), lax.axis_index("seq")
    lengths, res_weights, labels = (x[:, 0] for x in (lengths, res_weights, labels))
    lanes = pos_table.shape[2]
    width = lanes * deep
    grid_rows = pos_table.shape[1]

    part = blocks.shape[1] // size
    seen = jnp.broadcast_to(jnp.sum(res_weights).astype(wide), (lanes, 3))
    small = jnp.concatenate(
        [pos_table.reshape(2 * grid_rows, lanes).T, gains.T, seen, jnp.zeros((lanes, 120), wide)], axis=1
    ).astype(narrow)
    opening = my_rows(jnp.concatenate([blocks[0].astype(narrow), small], axis=1)[None])[0]
    project = my_rows(blocks[1:4]).astype(narrow).transpose(1, 0, 2).reshape(part, 3 * width)
    near = near_exchange(jnp.concatenate([opening, project], axis=1))
    every = far_exchange(near)
    positions, lengths, res_weights, labels, later, later_head, left_part, right_part, _ = lax.optimization_barrier(
        (positions, lengths, res_weights, labels, blocks, head, left_roots, right_roots, near)
    )
    left_part = pick_index(left_part.reshape(left_roots.shape[0], deep, size, part, width), me_s, 2).astype(narrow)
    right_part = right_part.astype(narrow)
    places = positions[:, :, 0, :ROWS]
    grid = jnp.arange(grid_rows)
    hot = jnp.concatenate([places[i][:, :, None] == grid for i in range(2)], axis=2).astype(narrow)
    index = jnp.arange(256)
    ones = jnp.where(index[:, None] // HEAD == index[None] // HEAD, 1 / HEAD, 0).astype(narrow)
    pick = (jnp.arange(width)[:, None] // HEAD == jnp.arange(128)[None]).astype(narrow)

    def column(x):
        x = jnp.pad(x, ((0, 0), (0, 6))).reshape(8 * mb, 1)
        return jnp.broadcast_to(x, (8 * mb, 128))

    seq_columns = [column(1.0 / lengths.astype(wide)), column(res_weights), column(labels)]
    rest_part = my_rows(later[4:13]).astype(narrow)
    head_part = my_rows(later_head[None])[0].astype(narrow)
    ahead = (hot, ones, pick, rest_part, head_part, left_part, right_part, *seq_columns)
    every = [every[0], tied(every[1], *ahead), *every[2:]]
    opening = stacked([x[:, :, : width + 256] for x in every])
    project = tied(stacked([x[:, :, width + 256 :] for x in every]), opening)
    opening = seq_parts(opening)
    w_embed = settle_rows(opening, [(0, part, 0, ())], [(deep, size, part, width + 256)])[0]
    w_embed = w_embed.reshape(width, width + 256)
    gains_full = w_embed[:, width + 128 :].T[:8].astype(wide)
    weight_sum = jnp.sum(gains_full[5].reshape(deep * size, part)[:, 0])
    w_rest = lax.all_gather(tied(rest_part, opening[-1]), ("fsdp", "seq"), axis=1, tiled=True)
    w_head = lax.all_gather(tied(head_part, opening[-1]), ("fsdp", "seq"), axis=0, tiled=True)

    embed, first = embed_call(patches, hot, tied(w_embed, project), gains_full)
    w_project = settle_rows(
        seq_parts(project, first), [(0, part, 0, ())], [(deep, size, part, 3 * width)]
    )[0].reshape(width, 3 * width)
    query, keys, values, *kept = project_call(first, w_project, gains_full, ones)
    mixed, stat = attend_call(lengths, query, keys, values)
    second, act, slope, unit2, unit3, row_stat, pool = forward_call(lengths, embed, mixed, w_rest, gains_full)

    loss, d_head, d_pool = head_call(pool.reshape(8 * mb, width), *seq_columns, w_head)
    head_sum = lax.psum_scatter(d_head, ("fsdp", "seq"), scatter_dimension=0, tiled=True)

    dm, d_up, dr, d_mixed, delta, d_gain_rest = backward_call(
        lengths, d_pool.reshape(mb, 8, width), unit3, unit2, row_stat, slope, mixed, w_rest, gains_full, pick
    )
    d_rest = weight_call(act, dm, second, d_up, mixed, dr)
    own_rest = lax.psum_scatter(d_rest, ("fsdp", "seq"), scatter_dimension=0, tiled=True)[0]

    pairs = HEADS // 2
    early = 4
    stats = jnp.stack([s[:, :, :HEADS].reshape(mb, ROWS, pairs, 2) for s in (stat, delta)], axis=3)
    stats = jnp.pad(stats.transpose(0, 2, 3, 4, 1).reshape(mb, pairs, 4, ROWS), ((0, 0), (0, 0), (0, 4), (0, 0)))
    stats = stats.reshape(mb, 8 * pairs, ROWS)

    def heads_back(after, start, count):
        out = attend_back_call(
            lengths, query, keys, values, d_mixed, kept, stats, gains_full, ones, start, count, after,
        )
        return out[:3], out[3]

    grads_one, gain_one = heads_back([d_rest], 0, early)
    mid_core = core_terms(*one_weight_call((first, *grads_one), first=[head_sum]))
    mid_x = Sum(mid_core, X)
    grads_two, gain_two = heads_back(mid_x.sent, early, pairs - early)
    mid_y = Sum(mid_x.after(grads_two[0]), Y)
    late_core = core_terms(*one_weight_call((first, *grads_two), first=mid_y.sent))
    late_x = Sum(late_core, X)
    d_embed, d_gain_first = first_call(
        (*grads_one, *grads_two), embed, dr, w_project, gains_full, late_x.sent
    )
    late_y = Sum(late_x.after(d_embed), Y)
    d_gain_heads = jnp.concatenate([gain_one, gain_two], axis=0).transpose(1, 0, 2).reshape(8, width)
    d_gains = jnp.concatenate(
        [jnp.zeros((1, width), wide), d_gain_heads[:2], d_gain_rest[3:5], jnp.zeros((3, width), wide)], axis=0
    )
    e_own, e_sent = embed_weight_call(
        patches, hot, d_embed, d_gain_first, d_gains, [own_rest, *late_y.sent, *mid_y.terms[1:]]
    )
    head_sum = tied(head_sum, e_own) / weight_sum
    scalars = jnp.stack([weight_sum, jnp.sum(jnp.square(head_sum)), loss[0, 0]])
    last_y = Sum(Sum(core_terms(e_own, e_sent), X).terms, Y)
    mid_z = Sum(mid_y.after(e_own), Z)
    z_terms = join_call([last_y.terms, late_y.terms], mid_z.terms[1:])

    per = left_stats.shape[0]
    count = blocks.shape[0]
    own, *outgoing = collect_call(
        block_slot, scalars, own_rest, z_terms, mid_z.terms, per,
        early * 2 * HEAD, [],
    )
    arrived = seq_parts(jnp.stack([swap(x, "fsdp", k) for k, x in enumerate(outgoing)]))
    slotted, notes, directions = direction_call(left_part, right_part, arrived)
    notes = jnp.sum(notes[:, :, :, 0].astype(wide), axis=(0, 1))
    loss_sum = notes[3] + notes[4] + notes[5]
    clip_norm = jnp.sqrt(notes[0] + notes[1] + notes[2])
    factor = jnp.minimum(1.0, clip_bound / clip_norm)
    came = lax.all_to_all(directions, "fsdp", split_axis=0, concat_axis=0, tiled=True)
    own_parts = seq_parts(tied(own, slotted))
    head_parts = seq_parts(tied(head_sum, slotted))
    left_new, right_new = stats_call(factor, slotted, left_stats, right_stats, [])
    back = select_call(block_slot, came, [own_parts[-1], head_parts[-1]])
    back_parts = seq_parts(back)
    split = (count, size, part, width)
    block_grads, small_grad = finish_call(
        grads_kernel, factor, [], own_parts, part, [split, (size, part // 3, width)], [back]
    )
    small_grad = jnp.concatenate([small_grad[:, :, i * 256 : (i + 1) * 256] for i in range(3)], axis=1)
    small_grad = small_grad.reshape(lanes, 256).T
    table_grad = small_grad[: 2 * grid_rows].reshape(2, grid_rows, lanes)
    gain_grad = small_grad[2 * grid_rows : 2 * grid_rows + 5]
    pos_new, pos_first_new, pos_second_new = adam(
        pos_table, table_grad, pos_first, pos_second, table_rate, decay_rate
    )
    gains_new, gain_first_new, gain_second_new = adam(gains, gain_grad, gain_first, gain_second, gain_rate, 0.0)
    head_shape = (size, *head_sum.shape)
    head_new, head_first_new, head_second_new = (
        x.reshape(head.shape)
        for x in finish_call(
            classifier_kernel, factor, [x.reshape(head_shape) for x in (head, head_first, head_second)], head_parts,
            part, [head_shape] * 3, [back],
        )
    )
    blocks_new = finish_call(
        update_kernel, factor, [blocks.reshape(split)], back_parts, part, [split],
        [block_grads, right_new, pos_new, gains_new, head_new],
    )[0].reshape(blocks.shape)
    block_grads = block_grads.reshape(blocks.shape)
    return (
        blocks_new, block_grads, left_new, right_new, pos_new, pos_first_new, pos_second_new,
        gains_new, gain_first_new, gain_second_new, head_new, head_first_new, head_second_new,
        clip_norm, loss_sum, weight_sum,
    )


def solution(mesh):
    placed = (
        P(None, ("seq", "fsdp"), None, None),
        P(None, None, ("seq", "fsdp"), None),
        P(None, ("seq", "fsdp"), None),
        P(None, ("seq", "fsdp"), None),
        P(None, ("seq", "fsdp"), None),
        P(),
        P(None, "fsdp", None),
        P(None, None, "fsdp"),
        P(None, "fsdp"),
        P("fsdp", None),
        P("fsdp", None, None),
        P("fsdp", None, None),
        P("fsdp", None, None),
        P("fsdp", None, None),
        P(None, None, "fsdp"),
        P(None, None, "fsdp"),
        P(None, "fsdp"),
        P(None, "fsdp"),
        P("fsdp", None),
        P("fsdp", None),
    )
    return jax.shard_map(
        local,
        mesh=mesh,
        in_specs=placed,
        out_specs=(
            P(None, "fsdp", None),
            P(None, "fsdp", None),
            P("fsdp", None, None),
            P("fsdp", None, None),
            P(None, None, "fsdp"),
            P(None, None, "fsdp"),
            P(None, None, "fsdp"),
            P(None, "fsdp"),
            P(None, "fsdp"),
            P(None, "fsdp"),
            P("fsdp", None),
            P("fsdp", None),
            P("fsdp", None),
            P(),
            P(),
            P(),
        ),
        check_vma=False,
    )
```
